32 devices in a mesh: docs: 4 (over y, x), wide: 8 (over z, core).
Axes of the slice: x: 2, y: 2, z: 4, core: 2. Of those that a mesh axis runs over, the one named last changes fastest.
Arguments:
- rows: bfloat16 [16384, 768], P(('docs', 'wide')), may hold values from -6 to 6
- cot_stream: float32 [16384, 768], P(('docs', 'wide')), may hold values from -6 to 6
- cot_joined: float32 [8192, 768], P(('docs', 'wide')), may hold values from -6 to 6
- page: int32 [16384], P(('docs', 'wide')), may hold values from -1 to 447, as said below
- key_mask: int32 [16384], P(('docs', 'wide')), may hold values 0 or 1
- w_qkv: float32 [2, 768, 2304], P(None, 'wide', 'docs'), may hold values from -0.21875 to 0.21875
- m_qkv: float32 [2, 768, 2304], P(None, 'wide', 'docs')
- v_qkv: float32 [2, 768, 2304], P(None, 'wide', 'docs'), as said below
- w_out: float32 [2, 768, 768], P(None, 'wide', 'docs'), may hold values from -0.875 to 0.875
- m_out: float32 [2, 768, 768], P(None, 'wide', 'docs')
- v_out: float32 [2, 768, 768], P(None, 'wide', 'docs'), as said below
- w_up: float32 [2, 768, 3072], P(None, 'wide', 'docs'), may hold values from -0.21875 to 0.21875
- m_up: float32 [2, 768, 3072], P(None, 'wide', 'docs')
- v_up: float32 [2, 768, 3072], P(None, 'wide', 'docs'), as said below
- w_down: float32 [2, 3072, 768], P(None, 'wide', 'docs'), may hold values from -0.109375 to 0.109375
- m_down: float32 [2, 3072, 768], P(None, 'wide', 'docs')
- v_down: float32 [2, 3072, 768], P(None, 'wide', 'docs'), as said below
- gains: float32 [5, 768], replicated
- m_gains: float32 [5, 768], replicated
- v_gains: float32 [5, 768], replicated, as said below
Outputs:
- stream_out: float32 [16384, 768], P(('docs', 'wide'))
- joined: float32 [8192, 768], P(('docs', 'wide'))
- grad_rows: float32 [16384, 768], P(('docs', 'wide'))
- new_w_qkv: float32 [2, 768, 2304], P(None, 'wide', 'docs')
- new_m_qkv: float32 [2, 768, 2304], P(None, 'wide', 'docs')
- new_v_qkv: float32 [2, 768, 2304], P(None, 'wide', 'docs')
- new_w_out: float32 [2, 768, 768], P(None, 'wide', 'docs')
- new_m_out: float32 [2, 768, 768], P(None, 'wide', 'docs')
- new_v_out: float32 [2, 768, 768], P(None, 'wide', 'docs')
- new_w_up: float32 [2, 768, 3072], P(None, 'wide', 'docs')
- new_m_up: float32 [2, 768, 3072], P(None, 'wide', 'docs')
- new_v_up: float32 [2, 768, 3072], P(None, 'wide', 'docs')
- new_w_down: float32 [2, 3072, 768], P(None, 'wide', 'docs')
- new_m_down: float32 [2, 3072, 768], P(None, 'wide', 'docs')
- new_v_down: float32 [2, 3072, 768], P(None, 'wide', 'docs')
- new_gains: float32 [5, 768], replicated
- new_m_gains: float32 [5, 768], replicated
- new_v_gains: float32 [5, 768], replicated
The draws below stay inside these ranges and needn't reach their ends.
Inputs may be any that keep to these rules, and one draw needn't show every extreme that they name: Within each packed row pages are numbered from 0 in order, each at most 64 blocks, the first exactly 64; padding (-1) closes every packed row; the text and image rows of a block carry the same number; the largest page number is reached in every draw. `v_qkv`: second moments are positive. `v_out`: second moments are positive. `v_up`: second moments are positive. `v_down`: second moments are positive. `v_gains`: second moments are positive.
All inputs are finite; a program needn't handle non-finite values. No bound on the sum of `key_mask` on one device may be relied on, other than what follows from the above.
Results may differ from the reference program's by a relative error of at most 0.015.
The reference program's roundings to bfloat16 on the way count: a program that leaves them out, or rounds other values in their place, can miss the bound.
Values may be sent and summed in bfloat16 or wider, within the bound.
No kernel may reach another device: no remote copies, remote signals or barrier semaphores. Data moves between devices by JAX's collectives and lax.ppermute only.
A program may use at most 192 MiB of HBM per device.

```python
import math
import jax
import jax.numpy as jnp
from jax import lax

D = 768
HEADS = 12
FF = 3072
TOK_DEV = 512
PAGE_MOST = 64
STEP = 10
PAIRS_DOC = 4
GROUPS = 16
BLOCKS = 8192
ROWS = 16384
N_DOCS = 4
N_WIDE = 8


def row_pages(ends):
    position = jnp.arange(TOK_DEV, dtype=jnp.int32)
    return jnp.searchsorted(ends, position, side='right').astype(jnp.int32)


def draw_page(key, part):
    group_index = jnp.arange(GROUPS, dtype=jnp.int32)[:, None]
    pads = jax.random.randint(jax.random.fold_in(key, 11), (GROUPS, 1), 1, TOK_DEV // 2 + 1)
    pads = jnp.where(group_index == 0, 1, pads).astype(jnp.int32)
    lengths = jax.random.randint(jax.random.fold_in(key, 12), (GROUPS, TOK_DEV), 1, PAGE_MOST + 1)
    lengths = jnp.where(group_index == 0, 1, lengths)
    position = jnp.arange(TOK_DEV, dtype=jnp.int32)[None, :]
    lengths = jnp.where(position == 0, PAGE_MOST, lengths).astype(jnp.int32)
    numbers = jax.vmap(row_pages)(jnp.cumsum(lengths, axis=1).astype(jnp.int32))
    numbers = jnp.where(position >= TOK_DEV - pads, -1, numbers)
    numbers = numbers.reshape(GROUPS // PAIRS_DOC, 1, PAIRS_DOC, TOK_DEV)
    numbers = jnp.broadcast_to(numbers, (GROUPS // PAIRS_DOC, 2, PAIRS_DOC, TOK_DEV))
    return numbers.reshape(ROWS).astype(jnp.int32)


def grad_size(weight_kind):
    return weight_kind * math.sqrt(BLOCKS)


def first_moment(key, shape, weight_kind):
    return grad_size(weight_kind) / 9.0 * jax.random.normal(jax.random.fold_in(key, 21), shape, jnp.float32)


def second_moment(key, shape, weight_kind):
    spread = jnp.exp(jax.random.uniform(jax.random.fold_in(key, 22), shape, jnp.float32, 0.0, math.log(4.0)))
    return 0.001001 * grad_size(weight_kind) ** 2 * spread


def draw_m_qkv(key, part):
    return first_moment(key, (2, D, 3 * D), 0.15)


def draw_v_qkv(key, part):
    return second_moment(key, (2, D, 3 * D), 0.15)


def draw_m_out(key, part):
    return first_moment(key, (2, D, D), 0.3)


def draw_v_out(key, part):
    return second_moment(key, (2, D, D), 0.3)


def draw_m_up(key, part):
    return first_moment(key, (2, D, FF), 0.25)


def draw_v_up(key, part):
    return second_moment(key, (2, D, FF), 0.25)


def draw_m_down(key, part):
    return first_moment(key, (2, FF, D), 0.6)


def draw_v_down(key, part):
    return second_moment(key, (2, FF, D), 0.6)


def draw_m_gains(key, part):
    return first_moment(key, (5, D), 0.3)


def draw_v_gains(key, part):
    return second_moment(key, (5, D), 0.3)


def draw_gains(key, part):
    norm_rows = jax.random.uniform(jax.random.fold_in(key, 31), (4, D), jnp.float32, 0.6, 1.4)
    gate_row = jax.random.uniform(jax.random.fold_in(key, 32), (1, D), jnp.float32, -2.0, 2.0)
    return jnp.concatenate((norm_rows, gate_row), axis=0)


def plant(drawn, key, low, high):
    place = [jax.random.randint(jax.random.fold_in(key, axis), (), 0, length) for axis, length in enumerate(drawn.shape)]
    widest = drawn.shape.index(max(drawn.shape))
    beside = place[:widest] + [(place[widest] + 1) % drawn.shape[widest]] + place[widest + 1:]
    return drawn.at[tuple(place)].set(low).at[tuple(beside)].set(high)


def level_of(stream_key, dims, cuts, least, high):
    factor_of, own = 1.0, jax.random.fold_in(stream_key, 6)
    for dim, parts in cuts:
        steps = jnp.exp(jax.random.uniform(jax.random.fold_in(own, dim), (parts,), jnp.float32, least / len(cuts), high / len(cuts)))
        factor_of = factor_of * jnp.repeat(steps, dims[dim] // parts).reshape([-1 if axis == dim else 1 for axis in range(len(dims))])
    return factor_of


def scatter_about(key, shape, deviation, most, shards=(), kind=jnp.bfloat16):
    level = level_of(key, shape, shards, -0.22, 0.18) if shards else 1.0
    values = jax.random.normal(key, shape, jnp.float32) * deviation * level
    return jnp.minimum(jnp.maximum(values, -most), most).astype(kind)


def setup_inputs(seed: int = 0) -> dict:
    seeds = jax.random.split(jax.random.key(seed), 21)
    rows = scatter_about(seeds[0], (ROWS, D), 1.0, 6.0, ((0, 32),))
    cot_stream = scatter_about(seeds[1], (ROWS, D), 1.0, 6.0, ((0, 32),), jnp.float32)
    cot_joined = scatter_about(seeds[2], (BLOCKS, D), 1.0, 6.0, ((0, 32),), jnp.float32)
    page = draw_page(jax.random.fold_in(seeds[20], 71), 0)
    key_mask = plant((jax.random.randint(seeds[4], (ROWS,), 0, 4) < 3).astype(jnp.int32), jax.random.fold_in(seeds[4], 1), 0, 1)
    w_qkv = scatter_about(seeds[5], (2, D, 3 * D), D ** -0.5, 0.21875, ((1, 8), (2, 4)), jnp.float32)
    m_qkv = draw_m_qkv(jax.random.fold_in(seeds[20], 71), 0)
    v_qkv = draw_v_qkv(jax.random.fold_in(seeds[20], 71), 0)
    w_out = scatter_about(seeds[8], (2, D, D), (D // 16) ** -0.5, 0.875, ((1, 8), (2, 4)), jnp.float32)
    m_out = draw_m_out(jax.random.fold_in(seeds[20], 71), 0)
    v_out = draw_v_out(jax.random.fold_in(seeds[20], 71), 0)
    w_up = scatter_about(seeds[11], (2, D, FF), D ** -0.5, 0.21875, ((1, 8), (2, 4)), jnp.float32)
    m_up = draw_m_up(jax.random.fold_in(seeds[20], 71), 0)
    v_up = draw_v_up(jax.random.fold_in(seeds[20], 71), 0)
    w_down = scatter_about(seeds[14], (2, FF, D), FF ** -0.5, 0.109375, ((1, 8), (2, 4)), jnp.float32)
    m_down = draw_m_down(jax.random.fold_in(seeds[20], 71), 0)
    v_down = draw_v_down(jax.random.fold_in(seeds[20], 71), 0)
    gains = draw_gains(jax.random.fold_in(seeds[20], 71), 0)
    m_gains = draw_m_gains(jax.random.fold_in(seeds[20], 71), 0)
    v_gains = draw_v_gains(jax.random.fold_in(seeds[20], 71), 0)
    return dict(rows=rows, cot_stream=cot_stream, cot_joined=cot_joined, page=page, key_mask=key_mask, w_qkv=w_qkv, m_qkv=m_qkv, v_qkv=v_qkv, w_out=w_out, m_out=m_out, v_out=v_out, w_up=w_up, m_up=m_up, v_up=v_up, w_down=w_down, m_down=m_down, v_down=v_down, gains=gains, m_gains=m_gains, v_gains=v_gains)


@jax.custom_vjp
def low(v):
    return lax.optimization_barrier(v.astype(jnp.bfloat16)).astype(jnp.float32)

@jax.custom_vjp
def low_back(v):
    return v

def low_keep(v):
    return (low(v), None)

def low_pass(kept, grad):
    return (grad,)

def back_keep(v):
    return (v, None)

def back_low(kept, grad):
    return (low(grad),)
low.defvjp(low_keep, low_pass)
low_back.defvjp(back_keep, back_low)

def layer_norm(values, gain):
    centred = values - lax.optimization_barrier(jnp.mean(values, axis=-1, keepdims=True))
    spread = lax.optimization_barrier(jnp.mean(centred * centred, axis=-1, keepdims=True))
    return centred * lax.rsqrt(spread + 1e-05) * gain

def gelu_tanh(values):
    return jax.nn.gelu(values, approximate=True)

def matmul(left, right):
    return jnp.dot(left, right, precision=lax.Precision.HIGHEST)

def by_pairs(array):
    shaped = array.reshape((N_DOCS, 2, N_WIDE // 2, TOK_DEV) + array.shape[1:])
    shaped = jnp.swapaxes(shaped, 0, 1)
    return shaped.reshape((2, N_DOCS * (N_WIDE // 2), TOK_DEV) + array.shape[1:])

def project_stream(inputs, gain, qkv_weight):
    normed = low(layer_norm(inputs, gain))
    projected = low(low_back(matmul(normed, qkv_weight)))
    return (projected[:, :D], projected[:, D:])

def finish_stream(inputs, queries, partner, pages, key_mask, gain, out_weight, up_weight, down_weight):
    rows_here = inputs.shape[0]
    head_size = D // HEADS
    factor = float(head_size) ** (-0.5)
    valid_rows = (pages >= 0).astype(inputs.dtype)[:, None]
    position = jnp.arange(rows_here)
    allowed = (pages[:, None] == pages[None, :]) & ((key_mask[None, :] == 1) | (position[:, None] == position[None, :]))
    query_heads = queries.reshape(rows_here, HEADS, head_size)
    key_heads = partner[:, :D].reshape(rows_here, HEADS, head_size)
    value_heads = partner[:, D:].reshape(rows_here, HEADS, head_size)
    raw = jnp.einsum('qhd,khd->hqk', query_heads, key_heads, precision=lax.Precision.HIGHEST) * factor
    scores = jnp.where(allowed[None], low_back(raw), -1000000000.0)
    row_top = lax.optimization_barrier(jnp.max(scores, axis=-1, keepdims=True))
    exponent = jnp.exp(scores - row_top)
    probability = low(exponent / lax.optimization_barrier(jnp.sum(exponent, axis=-1, keepdims=True)))
    attended = jnp.einsum('hqk,khd->qhd', probability, value_heads, precision=lax.Precision.HIGHEST).reshape(rows_here, D)
    attended = low(low_back(attended))
    middle = inputs + valid_rows * low_back(matmul(attended, out_weight))
    normed = low(layer_norm(middle, gain))
    hidden = low(gelu_tanh(low_back(matmul(normed, up_weight))))
    return middle + valid_rows * low_back(matmul(hidden, down_weight))

def forward(params, inputs, page, key_mask):
    qkv_weight, out_weight, up_weight, down_weight, gains = params
    rows_split = by_pairs(inputs)
    page_split = by_pairs(page)
    mask_split = by_pairs(key_mask)

    def stream_weights(index):
        return (low(qkv_weight[index]), low(out_weight[index]), low(up_weight[index]), low(down_weight[index]))
    text_weights = stream_weights(0)
    image_weights = stream_weights(1)

    def pair_rows(pieces):
        text_in, image_in, pages, text_mask, image_mask = pieces
        text_query, text_kv = project_stream(text_in, gains[0], text_weights[0])
        image_query, image_kv = project_stream(image_in, gains[1], image_weights[0])
        text_out = finish_stream(text_in, text_query, image_kv, pages, text_mask, gains[2], text_weights[1], text_weights[2], text_weights[3])
        image_out = finish_stream(image_in, image_query, text_kv, pages, image_mask, gains[3], image_weights[1], image_weights[2], image_weights[3])
        gate_mix = jax.nn.sigmoid(gains[4])
        return (text_out, image_out, gate_mix * text_out + (1.0 - gate_mix) * image_out)
    text_out, image_out, joined_rows = lax.map(jax.checkpoint(pair_rows), (rows_split[0], rows_split[1], page_split[0], mask_split[0], mask_split[1]))
    both = jnp.stack((text_out, image_out)).reshape(2, N_DOCS, N_WIDE // 2, TOK_DEV, D)
    stream_out = jnp.swapaxes(both, 0, 1).reshape(ROWS, D)
    joined = joined_rows.reshape(N_DOCS, N_WIDE // 2, 2, TOK_DEV // 2, D).transpose(0, 2, 1, 3, 4).reshape(BLOCKS, D)
    return (stream_out, joined)

def adam_update(weight, first, second, grad, rate, decay):
    first_new = 0.9 * first + 0.1 * grad
    second_new = 0.999 * second + 0.001 * grad * grad
    first_hat = first_new / (1.0 - 0.9 ** STEP)
    second_hat = second_new / (1.0 - 0.999 ** STEP)
    weight_new = weight - rate * (first_hat / (jnp.sqrt(second_hat) + 1e-08) + decay * weight)
    return (weight_new, first_new, second_new)

def reference(rows, cot_stream, cot_joined, page, key_mask, w_qkv, m_qkv, v_qkv, w_out, m_out, v_out, w_up, m_up, v_up, w_down, m_down, v_down, gains, m_gains, v_gains):
    inputs = rows.astype(jnp.float32)

    def whole_layer(params, values):
        return forward(params, values, page, key_mask)
    (stream_out, joined), pullback = jax.vjp(whole_layer, (w_qkv, w_out, w_up, w_down, gains), inputs)
    param_grads, grad_rows = pullback((cot_stream, cot_joined))
    qkv_new = adam_update(w_qkv, m_qkv, v_qkv, param_grads[0], 0.12, 0.01)
    out_new = adam_update(w_out, m_out, v_out, param_grads[1], 0.5, 0.01)
    up_new = adam_update(w_up, m_up, v_up, param_grads[2], 0.12, 0.01)
    down_new = adam_update(w_down, m_down, v_down, param_grads[3], 0.06, 0.01)
    gains_new = adam_update(gains, m_gains, v_gains, param_grads[4], 0.8, 0.0)
    return (stream_out, joined, grad_rows, qkv_new[0], qkv_new[1], qkv_new[2], out_new[0], out_new[1], out_new[2], up_new[0], up_new[1], up_new[2], down_new[0], down_new[1], down_new[2], gains_new[0], gains_new[1], gains_new[2])
```

```python
import functools

import jax
import jax.numpy as jnp
from jax import lax
from jax.experimental import pallas as pl
from jax.experimental.pallas import tpu as pltpu
from jax.sharding import PartitionSpec as P

HEADS = 12
STEP = 10
LANES = 128
CHUNK = 128
NEG = -1000000000.0
LOW = jnp.bfloat16
FULL = jnp.float32


def flip(value, axis, mask):
    count = lax.axis_size(axis)
    return lax.ppermute(value, axis, [(i, i ^ mask) for i in range(count)])


def flipped(codes, axis, mask):
    d_mask = mask if axis == "docs" else 0
    w_mask = mask if axis == "wide" else 0
    return [(d ^ d_mask, w ^ w_mask) for d, w in codes]


def gather(unit, order):
    arrays, codes = [unit[None]], [[(0, 0)]]
    for axis, mask in order:
        held = arrays[0] if len(arrays) == 1 else jnp.concatenate(arrays, axis=0)
        known = [code for group in codes for code in group]
        arrays.append(flip(held, axis, mask))
        codes.append(flipped(known, axis, mask))
    return arrays, codes


def sum_codes(order):
    codes = [(0, 0)]
    for axis, mask in reversed(order):
        codes = codes + flipped(codes, axis, mask)
    return codes


def reduce_pieces(keep, send, order):
    parts = [keep]
    outgoing = send
    for step, (axis, mask) in enumerate(order):
        parts.append(flip(outgoing, axis, mask))
        if step + 1 < len(order):
            half = parts[0].shape[0] // 2
            outgoing = sum(part[half:].astype(FULL) for part in parts).astype(LOW)
            parts = [part[:half] for part in parts]
    return sum(part[0].astype(FULL) for part in parts)


def small_sum(value, steps):
    for axis, mask in steps:
        value = value + flip(value, axis, mask)
    return value


class Blocks:
    def __init__(self, count, size):
        self.count, self.size = count, size
        shifts = [(i * size) % LANES for i in range(count)]
        self.shifts = sorted(set(shifts))
        self.wide = -(-(size + max(shifts)) // LANES) * LANES
        self.aligned = max(shifts) == 0 and size % LANES == 0
        self.total = count * size
        self.room = max(self.start(i) + self.wide for i in range(count))

    def start(self, index):
        return index * self.size // LANES * LANES

    def start_dynamic(self, index):
        return pl.multiple_of(index * self.size // LANES * LANES, LANES)

    def pad(self, value, index):
        result = None
        for shift in self.shifts:
            low = [(0, 0)] * (value.ndim - 1) + [(shift, self.wide - self.size - shift)]
            placed = jnp.pad(value, low)
            here = (index * self.size) % LANES == shift
            result = placed if result is None else jnp.where(here, placed, result)
        return result

    def cut(self, value, index):
        result = None
        for shift in self.shifts:
            piece = value[..., shift : shift + self.size]
            here = (index * self.size) % LANES == shift
            result = piece if result is None else jnp.where(here, piece, result)
        return result

    def tile_owners(self, tile):
        low, high = tile * LANES, (tile + 1) * LANES
        return [
            (i, low - self.start(i))
            for i in range(self.count)
            if i * self.size < high and (i + 1) * self.size > low
        ]


def matmul(left, right):
    return lax.dot_general(left, right, (((1,), (0,)), ((), ())), preferred_element_type=FULL)


def matmul_nt(left, right):
    return lax.dot_general(left, right, (((1,), (1,)), ((), ())), preferred_element_type=FULL)


def matmul_tn(left, right):
    return lax.dot_general(left, right, (((0,), (0,)), ((), ())), preferred_element_type=FULL)


def normed(values):
    centred = values - jnp.mean(values, axis=-1, keepdims=True)
    spread = jnp.mean(centred * centred, axis=-1, keepdims=True)
    scale = lax.rsqrt(spread + 1e-05)
    return centred * scale, scale


def norm_back(grad, unit, scale, gain):
    inner = grad * gain
    mean_inner = jnp.mean(inner, axis=-1, keepdims=True)
    mean_both = jnp.mean(inner * unit, axis=-1, keepdims=True)
    return scale * (inner - mean_inner - unit * mean_both)


def rows_at(index, size=CHUNK):
    return pl.ds(pl.multiple_of(index * size, size), size)


def places(pos, codes, half):
    for index, (d_mask, w_mask) in enumerate(codes):
        doc = pos[0] ^ d_mask
        inner = pos[1] ^ w_mask
        for slot in (0, 1):
            owner = pos[2] if slot == 0 else 1 - pos[2]
            yield index, slot, doc, owner * half + inner


def load_pieces(pos, refs, codes, half, lanes, target, sem):
    for ref, group in zip(refs, codes):
        for index, slot, doc, inner in places(pos, group, half):
            pltpu.make_async_copy(
                ref.at[index, slot, :, pl.ds(lanes[0], lanes[1])], target(doc, inner), sem
            ).start()


def wait_whole(ref, sem):
    pltpu.make_async_copy(ref, ref, sem).wait()


def row_target(ref, blocks, rows):
    if blocks.aligned:
        return lambda doc, inner: ref.at[
            pl.ds(pl.multiple_of(inner * rows, rows), rows),
            pl.ds(blocks.start_dynamic(doc), blocks.wide),
        ]
    return lambda doc, inner: ref.at[doc, pl.ds(pl.multiple_of(inner * rows, rows), rows), :]


def column_target(ref, blocks, rows):
    if blocks.aligned:
        return lambda doc, inner: ref.at[
            pl.ds(pl.multiple_of(doc * rows, rows), rows),
            pl.ds(blocks.start_dynamic(inner), blocks.wide),
        ]
    return lambda doc, inner: ref.at[inner, pl.ds(pl.multiple_of(doc * rows, rows), rows), :]


def held_shape(blocks, height):
    return (height, blocks.total) if blocks.aligned else (blocks.count, height, blocks.wide)


def merge_tiles(held, whole, blocks):
    for tile in range(blocks.total // LANES):
        value = None
        for index, offset in blocks.tile_owners(tile):
            piece = held[index, :, offset : offset + LANES]
            value = piece if value is None else value + piece
        whole[:, tile * LANES : (tile + 1) * LANES] = value


def project_kernel(
    shape, pos, own, other, gains, page_col, page_row, mask_row, *refs
):
    codes, half, rows, blocks, length, width, factor = shape
    pieces = refs[: len(codes)]
    (q_out, k_out, v_out, att_out, lse_out, weight) = refs[len(codes) : len(codes) + 6]
    (held, h_own, h_oth, allowed, sem) = refs[len(codes) + 6 :]
    load_pieces(pos, pieces, codes, half, (0, blocks.wide), row_target(held, blocks, rows), sem)
    for i in range(length // CHUNK):
        part = pl.ds(i * CHUNK, CHUNK)
        unit, _ = normed(own[part, :].astype(FULL))
        h_own[part, :] = (unit * gains[0:1, :]).astype(LOW)
        unit, _ = normed(other[part, :].astype(FULL))
        h_oth[part, :] = (unit * gains[1:2, :]).astype(LOW)
        row = lax.broadcasted_iota(jnp.int32, (CHUNK, length), 0) + i * CHUNK
        col = lax.broadcasted_iota(jnp.int32, (CHUNK, length), 1)
        ok = (page_col[part, :] == page_row[...]) & ((mask_row[...] == 1) | (row == col))
        allowed[part, :] = jnp.where(ok, 1.0, 0.0)
    wait_whole(held, sem)
    merge_tiles(held, weight, blocks)
    lse_out[...] = jnp.zeros_like(lse_out)

    q_out[...] = (matmul(h_own[...], weight[:, :width]).astype(LOW) * factor).astype(LOW)
    k_out[...] = matmul(h_oth[...], weight[:, width : 2 * width]).astype(LOW)
    v_out[...] = matmul(h_oth[...], weight[:, 2 * width :]).astype(LOW)
    size = width // HEADS
    per = LANES // size

    @pl.loop(0, width // LANES)
    def _(pair):
        cols = pl.ds(pl.multiple_of(pair * LANES, LANES), LANES)
        keys = k_out[:, cols]
        values = v_out[:, cols]
        for i in range(length // CHUNK):
            part = pl.ds(i * CHUNK, CHUNK)
            queries = q_out[part, cols]
            lane = lax.broadcasted_iota(jnp.int32, queries.shape, 1)
            result = None
            sums = lse_out[part, :]
            for sub in range(per):
                inside = lane // size == sub
                scores = matmul_nt(jnp.where(inside, queries, jnp.zeros_like(queries)), keys)
                scores = jnp.where(allowed[part, :] > 0.5, scores, NEG)
                top = jnp.max(scores, axis=-1, keepdims=True)
                exps = jnp.exp(scores - top)
                total = jnp.sum(exps, axis=-1, keepdims=True)
                probs = (exps * (1.0 / total)).astype(LOW)
                out = matmul(probs, values)
                result = out if result is None else jnp.where(inside, out, result)
                sums = jnp.where(lane == pair * per + sub, top + jnp.log(total), sums)
            lse_out[part, :] = sums
            att_out[part, cols] = result.astype(LOW)


def feed_kernel(
    shape, pos, att, own, cot, cotj_own, cotj_oth, coef, gain, page_col, *refs
):
    (up_codes, down_codes, up_sums, down_sums, half, rows, down_rows, ups, outs, downs, length, width, hidden, block) = shape
    n_up, n_down = len(up_codes), len(down_codes)
    up_pieces, down_pieces = refs[:n_up], refs[n_up : n_up + n_down]
    refs = refs[n_up + n_down :]
    (out_ref, away_ref, dmid_ref, datt_ref, dgain_ref, up_keep, up_send, down_keep, down_send) = refs[:9]
    (w_up, o_held, w_out, d_held, w_down, g_up, g_out, g_down, mid, unit_ref, scale_ref, dz, h2, h2_t, dffn, dffn_t, att_t, acts, dpre, acc, dacc, dbranch, sem_up, sem_out, sem_down, sem_keep, sem_send, sem_dkeep, sem_dsend) = refs[9:]
    load_pieces(pos, up_pieces, up_codes, half, (ups.wide, outs.wide), row_target(o_held, outs, rows), sem_out)
    load_pieces(pos, up_pieces, up_codes, half, (0, ups.wide), row_target(w_up, ups, rows), sem_up)
    load_pieces(pos, down_pieces, down_codes, half, (0, downs.wide), column_target(d_held, downs, down_rows), sem_down)
    half_rows = length // 2
    parts = length // CHUNK
    for which, ref in ((pos[2], cotj_own), (1 - pos[2], cotj_oth)):
        for i in range(half_rows // CHUNK):
            part = pl.ds(pl.multiple_of(which * half_rows + i * CHUNK, CHUNK), CHUNK)
            grad = cot[part, :] + coef[...] * ref[pl.ds(i * CHUNK, CHUNK), :].astype(FULL)
            valid = jnp.where(page_col[part, :] >= 0, 1.0, 0.0)
            dz[part, :] = grad
            dffn[part, :] = (grad * valid).astype(LOW)
    dffn_t[...] = dffn[...].T
    att_t[...] = att[...].T
    wait_whole(o_held, sem_out)
    merge_tiles(o_held, w_out, outs)

    @pl.loop(0, parts)
    def _(i):
        part = rows_at(i)
        valid = jnp.where(page_col[part, :] >= 0, 1.0, 0.0)
        middle = own[part, :].astype(FULL) + valid * matmul(att[part, :], w_out[...])
        unit, scale = normed(middle)
        mid[part, :] = middle
        unit_ref[part, :] = unit
        scale_ref[part, :] = jnp.broadcast_to(scale, (CHUNK, LANES))
        h2[part, :] = (unit * gain[...]).astype(LOW)

    h2_t[...] = h2[...].T
    acc[...] = jnp.zeros_like(acc)
    dacc[...] = jnp.zeros_like(dacc)
    wait_whole(w_up, sem_up)
    wait_whole(d_held, sem_down)
    if not downs.aligned:
        merge_tiles(d_held, w_down, downs)
    down = d_held if downs.aligned else w_down
    c0, c1 = 0.7978845608028654, 0.044715

    @pl.loop(0, hidden // block)
    def _(f):
        cols = pl.ds(pl.multiple_of(f * block, LANES), block)

        @pl.loop(0, parts)
        def _(i):
            part = rows_at(i)
            pre = matmul(h2[part, :], w_up[:, cols])
            dact = matmul(dffn[part, :], down[:, cols])
            square = pre * pre
            flat = jnp.tanh(c0 * (pre + c1 * square * pre))
            cdf = 0.5 * (1.0 + flat)
            slope = cdf + pre * (0.5 * (1.0 - flat * flat)) * (c0 * (1.0 + 3.0 * c1 * square))
            act = (pre * cdf).astype(LOW)
            dp = (slope * dact).astype(LOW)
            acts[part, :] = act
            dpre[part, :] = dp
            acc[part, :] += matmul_nt(act, down[:, cols])
            dacc[part, :] += matmul_nt(dp, w_up[:, cols])

        g_down[:, cols] = matmul(dffn_t[...], acts[...]).astype(LOW)
        g_up[:, cols] = matmul(h2_t[...], dpre[...]).astype(LOW)

    if downs.room > downs.total:
        g_down[:, downs.total :] = jnp.zeros((width, downs.room - downs.total), LOW)
    if outs.room > outs.total:
        g_out[:, outs.total :] = jnp.zeros((width, outs.room - outs.total), LOW)
    for codes, keep, send, s_keep, s_send in ((down_sums, down_keep, down_send, sem_dkeep, sem_dsend),):
        count = len(codes) // 2
        for index, slot, doc, inner in places(pos, codes, half):
            target, sem = (keep, s_keep) if index < count else (send, s_send)
            pltpu.make_async_copy(
                g_down.at[
                    pl.ds(pl.multiple_of(doc * down_rows, down_rows), down_rows),
                    pl.ds(downs.start_dynamic(inner), downs.wide),
                ],
                target.at[index % count, slot],
                sem,
            ).start()
    count = len(up_sums) // 2
    for index, slot, doc, inner in places(pos, up_sums, half):
        target, sem = (up_keep, sem_keep) if index < count else (up_send, sem_send)
        height = pl.ds(pl.multiple_of(inner * rows, rows), rows)
        pltpu.make_async_copy(
            g_up.at[height, pl.ds(ups.start_dynamic(doc), ups.wide)],
            target.at[index % count, slot, :, pl.ds(0, ups.wide)],
            sem,
        ).start()

    dgain_ref[...] = jnp.zeros_like(dgain_ref)

    @pl.loop(0, parts)
    def _(i):
        part = rows_at(i)
        valid = jnp.where(page_col[part, :] >= 0, 1.0, 0.0)
        out_ref[part, :] = mid[part, :] + valid * acc[part, :]
        grad, unit = dacc[part, :], unit_ref[part, :]
        dgain_ref[0:1, :] += jnp.sum(grad * unit, axis=0, keepdims=True)
        dmid = dz[part, :] + norm_back(grad, unit, scale_ref[part, 0:1], gain[...])
        dmid_ref[part, :] = dmid
        low = (dmid * valid).astype(LOW)
        dbranch[part, :] = low
        datt_ref[part, :] = matmul_nt(low, w_out[...]).astype(LOW)

    for i in range(half_rows // CHUNK):
        part = pl.ds(pl.multiple_of((1 - pos[2]) * half_rows + i * CHUNK, CHUNK), CHUNK)
        away_ref[pl.ds(i * CHUNK, CHUNK), :] = out_ref[part, :].astype(LOW)
    g_out[:, : outs.total] = matmul(att_t[...], dbranch[...]).astype(LOW)
    for index, slot, doc, inner in places(pos, up_sums, half):
        target, sem = (up_keep, sem_keep) if index < count else (up_send, sem_send)
        height = pl.ds(pl.multiple_of(inner * rows, rows), rows)
        pltpu.make_async_copy(
            g_out.at[height, pl.ds(outs.start_dynamic(doc), outs.wide)],
            target.at[index % count, slot, :, pl.ds(ups.wide, outs.wide)],
            sem,
        ).start()
    wait_whole(down_keep, sem_dkeep)
    wait_whole(down_send, sem_dsend)
    wait_whole(up_keep, sem_keep)
    wait_whole(up_send, sem_send)


def back_kernel(
    shape, pos, own, other, gains, page_col, page_row, mask_col, q_ref, k_ref, v_ref, att, datt, lse, weight, *refs
):
    (codes, half, rows, blocks, length, width, factor) = shape
    (own_ref, oth_ref, dgain_ref, keep, send) = refs[:5]
    (dq, dk, dv, h_t, allowed, flat, lse_t, dots_t, dscore, grad, sem_keep, sem_send) = refs[5:]
    size = width // HEADS
    per = LANES // size
    parts = length // CHUNK
    for i in range(parts):
        part = pl.ds(i * CHUNK, CHUNK)
        row = lax.broadcasted_iota(jnp.int32, (CHUNK, length), 0) + i * CHUNK
        col = lax.broadcasted_iota(jnp.int32, (CHUNK, length), 1)
        ok = (page_col[part, :] == page_row[...]) & ((mask_col[part, :] == 1) | (row == col))
        allowed[part, :] = jnp.where(ok, 1.0, 0.0)
    head = lax.broadcasted_iota(jnp.int32, (LANES, width), 0)
    lane = lax.broadcasted_iota(jnp.int32, (LANES, width), 1)
    chosen = jnp.where(lane // size == head, 1.0, 0.0)
    flat[...] = att[...].astype(FULL) * datt[...].astype(FULL)
    dots_t[...] = lax.dot_general(
        chosen, flat[...], (((1,), (1,)), ((), ())), preferred_element_type=FULL,
        precision=lax.Precision.HIGHEST,
    )
    lse_t[...] = lse[...].T

    @pl.loop(0, width // LANES)
    def _(pair):
        cols = pl.ds(pl.multiple_of(pair * LANES, LANES), LANES)
        queries, grads, keys_all = q_ref[:, cols], datt[:, cols], k_ref[:, cols]
        lane = lax.broadcasted_iota(jnp.int32, (length, LANES), 1)
        lane_part = lax.broadcasted_iota(jnp.int32, (CHUNK, LANES), 1)
        zero = jnp.zeros_like(queries)
        dq_pair = None
        for sub in range(per):
            inside = lane // size == sub
            inside_part = lane_part // size == sub
            q_head = jnp.where(inside, queries, zero)
            g_head = jnp.where(inside, grads, zero)
            lse_row = lse_t[pl.ds(pair * per + sub, 1), :]
            dot_row = dots_t[pl.ds(pair * per + sub, 1), :]
            for i in range(parts):
                part = pl.ds(i * CHUNK, CHUNK)
                scores = matmul_nt(k_ref[part, cols], q_head)
                scores = jnp.where(allowed[part, :] > 0.5, scores, NEG)
                probs = jnp.exp(scores - lse_row)
                dprob = matmul_nt(v_ref[part, cols], g_head)
                low = (probs * (dprob - dot_row)).astype(LOW)
                dscore[part, :] = low
                dv_part = matmul(probs.astype(LOW), grads).astype(LOW)
                dk_part = matmul(low, queries).astype(LOW)
                if sub > 0:
                    dv_part = jnp.where(inside_part, dv_part, dv[part, cols])
                    dk_part = jnp.where(inside_part, dk_part, dk[part, cols])
                dv[part, cols] = dv_part
                dk[part, cols] = dk_part
            dq_head = matmul_tn(dscore[...], keys_all)
            dq_pair = dq_head if dq_pair is None else jnp.where(inside, dq_head, dq_pair)
        dq[:, cols] = (dq_pair * factor).astype(LOW)

    for which, source in ((0, own), (1, other)):
        for i in range(parts):
            part = pl.ds(i * CHUNK, CHUNK)
            unit, _ = normed(source[part, :].astype(FULL))
            flat[part, :] = unit * gains[which : which + 1, :]
        h_t[which] = flat[...].astype(LOW).T
    grad[:, :width] = matmul(h_t[0], dq[...]).astype(LOW)
    grad[:, width : 2 * width] = matmul(h_t[1], dk[...]).astype(LOW)
    grad[:, 2 * width : 3 * width] = matmul(h_t[1], dv[...]).astype(LOW)
    if blocks.room > blocks.total:
        grad[:, blocks.total :] = jnp.zeros((width, blocks.room - blocks.total), LOW)
    count = len(codes) // 2
    for index, slot, doc, inner in places(pos, codes, half):
        target, sem = (keep, sem_keep) if index < count else (send, sem_send)
        pltpu.make_async_copy(
            grad.at[
                pl.ds(pl.multiple_of(inner * rows, rows), rows),
                pl.ds(blocks.start_dynamic(doc), blocks.wide),
            ],
            target.at[index % count, slot],
            sem,
        ).start()
    dgain_ref[...] = jnp.zeros_like(dgain_ref)
    for i in range(parts):
        part = pl.ds(i * CHUNK, CHUNK)
        unit, _ = normed(own[part, :].astype(FULL))
        value = matmul_nt(dq[part, :], weight[:, :width])
        own_ref[part, :] = value
        dgain_ref[0:1, :] += jnp.sum(value * unit, axis=0, keepdims=True)
        unit, _ = normed(other[part, :].astype(FULL))
        value = matmul_nt(dk[part, :], weight[:, width : 2 * width])
        value = value + matmul_nt(dv[part, :], weight[:, 2 * width :])
        oth_ref[part, :] = value.astype(LOW)
        dgain_ref[1:2, :] += jnp.sum(value * unit, axis=0, keepdims=True)
    wait_whole(keep, sem_keep)
    wait_whole(send, sem_send)


def tail_kernel(length, own, gain, mine, theirs, dmid, out_ref):
    for i in range(length // CHUNK):
        part = pl.ds(i * CHUNK, CHUNK)
        unit, scale = normed(own[part, :].astype(FULL))
        grad = mine[part, :] + theirs[part, :].astype(FULL)
        out_ref[part, :] = dmid[part, :] + norm_back(grad, unit, scale, gain[...])


VMEM = pl.BlockSpec(memory_space=pltpu.VMEM)
ANY = pl.BlockSpec(memory_space=pl.ANY)
SMEM = pl.BlockSpec(memory_space=pltpu.SMEM)


def params(mebibytes):
    return pltpu.CompilerParams(vmem_limit_bytes=mebibytes * 1024 * 1024)


def adam_update(weight, first, second, grad, rate, decay):
    first_new = 0.9 * first + 0.1 * grad
    second_new = 0.999 * second + 0.001 * grad * grad
    first_hat = first_new / (1.0 - 0.9**STEP)
    second_hat = second_new / (1.0 - 0.999**STEP)
    weight_new = weight - rate * (first_hat / (jnp.sqrt(second_hat) + 1e-08) + decay * weight)
    return (weight_new, first_new, second_new)


def shards(
    rows, cot_stream, cot_joined, page, key_mask,
    w_qkv, m_qkv, v_qkv, w_out, m_out, v_out, w_up, m_up, v_up, w_down, m_down, v_down,
    gains, m_gains, v_gains,
):
    docs, wide = lax.axis_size("docs"), lax.axis_size("wide")
    half = wide // 2
    doc, place = lax.axis_index("docs"), lax.axis_index("wide")
    stream = place // half
    is_text = stream == 0
    pos = jnp.stack((doc, place % half, stream)).astype(jnp.int32)
    length, width = rows.shape
    half_rows = length // 2
    factor = float(width // HEADS) ** (-0.5)
    piece_rows = w_qkv.shape[1]
    hidden = w_up.shape[2] * docs
    qkvs, outs, ups = Blocks(docs, w_qkv.shape[2]), Blocks(docs, w_out.shape[2]), Blocks(docs, w_up.shape[2])
    downs = Blocks(wide, w_down.shape[1])
    down_rows = w_down.shape[2]

    core = [("wide", 1)]
    along_x = [("docs", 1)]
    along_y = [("docs", 1 << b) for b in range(1, docs.bit_length() - 1)]
    along_z = [("wide", 1 << b) for b in range(1, half.bit_length() - 1)]
    across = ("wide", half)

    def swap(value):
        return flip(value, *across)

    other_rows = swap(rows)
    column = doc * w_qkv.shape[2] + lax.iota(jnp.int32, w_qkv.shape[2])
    is_query = (column < width)[None, None, :]
    pair_qkv = jnp.where(is_query, w_qkv, w_qkv[::-1]).astype(LOW)

    def own_first(pair):
        return jnp.where(is_text, pair, pair[::-1])

    unit_a = qkvs.pad(own_first(pair_qkv), doc)
    unit_b = jnp.concatenate(
        (ups.pad(own_first(w_up.astype(LOW)), doc), outs.pad(own_first(w_out.astype(LOW)), doc)), axis=-1
    )
    unit_c = downs.pad(jnp.swapaxes(own_first(w_down.astype(LOW)), 1, 2), place)
    unit_a = jnp.stack((unit_a[0], swap(unit_a[1])))
    unit_b = jnp.stack((unit_b[0], swap(unit_b[1])))
    if downs.aligned:
        unit_c = jnp.stack((unit_c[0], swap(unit_c[1])))
    else:
        raw = jnp.swapaxes(own_first(w_down.astype(LOW)), 1, 2)
        unit_c = jnp.stack((unit_c[0], downs.pad(swap(raw[1]), (place + half) % wide)))
    pieces_a, codes_a = gather(unit_a, along_z + along_x + along_y + core)
    pieces_b, codes_b = gather(unit_b, along_z + along_y + along_x + core)
    pieces_c, codes_c = gather(unit_c, along_x + along_z + along_y + core)
    other_joined = swap(cot_joined.astype(LOW))

    page_col, page_row = page[:, None], page[None, :]
    mask_col, mask_row = key_mask[:, None], key_mask[None, :]
    gain_own = lax.dynamic_index_in_dim(gains, stream, 0, keepdims=True)
    gain_oth = lax.dynamic_index_in_dim(gains, 1 - stream, 0, keepdims=True)
    gain_one = jnp.concatenate((gain_own, gain_oth), axis=0)
    gain_two = lax.dynamic_index_in_dim(gains, 2 + stream, 0, keepdims=True)
    mix = jax.nn.sigmoid(gains[4])[None, :]
    coef = jnp.where(is_text, mix, 1.0 - mix)

    low_rows = jax.ShapeDtypeStruct((length, width), LOW)
    full_rows = jax.ShapeDtypeStruct((length, width), FULL)

    shape = (codes_a, half, piece_rows, qkvs, length, width, factor)
    queries, keys, values, attended, lse, weight_qkv = pl.pallas_call(
        functools.partial(project_kernel, shape),
        out_shape=(low_rows, low_rows, low_rows, low_rows,
                   jax.ShapeDtypeStruct((length, LANES), FULL),
                   jax.ShapeDtypeStruct((width, 3 * width), LOW)),
        in_specs=[SMEM] + [VMEM] * 6 + [ANY] * len(pieces_a),
        out_specs=(VMEM,) * 6,
        scratch_shapes=[
            pltpu.VMEM((docs, width, qkvs.wide), LOW),
            pltpu.VMEM((length, width), LOW),
            pltpu.VMEM((length, width), LOW),
            pltpu.VMEM((length, length), FULL),
            pltpu.SemaphoreType.DMA,
        ],
        compiler_params=params(48),
        cost_estimate=pl.CostEstimate(flops=5_000_000_000, bytes_accessed=20_000_000, transcendentals=3_000_000),
        name="project_attend",
    )(pos, rows, other_rows, gain_one, page_col, page_row, mask_row, *pieces_a)

    order_b = core + along_x + along_y + along_z
    order_c = core + along_y + along_x + along_z
    order_a = core + along_x + along_y + along_z
    sums_a, sums_b, sums_c = sum_codes(order_a), sum_codes(order_b), sum_codes(order_c)
    sent = len(sums_a) // 2
    block = 3 * LANES
    shape = (codes_b, codes_c, sums_b, sums_c, half, piece_rows, down_rows, ups, outs, downs, length, width, hidden, block)
    shape_b = jax.ShapeDtypeStruct((sent, 2, piece_rows, ups.wide + outs.wide), LOW)
    shape_c = jax.ShapeDtypeStruct((sent, 2, down_rows, downs.wide), LOW)
    (stream_out, away, middle_grad, attended_grad, dgain_two, keep_b, send_b, keep_c, send_c) = pl.pallas_call(
        functools.partial(feed_kernel, shape),
        out_shape=(full_rows, jax.ShapeDtypeStruct((half_rows, width), LOW), full_rows, low_rows,
                   jax.ShapeDtypeStruct((8, width), FULL), shape_b, shape_b, shape_c, shape_c),
        in_specs=[SMEM] + [VMEM] * 8 + [ANY] * (len(pieces_b) + len(pieces_c)),
        out_specs=(VMEM,) * 5 + (ANY,) * 4,
        scratch_shapes=[
            pltpu.VMEM((width, hidden), LOW),
            pltpu.VMEM(held_shape(outs, width), LOW),
            pltpu.VMEM((width, width), LOW),
            pltpu.VMEM(held_shape(downs, width), LOW),
            pltpu.VMEM((8, LANES) if downs.aligned else (width, hidden), LOW),
            pltpu.VMEM((width, hidden), LOW),
            pltpu.VMEM((width, outs.room), LOW),
            pltpu.VMEM((width, downs.room), LOW),
            pltpu.VMEM((length, width), FULL),
            pltpu.VMEM((length, width), FULL),
            pltpu.VMEM((length, LANES), FULL),
            pltpu.VMEM((length, width), FULL),
            pltpu.VMEM((length, width), LOW),
            pltpu.VMEM((width, length), LOW),
            pltpu.VMEM((length, width), LOW),
            pltpu.VMEM((width, length), LOW),
            pltpu.VMEM((width, length), LOW),
            pltpu.VMEM((length, block), LOW),
            pltpu.VMEM((length, block), LOW),
            pltpu.VMEM((length, width), FULL),
            pltpu.VMEM((length, width), FULL),
            pltpu.VMEM((length, width), LOW),
        ] + [pltpu.SemaphoreType.DMA] * 7,
        compiler_params=params(60),
        cost_estimate=pl.CostEstimate(flops=17_000_000_000, bytes_accessed=45_000_000, transcendentals=1_600_000),
        name="feed_forward_back",
    )(pos, attended, rows, cot_stream, cot_joined, other_joined, coef, gain_two, page_col, *pieces_b, *pieces_c)

    partner_rows = swap(away)

    shape = (sums_a, half, piece_rows, qkvs, length, width, factor)
    shape_a = jax.ShapeDtypeStruct((sent, 2, piece_rows, qkvs.wide), LOW)
    own_part, away_part, dgain_one, keep_a, send_a = pl.pallas_call(
        functools.partial(back_kernel, shape),
        out_shape=(full_rows, low_rows, jax.ShapeDtypeStruct((8, width), FULL), shape_a, shape_a),
        in_specs=[SMEM] + [VMEM] * 13,
        out_specs=(VMEM,) * 3 + (ANY,) * 2,
        scratch_shapes=[
            pltpu.VMEM((length, width), LOW),
            pltpu.VMEM((length, width), LOW),
            pltpu.VMEM((length, width), LOW),
            pltpu.VMEM((2, width, length), LOW),
            pltpu.VMEM((length, length), FULL),
            pltpu.VMEM((length, width), FULL),
            pltpu.VMEM((LANES, length), FULL),
            pltpu.VMEM((LANES, length), FULL),
            pltpu.VMEM((length, length), LOW),
            pltpu.VMEM((width, qkvs.room), LOW),
        ] + [pltpu.SemaphoreType.DMA] * 2,
        compiler_params=params(56),
        cost_estimate=pl.CostEstimate(flops=9_000_000_000, bytes_accessed=20_000_000, transcendentals=3_000_000),
        name="attend_back",
    )(pos, rows, other_rows, gain_one, page_col, page_row, mask_col, queries, keys, values, attended, attended_grad, lse, weight_qkv)

    back_part = swap(away_part)
    grad_rows = pl.pallas_call(
        functools.partial(tail_kernel, length),
        out_shape=full_rows,
        in_specs=[VMEM] * 5,
        out_specs=VMEM,
        compiler_params=params(32),
        name="norm_tail",
    )(rows, gain_own, own_part, back_part, middle_grad)

    own_rows = lax.dynamic_slice_in_dim(stream_out, stream * half_rows, half_rows, 0)
    partner_rows = partner_rows.astype(FULL)
    text_rows = jnp.where(is_text, own_rows, partner_rows)
    image_rows = jnp.where(is_text, partner_rows, own_rows)
    joined_rows = mix * text_rows + (1.0 - mix) * image_rows
    gate_grad = jnp.sum(cot_joined * (text_rows - image_rows), axis=0, keepdims=True) * mix * (1.0 - mix)

    total_b = reduce_pieces(keep_b, send_b, order_b)
    total_c = reduce_pieces(keep_c, send_c, order_c)
    total_a = reduce_pieces(keep_a, send_a, order_a)

    def both(total):
        mine = total[0]
        theirs = swap(total[1].astype(LOW)).astype(FULL)
        return mine, theirs

    def placed(mine, theirs):
        return jnp.where(is_text, jnp.stack((mine, theirs)), jnp.stack((theirs, mine)))

    mine_b, theirs_b = both(total_b)
    grad_b = placed(mine_b, theirs_b)
    grad_up = ups.cut(grad_b[..., : ups.wide], doc)
    grad_out = outs.cut(grad_b[..., ups.wide :], doc)
    if downs.aligned:
        mine_c, theirs_c = both(total_c)
    else:
        mine_c = downs.cut(total_c[0], place)
        theirs_c = swap(downs.cut(total_c[1], (place + half) % wide).astype(LOW)).astype(FULL)
    grad_down = jnp.swapaxes(placed(mine_c, theirs_c), 1, 2)
    mine_a, theirs_a = both(total_a)
    mine_a, theirs_a = qkvs.cut(mine_a, doc), qkvs.cut(theirs_a, doc)
    query_here = is_query[0]
    grad_qkv = placed(
        jnp.where(query_here, mine_a, theirs_a), jnp.where(query_here, theirs_a, mine_a)
    )

    slot_index = lax.iota(jnp.int32, 5)[:, None]
    small_terms = (
        jnp.where(slot_index == stream, dgain_one[0:1], 0.0)
        + jnp.where(slot_index == 1 - stream, dgain_one[1:2], 0.0)
        + jnp.where(slot_index == 2 + stream, dgain_two[0:1], 0.0)
        + jnp.where(slot_index == 4, gate_grad, 0.0)
    )
    gains_grad = small_sum(small_terms, core + along_x + along_y + along_z + [across])

    qkv_new = adam_update(w_qkv, m_qkv, v_qkv, grad_qkv, 0.12, 0.01)
    out_new = adam_update(w_out, m_out, v_out, grad_out, 0.5, 0.01)
    up_new = adam_update(w_up, m_up, v_up, grad_up, 0.12, 0.01)
    down_new = adam_update(w_down, m_down, v_down, grad_down, 0.06, 0.01)
    gains_new = adam_update(gains, m_gains, v_gains, gains_grad, 0.8, 0.0)
    return (stream_out, joined_rows, grad_rows, *qkv_new, *out_new, *up_new, *down_new, *gains_new)


def solution(mesh):
    by_rows = P(("docs", "wide"), None)
    by_row = P(("docs", "wide"))
    weight = P(None, "wide", "docs")
    return jax.shard_map(
        shards,
        mesh=mesh,
        in_specs=(by_rows,) * 3 + (by_row,) * 2 + (weight,) * 12 + (P(),) * 3,
        out_specs=(by_rows,) * 3 + (weight,) * 12 + (P(),) * 3,
        check_vma=False,
    )
```

```python
import functools

import jax
import jax.numpy as jnp
from jax import lax
from jax.experimental import pallas as pl
from jax.experimental.pallas import tpu as pltpu
from jax.sharding import PartitionSpec as P

HEADS = 12
STEP = 10
LANES = 128
CHUNK = 128
ROW_PARTS = (1, 2, 5)
NEG = -1000000000.0
LOW = jnp.bfloat16
FULL = jnp.float32


def flip(value, axis, mask):
    count = lax.axis_size(axis)
    return lax.ppermute(value, axis, [(i, i ^ mask) for i in range(count)])


def flipped(codes, axis, mask):
    d_mask = mask if axis == "docs" else 0
    w_mask = mask if axis == "wide" else 0
    return [(d ^ d_mask, w ^ w_mask) for d, w in codes]


def after(value, *others):
    return lax.optimization_barrier((value, *others))[0]


class Doubling:
    def __init__(self, unit, slot, order, last):
        self.slot, self.last = slot, last
        self.arrays, self.codes = [unit[None]], [[(0, 0)]]
        for axis, mask in order:
            held, known = self.held()
            self.arrays.append(flip(held, axis, mask))
            self.codes.append(flipped(known, axis, mask))

    def held(self):
        held = self.arrays[0] if len(self.arrays) == 1 else jnp.concatenate(self.arrays, axis=0)
        return held, [code for group in self.codes for code in group]

    def finish(self, *others):
        newest, newest_known = self.arrays.pop(), self.codes.pop()
        held, known = self.held()
        axis, mask = self.last
        crossed = flip(after(newest, *others) if others else newest, axis, mask)
        arrays = self.arrays + [newest, flip(held, axis, mask), crossed]
        codes = self.codes + [newest_known, flipped(known, axis, mask), flipped(newest_known, axis, mask)]
        return arrays, [(self.slot, group) for group in codes]


def finish_both(pair, *others):
    arrays, codes = [], []
    for one in pair:
        some, known = one.finish(*others)
        arrays += some
        codes += known
    return arrays, codes


def sum_codes(order):
    codes = [(0, 0)]
    for axis, mask in reversed(order):
        codes = codes + flipped(codes, axis, mask)
    return codes


class Halving:
    def __init__(self, kept, sent, first, orders, after_both):
        self.parts, self.outgoing = [kept], sent
        self.first, self.orders, self.joint = first, orders, after_both
        self.step, self.last = 0, ()
        self.count = 1 + len(orders[0]) + len(after_both)

    def left(self):
        return self.step < self.count

    def hold(self, *others):
        self.outgoing = jax.tree.map(lambda value: after(value, *others), self.outgoing)

    def send(self):
        own = len(self.orders[0])
        if self.step == 0:
            arrived = flip(self.outgoing, *self.first)
            parts = self.parts + [arrived]
            middle = arrived.shape[0] // 2
            self.slots = [[part[:middle] for part in parts], [part[middle:] for part in parts]]
            self.last = (arrived,)
            self.outgoing = [None, None]
            for slot in (0, 1):
                self.outgoing[slot], self.slots[slot] = split_sums(self.slots[slot])
        elif self.step < own:
            arrived = [flip(self.outgoing[slot], *self.orders[slot][self.step - 1]) for slot in (0, 1)]
            self.last = tuple(arrived)
            for slot in (0, 1):
                self.outgoing[slot], self.slots[slot] = split_sums(self.slots[slot] + [arrived[slot]])
        elif self.step == own:
            arrived = [flip(self.outgoing[slot], *self.orders[slot][self.step - 1]) for slot in (0, 1)]
            self.last = tuple(arrived)
            self.slots = [self.slots[slot] + [arrived[slot]] for slot in (0, 1)]
            pairs = [split_sums(parts) if self.joint else (None, parts) for parts in self.slots]
            if self.joint:
                self.outgoing = jnp.concatenate([pair[0] for pair in pairs], axis=0)
            self.slots = [pair[1] for pair in pairs]
        else:
            arrived = flip(self.outgoing, *self.joint[self.step - 1 - own])
            middle = arrived.shape[0] // 2
            self.last = (arrived,)
            self.slots = [self.slots[0] + [arrived[:middle]], self.slots[1] + [arrived[middle:]]]
            if self.step + 1 < self.count:
                pairs = [split_sums(parts) for parts in self.slots]
                self.outgoing = jnp.concatenate([pair[0] for pair in pairs], axis=0)
                self.slots = [pair[1] for pair in pairs]
        self.step += 1

    def total(self):
        while self.left():
            self.send()
        return tuple(sum(part[0].astype(FULL) for part in parts) for parts in self.slots)


def split_sums(parts):
    half = parts[0].shape[0] // 2
    outgoing = sum(part[half:].astype(FULL) for part in parts).astype(LOW)
    return outgoing, [part[:half] for part in parts]


class Blocks:
    def __init__(self, count, size):
        self.count, self.size = count, size
        shifts = [(i * size) % LANES for i in range(count)]
        self.shifts = sorted(set(shifts))
        self.wide = -(-(size + max(shifts)) // LANES) * LANES
        self.aligned = max(shifts) == 0 and size % LANES == 0
        self.total = count * size
        self.room = max(self.start(i) + self.wide for i in range(count))

    def start(self, index):
        return index * self.size // LANES * LANES

    def start_dynamic(self, index):
        return pl.multiple_of(index * self.size // LANES * LANES, LANES)

    def pad(self, value, index):
        result = None
        for shift in self.shifts:
            low = [(0, 0)] * (value.ndim - 1) + [(shift, self.wide - self.size - shift)]
            placed = jnp.pad(value, low)
            here = (index * self.size) % LANES == shift
            result = placed if result is None else jnp.where(here, placed, result)
        return result

    def cut(self, value, index):
        result = None
        for shift in self.shifts:
            piece = value[..., shift : shift + self.size]
            here = (index * self.size) % LANES == shift
            result = piece if result is None else jnp.where(here, piece, result)
        return result

    def tile_owners(self, tile):
        low, high = tile * LANES, (tile + 1) * LANES
        return [
            (i, low - self.start(i))
            for i in range(self.count)
            if i * self.size < high and (i + 1) * self.size > low
        ]


def matmul(left, right):
    return lax.dot_general(left, right, (((1,), (0,)), ((), ())), preferred_element_type=FULL)


def matmul_nt(left, right):
    return lax.dot_general(left, right, (((1,), (1,)), ((), ())), preferred_element_type=FULL)


def matmul_tn(left, right):
    return lax.dot_general(left, right, (((0,), (0,)), ((), ())), preferred_element_type=FULL)


def normed(values):
    centred = values - jnp.mean(values, axis=-1, keepdims=True)
    spread = jnp.mean(centred * centred, axis=-1, keepdims=True)
    scale = lax.rsqrt(spread + 1e-05)
    return centred * scale, scale


def norm_back(grad, unit, scale, gain):
    inner = grad * gain
    mean_inner = jnp.mean(inner, axis=-1, keepdims=True)
    mean_both = jnp.mean(inner * unit, axis=-1, keepdims=True)
    return scale * (inner - mean_inner - unit * mean_both)


def rows_at(index, size=CHUNK):
    return pl.ds(pl.multiple_of(index * size, size), size)


def places(pos, slot, codes, half):
    owner = pos[2] if slot == 0 else 1 - pos[2]
    for index, (d_mask, w_mask) in enumerate(codes):
        yield index, pos[0] ^ d_mask, owner * half + (pos[1] ^ w_mask)


def load_pieces(pos, refs, codes, half, lanes, target, sem):
    for ref, (slot, group) in zip(refs, codes):
        for index, doc, inner in places(pos, slot, group, half):
            pltpu.make_async_copy(
                ref.at[index, :, pl.ds(lanes[0], lanes[1])], target(doc, inner), sem
            ).start()


def store_pieces(pos, source, sums, half, targets, lanes, sem):
    for slot, codes in enumerate(sums):
        count = len(codes) // 2
        for index, doc, inner in places(pos, slot, codes, half):
            pltpu.make_async_copy(
                source(doc, inner),
                targets[index // count].at[slot * count + index % count, :, pl.ds(lanes[0], lanes[1])],
                sem,
            ).start()


def wait_whole(ref, sem):
    pltpu.make_async_copy(ref, ref, sem).wait()


def row_target(ref, blocks, rows):
    if blocks.aligned:
        return lambda doc, inner: ref.at[
            pl.ds(pl.multiple_of(inner * rows, rows), rows),
            pl.ds(blocks.start_dynamic(doc), blocks.wide),
        ]
    return lambda doc, inner: ref.at[doc, pl.ds(pl.multiple_of(inner * rows, rows), rows), :]


def column_target(ref, blocks, rows):
    if blocks.aligned:
        return lambda doc, inner: ref.at[
            pl.ds(pl.multiple_of(doc * rows, rows), rows),
            pl.ds(blocks.start_dynamic(inner), blocks.wide),
        ]
    return lambda doc, inner: ref.at[inner, pl.ds(pl.multiple_of(doc * rows, rows), rows), :]


def held_shape(blocks, height):
    return (height, blocks.total) if blocks.aligned else (blocks.count, height, blocks.wide)


def merge_tiles(held, whole, blocks):
    for tile in range(blocks.total // LANES):
        value = None
        for index, offset in blocks.tile_owners(tile):
            piece = held[index, :, offset : offset + LANES]
            value = piece if value is None else value + piece
        whole[:, tile * LANES : (tile + 1) * LANES] = value


def project_kernel(
    shape, pos, own, other, gains, page_col, page_row, mask_row, *refs
):
    codes, half, rows, blocks, length, width, factor = shape
    pieces = refs[: len(codes)]
    (q_out, k_out, v_out, att_out, lse_out, weight) = refs[len(codes) : len(codes) + 6]
    (held, h_own, h_oth, allowed, sem) = refs[len(codes) + 6 :]
    load_pieces(pos, pieces, codes, half, (0, blocks.wide), row_target(held, blocks, rows), sem)
    for i in range(length // CHUNK):
        part = pl.ds(i * CHUNK, CHUNK)
        unit, _ = normed(own[part, :].astype(FULL))
        h_own[part, :] = (unit * gains[0:1, :]).astype(LOW)
        unit, _ = normed(other[part, :].astype(FULL))
        h_oth[part, :] = (unit * gains[1:2, :]).astype(LOW)
        row = lax.broadcasted_iota(jnp.int32, (CHUNK, length), 0) + i * CHUNK
        col = lax.broadcasted_iota(jnp.int32, (CHUNK, length), 1)
        ok = (page_col[part, :] == page_row[...]) & ((mask_row[...] == 1) | (row == col))
        allowed[part, :] = jnp.where(ok, 1.0, 0.0)
    wait_whole(held, sem)
    merge_tiles(held, weight, blocks)
    lse_out[...] = jnp.zeros_like(lse_out)

    q_out[...] = (matmul(h_own[...], weight[:, :width]).astype(LOW) * factor).astype(LOW)
    k_out[...] = matmul(h_oth[...], weight[:, width : 2 * width]).astype(LOW)
    v_out[...] = matmul(h_oth[...], weight[:, 2 * width :]).astype(LOW)
    size = width // HEADS
    per = LANES // size

    @pl.loop(0, width // LANES)
    def _(pair):
        cols = pl.ds(pl.multiple_of(pair * LANES, LANES), LANES)
        keys = k_out[:, cols]
        values = v_out[:, cols]
        for i in range(length // CHUNK):
            part = pl.ds(i * CHUNK, CHUNK)
            queries = q_out[part, cols]
            lane = lax.broadcasted_iota(jnp.int32, queries.shape, 1)
            result = None
            sums = lse_out[part, :]
            for sub in range(per):
                inside = lane // size == sub
                scores = matmul_nt(jnp.where(inside, queries, jnp.zeros_like(queries)), keys)
                scores = jnp.where(allowed[part, :] > 0.5, scores, NEG)
                top = jnp.max(scores, axis=-1, keepdims=True)
                exps = jnp.exp(scores - top)
                total = jnp.sum(exps, axis=-1, keepdims=True)
                probs = (exps * (1.0 / total)).astype(LOW)
                out = matmul(probs, values)
                result = out if result is None else jnp.where(inside, out, result)
                sums = jnp.where(lane == pair * per + sub, top + jnp.log(total), sums)
            lse_out[part, :] = sums
            att_out[part, cols] = result.astype(LOW)


def feed_kernel(
    shape, pos, att, own, cot, cotj_own, cotj_oth, coef, gain, page_col, *refs
):
    (up_codes, down_codes, sums, half, rows, down_rows, ups, outs, downs, length, width, hidden, block) = shape
    n_up, n_down = len(up_codes), len(down_codes)
    up_pieces, down_pieces = refs[:n_up], refs[n_up : n_up + n_down]
    refs = refs[n_up + n_down :]
    mid, unit_ref, scale_ref, dz, acc, dacc, w_out, g_up = refs[:8]
    down_targets = refs[8:10]
    (w_up, o_held, d_held, w_down, g_down, h2, h2_t, dffn, dffn_t, acts, dpre, sem_up, sem_out, sem_down, sem_gdown) = refs[10:]
    load_pieces(pos, up_pieces, up_codes, half, (ups.wide, outs.wide), row_target(o_held, outs, rows), sem_out)
    load_pieces(pos, up_pieces, up_codes, half, (0, ups.wide), row_target(w_up, ups, rows), sem_up)
    load_pieces(pos, down_pieces, down_codes, half, (0, downs.wide), column_target(d_held, downs, down_rows), sem_down)
    half_rows = length // 2
    parts = length // CHUNK
    for which, ref in ((pos[2], cotj_own), (1 - pos[2], cotj_oth)):
        for i in range(half_rows // CHUNK):
            part = pl.ds(pl.multiple_of(which * half_rows + i * CHUNK, CHUNK), CHUNK)
            grad = cot[part, :] + coef[...] * ref[pl.ds(i * CHUNK, CHUNK), :].astype(FULL)
            valid = jnp.where(page_col[part, :] >= 0, 1.0, 0.0)
            dz[part, :] = grad
            dffn[part, :] = (grad * valid).astype(LOW)
    dffn_t[...] = dffn[...].T
    wait_whole(o_held, sem_out)
    merge_tiles(o_held, w_out, outs)

    @pl.loop(0, parts)
    def _(i):
        part = rows_at(i)
        valid = jnp.where(page_col[part, :] >= 0, 1.0, 0.0)
        middle = own[part, :].astype(FULL) + valid * matmul(att[part, :], w_out[...])
        unit, scale = normed(middle)
        mid[part, :] = middle
        unit_ref[part, :] = unit
        scale_ref[part, :] = jnp.broadcast_to(scale, (CHUNK, LANES))
        h2[part, :] = (unit * gain[...]).astype(LOW)

    h2_t[...] = h2[...].T
    acc[...] = jnp.zeros_like(acc)
    dacc[...] = jnp.zeros_like(dacc)
    wait_whole(w_up, sem_up)
    wait_whole(d_held, sem_down)
    if not downs.aligned:
        merge_tiles(d_held, w_down, downs)
    down = d_held if downs.aligned else w_down
    c0, c1 = 0.7978845608028654, 0.044715

    @pl.loop(0, hidden // block)
    def _(f):
        cols = pl.ds(pl.multiple_of(f * block, LANES), block)

        @pl.loop(0, parts)
        def _(i):
            part = rows_at(i)
            pre = matmul(h2[part, :], w_up[:, cols])
            dact = matmul(dffn[part, :], down[:, cols])
            square = pre * pre
            flat = jnp.tanh(c0 * (pre + c1 * square * pre))
            cdf = 0.5 * (1.0 + flat)
            slope = cdf + pre * (0.5 * (1.0 - flat * flat)) * (c0 * (1.0 + 3.0 * c1 * square))
            act = (pre * cdf).astype(LOW)
            dp = (slope * dact).astype(LOW)
            acts[part, :] = act
            dpre[part, :] = dp
            acc[part, :] += matmul_nt(act, down[:, cols])
            dacc[part, :] += matmul_nt(dp, w_up[:, cols])

        g_down[:, cols] = matmul(dffn_t[...], acts[...]).astype(LOW)
        g_up[:, cols] = matmul(h2_t[...], dpre[...]).astype(LOW)

    if downs.room > downs.total:
        g_down[:, downs.total :] = jnp.zeros((width, downs.room - downs.total), LOW)
    store_pieces(
        pos,
        lambda doc, inner: g_down.at[
            pl.ds(pl.multiple_of(doc * down_rows, down_rows), down_rows),
            pl.ds(downs.start_dynamic(inner), downs.wide),
        ],
        sums, half, down_targets, (0, downs.wide), sem_gdown,
    )
    for target in down_targets:
        wait_whole(target, sem_gdown)


def branch_kernel(shape, pos, att, gain, page_col, mid, unit_ref, scale_ref, dz, acc, dacc, w_out, g_up, *refs):
    sums, half, rows, ups, outs, length, width = shape
    out_ref, away_ref, dmid_ref, datt_ref, dgain_ref = refs[:5]
    up_targets = refs[5:7]
    g_out, att_t, dbranch, sem_gup = refs[7:]
    half_rows = length // 2
    parts = length // CHUNK
    store_pieces(
        pos,
        lambda doc, inner: g_up.at[
            pl.ds(pl.multiple_of(inner * rows, rows), rows),
            pl.ds(ups.start_dynamic(doc), ups.wide),
        ],
        sums, half, up_targets, (0, ups.wide), sem_gup,
    )
    att_t[...] = att[...].T
    dgain_ref[...] = jnp.zeros_like(dgain_ref)

    @pl.loop(0, parts)
    def _(i):
        part = rows_at(i)
        valid = jnp.where(page_col[part, :] >= 0, 1.0, 0.0)
        out_ref[part, :] = mid[part, :] + valid * acc[part, :]
        grad, unit = dacc[part, :], unit_ref[part, :]
        dgain_ref[0:1, :] += jnp.sum(grad * unit, axis=0, keepdims=True)
        dmid = dz[part, :] + norm_back(grad, unit, scale_ref[part, 0:1], gain[...])
        dmid_ref[part, :] = dmid
        low = (dmid * valid).astype(LOW)
        dbranch[part, :] = low
        datt_ref[part, :] = matmul_nt(low, w_out[...]).astype(LOW)

    for i in range(half_rows // CHUNK):
        part = pl.ds(pl.multiple_of((1 - pos[2]) * half_rows + i * CHUNK, CHUNK), CHUNK)
        away_ref[pl.ds(i * CHUNK, CHUNK), :] = out_ref[part, :].astype(LOW)
    g_out[:, : outs.total] = matmul(att_t[...], dbranch[...]).astype(LOW)
    if outs.room > outs.total:
        g_out[:, outs.total :] = jnp.zeros((width, outs.room - outs.total), LOW)
    store_pieces(
        pos,
        lambda doc, inner: g_out.at[
            pl.ds(pl.multiple_of(inner * rows, rows), rows),
            pl.ds(outs.start_dynamic(doc), outs.wide),
        ],
        sums, half, up_targets, (ups.wide, outs.wide), sem_gup,
    )
    for target in up_targets:
        wait_whole(target, sem_gup)


def scores_back_kernel(
    shape, pairs, page_col, page_row, mask_col, q_ref, k_ref, v_ref, att, datt, lse, dq, dk, dv,
    allowed, flat, lse_t, dots_t, dscore,
):
    length, width, factor = shape
    size = width // HEADS
    per = LANES // size
    parts = length // CHUNK
    for i in range(parts):
        part = pl.ds(i * CHUNK, CHUNK)
        row = lax.broadcasted_iota(jnp.int32, (CHUNK, length), 0) + i * CHUNK
        col = lax.broadcasted_iota(jnp.int32, (CHUNK, length), 1)
        ok = (page_col[part, :] == page_row[...]) & ((mask_col[part, :] == 1) | (row == col))
        allowed[part, :] = jnp.where(ok, 1.0, 0.0)
    head = lax.broadcasted_iota(jnp.int32, (LANES, width), 0)
    lane = lax.broadcasted_iota(jnp.int32, (LANES, width), 1)
    chosen = jnp.where(lane // size == head, 1.0, 0.0)
    flat[...] = att[...].astype(FULL) * datt[...].astype(FULL)
    dots_t[...] = lax.dot_general(
        chosen, flat[...], (((1,), (1,)), ((), ())), preferred_element_type=FULL,
        precision=lax.Precision.HIGHEST,
    )
    lse_t[...] = lse[...].T

    @pl.loop(pairs[0], pairs[1])
    def _(pair):
        cols = pl.ds(pl.multiple_of(pair * LANES, LANES), LANES)
        here = pl.ds(pl.multiple_of((pair - pairs[0]) * LANES, LANES), LANES)
        queries, grads, keys_all = q_ref[:, cols], datt[:, cols], k_ref[:, cols]
        lane = lax.broadcasted_iota(jnp.int32, (length, LANES), 1)
        lane_part = lax.broadcasted_iota(jnp.int32, (CHUNK, LANES), 1)
        zero = jnp.zeros_like(queries)
        dq_pair = None
        for sub in range(per):
            inside = lane // size == sub
            inside_part = lane_part // size == sub
            q_head = jnp.where(inside, queries, zero)
            g_head = jnp.where(inside, grads, zero)
            lse_row = lse_t[pl.ds(pair * per + sub, 1), :]
            dot_row = dots_t[pl.ds(pair * per + sub, 1), :]
            for i in range(parts):
                part = pl.ds(i * CHUNK, CHUNK)
                scores = matmul_nt(k_ref[part, cols], q_head)
                scores = jnp.where(allowed[part, :] > 0.5, scores, NEG)
                probs = jnp.exp(scores - lse_row)
                dprob = matmul_nt(v_ref[part, cols], g_head)
                low = (probs * (dprob - dot_row)).astype(LOW)
                dscore[part, :] = low
                dv_part = matmul(probs.astype(LOW), grads).astype(LOW)
                dk_part = matmul(low, queries).astype(LOW)
                if sub > 0:
                    dv_part = jnp.where(inside_part, dv_part, dv[part, here])
                    dk_part = jnp.where(inside_part, dk_part, dk[part, here])
                dv[part, here] = dv_part
                dk[part, here] = dk_part
            dq_head = matmul_tn(dscore[...], keys_all)
            dq_pair = dq_head if dq_pair is None else jnp.where(inside, dq_head, dq_pair)
        dq[:, here] = (dq_pair * factor).astype(LOW)


def project_back_kernel(shape, pos, own, other, gains, weight, *refs):
    (sums, half, rows, blocks, length, width, runs) = shape
    grads = [refs[3 * i : 3 * i + 3] for i in range(len(runs))]
    refs = refs[3 * len(runs) :]
    own_ref, oth_ref, dgain_ref = refs[:3]
    targets = refs[3:5]
    h_t, flat, grad, sem = refs[5:]
    parts = length // CHUNK
    for which, source in ((0, own), (1, other)):
        for i in range(parts):
            part = pl.ds(i * CHUNK, CHUNK)
            unit, _ = normed(source[part, :].astype(FULL))
            flat[part, :] = unit * gains[which : which + 1, :]
        h_t[which] = flat[...].astype(LOW).T
    for (low, high), trio in zip(runs, grads):
        for block, (which, ref) in enumerate(zip((0, 1, 1), trio)):
            grad[:, block * width + low : block * width + high] = matmul(h_t[which], ref[...]).astype(LOW)
    if blocks.room > blocks.total:
        grad[:, blocks.total :] = jnp.zeros((width, blocks.room - blocks.total), LOW)
    store_pieces(
        pos,
        lambda doc, inner: grad.at[
            pl.ds(pl.multiple_of(inner * rows, rows), rows),
            pl.ds(blocks.start_dynamic(doc), blocks.wide),
        ],
        sums, half, targets, (0, blocks.wide), sem,
    )
    dgain_ref[...] = jnp.zeros_like(dgain_ref)
    for i in range(parts):
        part = pl.ds(i * CHUNK, CHUNK)
        unit, _ = normed(own[part, :].astype(FULL))
        value = sum(
            matmul_nt(trio[0][part, :], weight[:, low:high]) for (low, high), trio in zip(runs, grads)
        )
        own_ref[part, :] = value
        dgain_ref[0:1, :] += jnp.sum(value * unit, axis=0, keepdims=True)
        unit, _ = normed(other[part, :].astype(FULL))
        value = sum(
            matmul_nt(trio[block][part, :], weight[:, block * width + low : block * width + high])
            for (low, high), trio in zip(runs, grads)
            for block in (1, 2)
        )
        oth_ref[part, :] = value.astype(LOW)
        dgain_ref[1:2, :] += jnp.sum(value * unit, axis=0, keepdims=True)
    for target in targets:
        wait_whole(target, sem)


def tail_kernel(length, own, gain, mine, theirs, dmid, out_ref):
    for i in range(length // CHUNK):
        part = pl.ds(i * CHUNK, CHUNK)
        unit, scale = normed(own[part, :].astype(FULL))
        grad = mine[part, :] + theirs[part, :].astype(FULL)
        out_ref[part, :] = dmid[part, :] + norm_back(grad, unit, scale, gain[...])


VMEM = pl.BlockSpec(memory_space=pltpu.VMEM)
ANY = pl.BlockSpec(memory_space=pl.ANY)
SMEM = pl.BlockSpec(memory_space=pltpu.SMEM)


LITTLE = pl.CostEstimate(flops=1_000, bytes_accessed=1_000, transcendentals=0)


def params(mebibytes):
    return pltpu.CompilerParams(vmem_limit_bytes=mebibytes * 1024 * 1024)


def adam_update(weight, first, second, grad, rate, decay):
    first_new = 0.9 * first + 0.1 * grad
    second_new = 0.999 * second + 0.001 * grad * grad
    first_hat = first_new / (1.0 - 0.9**STEP)
    second_hat = second_new / (1.0 - 0.999**STEP)
    weight_new = weight - rate * (first_hat / (jnp.sqrt(second_hat) + 1e-08) + decay * weight)
    return (weight_new, first_new, second_new)


def shards(
    rows, cot_stream, cot_joined, page, key_mask,
    w_qkv, m_qkv, v_qkv, w_out, m_out, v_out, w_up, m_up, v_up, w_down, m_down, v_down,
    gains, m_gains, v_gains,
):
    docs, wide = lax.axis_size("docs"), lax.axis_size("wide")
    half = wide // 2
    doc, place = lax.axis_index("docs"), lax.axis_index("wide")
    stream = place // half
    is_text = stream == 0
    pos = jnp.stack((doc, place % half, stream)).astype(jnp.int32)
    length, width = rows.shape
    half_rows = length // 2
    factor = float(width // HEADS) ** (-0.5)
    piece_rows = w_qkv.shape[1]
    hidden = w_up.shape[2] * docs
    qkvs, outs, ups = Blocks(docs, w_qkv.shape[2]), Blocks(docs, w_out.shape[2]), Blocks(docs, w_up.shape[2])
    downs = Blocks(wide, w_down.shape[1])
    down_rows = w_down.shape[2]

    core = [("wide", 1)]
    along_x = [("docs", 1)]
    along_y = [("docs", 1 << b) for b in range(1, docs.bit_length() - 1)]
    along_z = [("wide", 1 << b) for b in range(1, half.bit_length() - 1)]
    across = ("wide", half)

    def swap(value):
        return flip(value, *across)

    column = doc * w_qkv.shape[2] + lax.iota(jnp.int32, w_qkv.shape[2])
    is_query = (column < width)[None, None, :]
    pair_qkv = jnp.where(is_query, w_qkv, w_qkv[::-1]).astype(LOW)

    def own_first(pair):
        return jnp.where(is_text, pair, pair[::-1])

    unit_a = qkvs.pad(own_first(pair_qkv), doc)
    unit_b = jnp.concatenate(
        (ups.pad(own_first(w_up.astype(LOW)), doc), outs.pad(own_first(w_out.astype(LOW)), doc)), axis=-1
    )
    unit_c = downs.pad(jnp.swapaxes(own_first(w_down.astype(LOW)), 1, 2), place)
    unit_a = (unit_a[0], swap(unit_a[1]))
    unit_b = (unit_b[0], swap(unit_b[1]))
    if downs.aligned:
        unit_c = (unit_c[0], swap(unit_c[1]))
    else:
        raw = jnp.swapaxes(own_first(w_down.astype(LOW)), 1, 2)
        unit_c = (unit_c[0], downs.pad(swap(raw[1]), (place + half) % wide))
    chunks, begin = [], 0
    for size in [length * part // 8 for part in ROW_PARTS]:
        some = rows[begin : begin + size]
        chunks.append(swap(after(some, chunks[-1]) if chunks else some))
        begin += size
    other_rows = jnp.concatenate(chunks, axis=0)
    zxy, zyx = along_z + along_x + along_y, along_z + along_y + along_x
    both_a = [Doubling(unit_a[i], i, order, core[0]) for i, order in enumerate((zxy, zyx))]
    both_b = [Doubling(unit_b[i], i, order, core[0]) for i, order in enumerate((zxy, zyx))]
    both_c = [Doubling(unit_c[i], i, order, core[0]) for i, order in enumerate((zyx, zxy))]
    pieces_a, codes_a = finish_both(both_a)
    other_joined = swap(after(cot_joined.astype(LOW), chunks[-1]))

    page_col, page_row = page[:, None], page[None, :]
    mask_col, mask_row = key_mask[:, None], key_mask[None, :]
    gain_own = lax.dynamic_index_in_dim(gains, stream, 0, keepdims=True)
    gain_oth = lax.dynamic_index_in_dim(gains, 1 - stream, 0, keepdims=True)
    gain_one = jnp.concatenate((gain_own, gain_oth), axis=0)
    gain_two = lax.dynamic_index_in_dim(gains, 2 + stream, 0, keepdims=True)
    mix = jax.nn.sigmoid(gains[4])[None, :]
    coef = jnp.where(is_text, mix, 1.0 - mix)

    low_rows = jax.ShapeDtypeStruct((length, width), LOW)
    full_rows = jax.ShapeDtypeStruct((length, width), FULL)

    shape = (codes_a, half, piece_rows, qkvs, length, width, factor)
    queries, keys, values, attended, lse, weight_qkv = pl.pallas_call(
        functools.partial(project_kernel, shape),
        out_shape=(low_rows, low_rows, low_rows, low_rows,
                   jax.ShapeDtypeStruct((length, LANES), FULL),
                   jax.ShapeDtypeStruct((width, 3 * width), LOW)),
        in_specs=[SMEM] + [VMEM] * 6 + [ANY] * len(pieces_a),
        out_specs=(VMEM,) * 6,
        scratch_shapes=[
            pltpu.VMEM((docs, width, qkvs.wide), LOW),
            pltpu.VMEM((length, width), LOW),
            pltpu.VMEM((length, width), LOW),
            pltpu.VMEM((length, length), FULL),
            pltpu.SemaphoreType.DMA,
        ],
        compiler_params=params(48),
        cost_estimate=LITTLE,
        name="project_attend",
    )(pos, rows, other_rows, gain_one, page_col, page_row, mask_row, *pieces_a)

    pieces_b, codes_b = finish_both(both_b, lse)
    pieces_c, codes_c = finish_both(both_c, lse)
    orders = (core + along_x + along_y + along_z, core + along_y + along_x + along_z)
    own_orders = tuple(order[1 : 1 + len(along_x + along_y)] for order in orders)
    sums = tuple(sum_codes(order) for order in orders)
    sent_count = len(sums[0])
    block = 3 * LANES
    shape = (codes_b, codes_c, sums, half, piece_rows, down_rows, ups, outs, downs, length, width, hidden, block)
    shape_b = jax.ShapeDtypeStruct((sent_count, piece_rows, ups.wide + outs.wide), LOW)
    shape_c = jax.ShapeDtypeStruct((sent_count, down_rows, downs.wide), LOW)
    *carried, kept_c, sent_c = pl.pallas_call(
        functools.partial(feed_kernel, shape),
        out_shape=(full_rows, full_rows, jax.ShapeDtypeStruct((length, LANES), FULL), full_rows, full_rows, full_rows,
                   jax.ShapeDtypeStruct((width, width), LOW), jax.ShapeDtypeStruct((width, hidden), LOW)) + (shape_c,) * 2,
        in_specs=[SMEM] + [VMEM] * 8 + [ANY] * (len(pieces_b) + len(pieces_c)),
        out_specs=(VMEM,) * 8 + (ANY,) * 2,
        scratch_shapes=[
            pltpu.VMEM((width, hidden), LOW),
            pltpu.VMEM(held_shape(outs, width), LOW),
            pltpu.VMEM(held_shape(downs, width), LOW),
            pltpu.VMEM((8, LANES) if downs.aligned else (width, hidden), LOW),
            pltpu.VMEM((width, downs.room), LOW),
            pltpu.VMEM((length, width), LOW),
            pltpu.VMEM((width, length), LOW),
            pltpu.VMEM((length, width), LOW),
            pltpu.VMEM((width, length), LOW),
            pltpu.VMEM((length, block), LOW),
            pltpu.VMEM((length, block), LOW),
        ] + [pltpu.SemaphoreType.DMA] * 4,
        compiler_params=params(60),
        cost_estimate=LITTLE,
        name="feed_forward_back",
    )(pos, attended, rows, cot_stream, cot_joined, other_joined, coef, gain_two, page_col, *pieces_b, *pieces_c)

    shape = (sums, half, piece_rows, ups, outs, length, width)
    (stream_out, away, middle_grad, attended_grad, dgain_two, kept_b, sent_b) = pl.pallas_call(
        functools.partial(branch_kernel, shape),
        out_shape=(full_rows, jax.ShapeDtypeStruct((half_rows, width), LOW), full_rows, low_rows,
                   jax.ShapeDtypeStruct((8, width), FULL)) + (shape_b,) * 2,
        in_specs=[SMEM] + [VMEM] * 11,
        out_specs=(VMEM,) * 5 + (ANY,) * 2,
        scratch_shapes=[
            pltpu.VMEM((width, outs.room), LOW),
            pltpu.VMEM((width, length), LOW),
            pltpu.VMEM((length, width), LOW),
            pltpu.SemaphoreType.DMA,
        ],
        compiler_params=params(48),
        cost_estimate=LITTLE,
        name="branch_back",
    )(pos, attended, gain_two, page_col, *carried)

    def attend_back(pairs, *operands):
        low_cols = jax.ShapeDtypeStruct((length, (pairs[1] - pairs[0]) * LANES), LOW)
        return pl.pallas_call(
            functools.partial(scores_back_kernel, (length, width, factor), pairs),
            out_shape=(low_cols,) * 3,
            in_specs=[VMEM] * 9,
            out_specs=(VMEM,) * 3,
            scratch_shapes=[
                pltpu.VMEM((length, length), FULL),
                pltpu.VMEM((length, width), FULL),
                pltpu.VMEM((LANES, length), FULL),
                pltpu.VMEM((LANES, length), FULL),
                pltpu.VMEM((length, length), LOW),
            ],
            compiler_params=params(40),
            cost_estimate=LITTLE,
            name="attend_back",
        )(page_col, page_row, mask_col, *operands)

    def halving(kept, sent):
        return Halving(kept, sent, core[0], own_orders, along_z)

    sums_c, sums_b = halving(kept_c, sent_c), halving(kept_b, sent_b)
    sums_c.send()
    first = after(queries, *sums_c.last)
    sums_c.send()
    sums_b.send()
    partner_rows = swap(after(away, first))
    pair_count = width // LANES
    cuts = (0, pair_count // 2, pair_count)
    grads_one = attend_back(cuts[:2], first, keys, values, attended, attended_grad, lse)
    second = after(queries, *grads_one, *sums_c.last, *sums_b.last)
    sums_b.hold(grads_one[0], *sums_c.last)
    sums_c.hold(grads_one[0], *sums_b.last)
    sums_b.send()
    sums_c.send()
    grads_two = attend_back(cuts[1:], second, keys, values, attended, attended_grad, lse)

    runs = tuple((low * LANES, high * LANES) for low, high in zip(cuts[:-1], cuts[1:]))
    shape = (sums, half, piece_rows, qkvs, length, width, runs)
    shape_a = jax.ShapeDtypeStruct((sent_count, piece_rows, qkvs.wide), LOW)
    own_part, away_part, dgain_one, kept_a, sent_a = pl.pallas_call(
        functools.partial(project_back_kernel, shape),
        out_shape=(full_rows, low_rows, jax.ShapeDtypeStruct((8, width), FULL)) + (shape_a,) * 2,
        in_specs=[SMEM] + [VMEM] * (4 + 3 * len(runs)),
        out_specs=(VMEM,) * 3 + (ANY,) * 2,
        scratch_shapes=[
            pltpu.VMEM((2, width, length), LOW),
            pltpu.VMEM((length, width), FULL),
            pltpu.VMEM((width, qkvs.room), LOW),
            pltpu.SemaphoreType.DMA,
        ],
        compiler_params=params(40),
        cost_estimate=LITTLE,
        name="project_back",
    )(pos, rows, other_rows, gain_one, weight_qkv, *grads_one, *grads_two)

    back_part = swap(away_part)
    sums_a = halving(kept_a, sent_a)
    sums_a.hold(*sums_c.last, *sums_b.last)
    sums_b.hold(*sums_c.last)
    sums_c.hold(*sums_b.last)
    sums_a.send()
    sums_b.send()
    sums_c.send()
    own_rows = lax.dynamic_slice_in_dim(stream_out, stream * half_rows, half_rows, 0)
    partner_rows = partner_rows.astype(FULL)
    text_rows = jnp.where(is_text, own_rows, partner_rows)
    image_rows = jnp.where(is_text, partner_rows, own_rows)
    joined_rows = mix * text_rows + (1.0 - mix) * image_rows
    gate_grad = jnp.sum(cot_joined * (text_rows - image_rows), axis=0, keepdims=True) * mix * (1.0 - mix)

    slot_index = lax.iota(jnp.int32, 5)[:, None]
    small = (
        jnp.where(slot_index == stream, dgain_one[0:1], 0.0)
        + jnp.where(slot_index == 1 - stream, dgain_one[1:2], 0.0)
        + jnp.where(slot_index == 2 + stream, dgain_two[0:1], 0.0)
        + jnp.where(slot_index == 4, gate_grad, 0.0)
    )
    for step in core + along_x + along_y + along_z + [across]:
        small = after(small, *sums_a.last)
        small = small + flip(small, *step)
        for sums_of in (sums_a, sums_b, sums_c):
            if sums_of.left():
                sums_of.send()
    gains_grad = small
    grad_rows = pl.pallas_call(
        functools.partial(tail_kernel, length),
        out_shape=full_rows,
        in_specs=[VMEM] * 5,
        out_specs=VMEM,
        compiler_params=params(32),
        name="norm_tail",
    )(rows, gain_own, own_part, back_part, after(middle_grad, *sums_a.last))

    total_a, total_b, total_c = sums_a.total(), sums_b.total(), sums_c.total()

    def both(total):
        mine = total[0]
        theirs = swap(total[1].astype(LOW)).astype(FULL)
        return mine, theirs

    def placed(mine, theirs):
        return jnp.where(is_text, jnp.stack((mine, theirs)), jnp.stack((theirs, mine)))

    mine_b, theirs_b = both(total_b)
    grad_b = placed(mine_b, theirs_b)
    grad_up = ups.cut(grad_b[..., : ups.wide], doc)
    grad_out = outs.cut(grad_b[..., ups.wide :], doc)
    if downs.aligned:
        mine_c, theirs_c = both(total_c)
    else:
        mine_c = downs.cut(total_c[0], place)
        theirs_c = swap(downs.cut(total_c[1], (place + half) % wide).astype(LOW)).astype(FULL)
    grad_down = jnp.swapaxes(placed(mine_c, theirs_c), 1, 2)
    mine_a, theirs_a = both(total_a)
    mine_a, theirs_a = qkvs.cut(mine_a, doc), qkvs.cut(theirs_a, doc)
    query_here = is_query[0]
    grad_qkv = placed(
        jnp.where(query_here, mine_a, theirs_a), jnp.where(query_here, theirs_a, mine_a)
    )

    qkv_new = adam_update(w_qkv, m_qkv, v_qkv, grad_qkv, 0.12, 0.01)
    out_new = adam_update(w_out, m_out, v_out, grad_out, 0.5, 0.01)
    up_new = adam_update(w_up, m_up, v_up, grad_up, 0.12, 0.01)
    down_new = adam_update(w_down, m_down, v_down, grad_down, 0.06, 0.01)
    gains_new = adam_update(gains, m_gains, v_gains, gains_grad, 0.8, 0.0)
    return (stream_out, joined_rows, grad_rows, *qkv_new, *out_new, *up_new, *down_new, *gains_new)


def solution(mesh):
    by_rows = P(("docs", "wide"), None)
    by_row = P(("docs", "wide"))
    weight = P(None, "wide", "docs")
    return jax.shard_map(
        shards,
        mesh=mesh,
        in_specs=(by_rows,) * 3 + (by_row,) * 2 + (weight,) * 12 + (P(),) * 3,
        out_specs=(by_rows,) * 3 + (weight,) * 12 + (P(),) * 3,
        check_vma=False,
    )
```

```python
import functools

import jax
import jax.numpy as jnp
from jax import lax
from jax.experimental import pallas as pl
from jax.experimental.pallas import tpu as pltpu
from jax.sharding import PartitionSpec as P

HEADS = 12
STEP = 10
LANES = 128
CHUNK = 128
ROW_PARTS = (5, 6, 5)
BACK_PARTS = (4, 5, 4, 3)
FIRST_A = False
NEG = -1000000000.0
LOW = jnp.bfloat16
FULL = jnp.float32


def flip(value, axis, mask):
    count = lax.axis_size(axis)
    return lax.ppermute(value, axis, [(i, i ^ mask) for i in range(count)])


def flipped(codes, axis, mask):
    d_mask = mask if axis == "docs" else 0
    w_mask = mask if axis == "wide" else 0
    return [(d ^ d_mask, w ^ w_mask) for d, w in codes]


def after(value, *others):
    return lax.optimization_barrier((value, *others))[0]


class Doubling:
    def __init__(self, unit, slot, order):
        self.slot, self.order, self.step = slot, order, 0
        self.arrays, self.codes = [unit[None]], [[(0, 0)]]
        self.last = ()

    def held(self):
        held = self.arrays[0] if len(self.arrays) == 1 else jnp.concatenate(self.arrays, axis=0)
        return held, [code for group in self.codes for code in group]

    def send(self, *others):
        held, known = self.held()
        if others:
            held = after(held, *others)
        axis, mask = self.order[self.step]
        self.arrays.append(flip(held, axis, mask))
        self.codes.append(flipped(known, axis, mask))
        self.step, self.last = self.step + 1, (self.arrays[-1],)

    def send_all(self):
        while self.step < len(self.order):
            self.send()

    def split_newest(self):
        newest, newest_known = self.arrays.pop(), self.codes.pop()
        held, known = self.held()
        self.arrays.append(newest)
        self.codes.append(newest_known)
        return (held, known), (newest, newest_known)

    def add(self, value, known, axis, mask):
        self.arrays.append(flip(value, axis, mask))
        self.codes.append(flipped(known, axis, mask))
        return self.arrays[-1]

    def slotted(self):
        return [(self.slot, group) for group in self.codes]


def sum_codes(order):
    codes = [(0, 0)]
    for axis, mask in reversed(order):
        codes = codes + flipped(codes, axis, mask)
    return codes


class Halving:
    def __init__(self, kept, sent, steps):
        self.slots, self.sent, self.steps = split(kept), sent, steps
        self.step, self.last = 0, ()
        self.slots = [[half] for half in self.slots]
        self.outgoing = [None, None]

    def left(self):
        return self.step < len(self.steps)

    def hold(self, *others):
        if self.step == 0:
            self.sent = after(self.sent, *others)
        elif self.left():
            self.outgoing = [after(value, *others) for value in self.outgoing]

    def send(self):
        one, two = self.steps[self.step]
        if one == two:
            whole = self.sent if self.step == 0 else jnp.concatenate(self.outgoing, axis=0)
            arrived = flip(whole, *one)
            self.last = (arrived,)
            arrived = split(arrived)
        else:
            arrived = [flip(self.outgoing[0], *one), flip(self.outgoing[1], *two)]
            self.last = tuple(arrived)
        self.slots = [parts + [new] for parts, new in zip(self.slots, arrived)]
        self.step += 1
        if self.left():
            for slot, parts in enumerate(self.slots):
                half = parts[0].shape[0] // 2
                self.outgoing[slot] = sum(part[half:].astype(FULL) for part in parts).astype(LOW)
                self.slots[slot] = [part[:half] for part in parts]

    def total(self):
        while self.left():
            self.send()
        return tuple(sum(part[0].astype(FULL) for part in parts) for parts in self.slots)


def split(value):
    middle = value.shape[0] // 2
    return [value[:middle], value[middle:]]


class Blocks:
    def __init__(self, count, size):
        self.count, self.size = count, size
        shifts = [(i * size) % LANES for i in range(count)]
        self.shifts = sorted(set(shifts))
        self.wide = -(-(size + max(shifts)) // LANES) * LANES
        self.aligned = max(shifts) == 0 and size % LANES == 0
        self.total = count * size
        self.room = max(self.start(i) + self.wide for i in range(count))

    def start(self, index):
        return index * self.size // LANES * LANES

    def start_dynamic(self, index):
        return pl.multiple_of(index * self.size // LANES * LANES, LANES)

    def pad(self, value, index):
        result = None
        for shift in self.shifts:
            low = [(0, 0)] * (value.ndim - 1) + [(shift, self.wide - self.size - shift)]
            placed = jnp.pad(value, low)
            here = (index * self.size) % LANES == shift
            result = placed if result is None else jnp.where(here, placed, result)
        return result

    def cut(self, value, index):
        result = None
        for shift in self.shifts:
            piece = value[..., shift : shift + self.size]
            here = (index * self.size) % LANES == shift
            result = piece if result is None else jnp.where(here, piece, result)
        return result

    def tile_owners(self, tile):
        low, high = tile * LANES, (tile + 1) * LANES
        return [
            (i, low - self.start(i))
            for i in range(self.count)
            if i * self.size < high and (i + 1) * self.size > low
        ]


def matmul(left, right):
    return lax.dot_general(left, right, (((1,), (0,)), ((), ())), preferred_element_type=FULL)


def matmul_nt(left, right):
    return lax.dot_general(left, right, (((1,), (1,)), ((), ())), preferred_element_type=FULL)


def matmul_tn(left, right):
    return lax.dot_general(left, right, (((0,), (0,)), ((), ())), preferred_element_type=FULL)


def normed(values):
    centred = values - jnp.mean(values, axis=-1, keepdims=True)
    spread = jnp.mean(centred * centred, axis=-1, keepdims=True)
    scale = lax.rsqrt(spread + 1e-05)
    return centred * scale, scale


def norm_back(grad, unit, scale, gain):
    inner = grad * gain
    mean_inner = jnp.mean(inner, axis=-1, keepdims=True)
    mean_both = jnp.mean(inner * unit, axis=-1, keepdims=True)
    return scale * (inner - mean_inner - unit * mean_both)


def rows_at(index, size=CHUNK):
    return pl.ds(pl.multiple_of(index * size, size), size)


def places(pos, slot, codes, half):
    owner = pos[2] if slot == 0 else 1 - pos[2]
    for index, (d_mask, w_mask) in enumerate(codes):
        yield index, pos[0] ^ d_mask, owner * half + (pos[1] ^ w_mask)


def load_pieces(pos, refs, codes, half, lanes, target, sem):
    for ref, (slot, group) in zip(refs, codes):
        for index, doc, inner in places(pos, slot, group, half):
            pltpu.make_async_copy(
                ref.at[index, :, pl.ds(lanes[0], lanes[1])], target(doc, inner), sem
            ).start()


def load_folded(pos, refs, codes, half, rows, blocks, begin, folds, held, sem):
    for fold in range(folds):
        def target(doc, inner):
            first = pl.ds(pl.multiple_of((doc * folds + fold) * rows, rows), rows)
            if blocks.aligned:
                return held.at[first, pl.ds(blocks.start_dynamic(inner), blocks.wide)]
            return held.at[inner, first, :]

        load_pieces(pos, refs, codes, half, (begin + fold * blocks.wide, blocks.wide), target, sem)


def begin(source, target, sem):
    pltpu.make_async_copy(source, target, sem).start()


def finish(source, target, sem):
    pltpu.make_async_copy(source, target, sem).wait()


def store_pieces(pos, source, sums, half, targets, lanes, sem):
    for slot, codes in enumerate(sums):
        count = len(codes) // 2
        for index, doc, inner in places(pos, slot, codes, half):
            pltpu.make_async_copy(
                source(doc, inner),
                targets[index // count].at[slot * count + index % count, :, pl.ds(lanes[0], lanes[1])],
                sem,
            ).start()


def wait_whole(ref, sem):
    pltpu.make_async_copy(ref, ref, sem).wait()


def row_target(ref, blocks, rows):
    if blocks.aligned:
        return lambda doc, inner: ref.at[
            pl.ds(pl.multiple_of(inner * rows, rows), rows),
            pl.ds(blocks.start_dynamic(doc), blocks.wide),
        ]
    return lambda doc, inner: ref.at[doc, pl.ds(pl.multiple_of(inner * rows, rows), rows), :]


def held_shape(blocks, height):
    return (height, blocks.total) if blocks.aligned else (blocks.count, height, blocks.wide)


def merge_tiles(held, whole, blocks):
    for tile in range(blocks.total // LANES):
        value = None
        for index, offset in blocks.tile_owners(tile):
            piece = held[index, :, offset : offset + LANES]
            value = piece if value is None else value + piece
        whole[:, tile * LANES : (tile + 1) * LANES] = value


def project_kernel(shape, pos, gains, page_col, page_row, mask_row, own_hbm, *refs):
    codes, half, rows, blocks, length, width, factor, chunks = shape
    arrived, refs = refs[: len(chunks)], refs[len(chunks) :]
    pieces, refs = refs[: len(codes)], refs[len(codes) :]
    outs, refs = refs[:7], refs[7:]
    (q_out, k_out, v_out, att_out, lse_out, weight, other) = kept = refs[:7]
    (own, held, h_own, h_oth, allowed, sem, sem_out, sem_in) = refs[7:]
    begin(own_hbm, own, sem_in.at[0])
    load_pieces(pos, pieces, codes, half, (0, blocks.wide), row_target(held, blocks, rows), sem)
    starts = [sum(chunks[:i]) for i in range(len(chunks))]
    places_in = [other.at[pl.ds(start, size), :] for start, size in zip(starts, chunks)]
    for i, (ref, place) in enumerate(zip(arrived, places_in)):
        begin(ref, place, sem_in.at[i + 1])
    finish(own_hbm, own, sem_in.at[0])
    for i, (ref, place) in enumerate(zip(arrived, places_in)):
        finish(ref, place, sem_in.at[i + 1])
    begin(other, outs[6], sem_out.at[6])
    for i in range(length // CHUNK):
        part = pl.ds(i * CHUNK, CHUNK)
        unit, _ = normed(own[part, :].astype(FULL))
        h_own[part, :] = (unit * gains[0:1, :]).astype(LOW)
        unit, _ = normed(other[part, :].astype(FULL))
        h_oth[part, :] = (unit * gains[1:2, :]).astype(LOW)
        row = lax.broadcasted_iota(jnp.int32, (CHUNK, length), 0) + i * CHUNK
        col = lax.broadcasted_iota(jnp.int32, (CHUNK, length), 1)
        ok = (page_col[part, :] == page_row[...]) & ((mask_row[...] == 1) | (row == col))
        allowed[part, :] = jnp.where(ok, 1.0, 0.0)
    wait_whole(held, sem)
    merge_tiles(held, weight, blocks)
    begin(weight, outs[5], sem_out.at[5])
    lse_out[...] = jnp.zeros_like(lse_out)

    q_out[...] = (matmul(h_own[...], weight[:, :width]).astype(LOW) * factor).astype(LOW)
    k_out[...] = matmul(h_oth[...], weight[:, width : 2 * width]).astype(LOW)
    v_out[...] = matmul(h_oth[...], weight[:, 2 * width :]).astype(LOW)
    for i in range(3):
        begin(kept[i], outs[i], sem_out.at[i])
    size = width // HEADS
    per = LANES // size

    @pl.loop(0, width // LANES)
    def _(pair):
        cols = pl.ds(pl.multiple_of(pair * LANES, LANES), LANES)
        keys, values, queries = k_out[:, cols], v_out[:, cols], q_out[:, cols]
        lane = lax.broadcasted_iota(jnp.int32, queries.shape, 1)
        result, sums = None, lse_out[...]
        for sub in range(per):
            inside = lane // size == sub
            scores = matmul_nt(jnp.where(inside, queries, jnp.zeros_like(queries)), keys)
            scores = jnp.where(allowed[...] > 0.5, scores, NEG)
            top = jnp.max(scores, axis=-1, keepdims=True)
            exps = jnp.exp(scores - top)
            total = jnp.sum(exps, axis=-1, keepdims=True)
            out = matmul(exps.astype(LOW), values) * (1.0 / total)
            result = out if result is None else jnp.where(inside, out, result)
            sums = jnp.where(lane == pair * per + sub, top + jnp.log(total), sums)
        lse_out[...] = sums
        att_out[:, cols] = result.astype(LOW)

    for i in (3, 4):
        begin(kept[i], outs[i], sem_out.at[i])
    for i, ref in enumerate(kept):
        finish(ref, outs[i], sem_out.at[i])


def feed_kernel(shape, pos, coef, gain, page_col, att_hbm, own_hbm, cot_hbm, cotj_hbm, arrived_hbm, *refs):
    (codes, counts, sums_b, sums_c, half, rows, down_rows, ups, outs, downs, length, width, hidden, block) = shape
    pieces, refs = refs[: len(codes)], refs[len(codes) :]
    out_ref, dmid_ref, datt_ref, away_ref, dgain_ref = refs[:5]
    up_targets, down_targets = refs[5:7], refs[7:9]
    (w_up, o_held, w_out, d_held, w_down, g_up, g_out, g_down, att, own, cot, cotj_own, cotj_oth, mid, h2, h2_t, dffn, dffn_t,
     att_t, acts, dpre, acc, dacc, dbranch, sem_up, sem_out, sem_down, sem_gup, sem_gdown, sems) = refs[9:]
    begin(att_hbm, att, sems.at[0])
    last = counts
    load_pieces(pos, pieces[:last], codes[:last], half, (ups.wide, outs.wide), row_target(o_held, outs, rows), sem_out)
    begin(own_hbm, own, sems.at[1])
    begin(cot_hbm, cot, sems.at[2])
    begin(cotj_hbm, cotj_own, sems.at[3])
    begin(arrived_hbm, cotj_oth, sems.at[4])
    load_pieces(pos, pieces[:last], codes[:last], half, (0, ups.wide), row_target(w_up, ups, rows), sem_up)
    folds = down_rows // rows
    load_folded(pos, pieces[last:], codes[last:], half, rows, downs, 0, folds, d_held, sem_down)
    half_rows = length // 2
    parts = length // CHUNK

    def valid_at(part):
        return jnp.where(page_col[part, :] >= 0, 1.0, 0.0)

    finish(att_hbm, att, sems.at[0])
    wait_whole(o_held, sem_out)
    merge_tiles(o_held, w_out, outs)
    mid[...] = matmul(att[...], w_out[...])
    att_t[...] = att[...].T
    finish(own_hbm, own, sems.at[1])
    for i in range(parts):
        part = pl.ds(i * CHUNK, CHUNK)
        middle = own[part, :].astype(FULL) + valid_at(part) * mid[part, :]
        mid[part, :] = middle
        unit, _ = normed(middle)
        h2[part, :] = (unit * gain[...]).astype(LOW)
    finish(cot_hbm, cot, sems.at[2])
    finish(cotj_hbm, cotj_own, sems.at[3])
    finish(arrived_hbm, cotj_oth, sems.at[4])
    for which, ref in ((pos[2], cotj_own), (1 - pos[2], cotj_oth)):
        for i in range(half_rows // CHUNK):
            part = pl.ds(pl.multiple_of(which * half_rows + i * CHUNK, CHUNK), CHUNK)
            grad = cot[part, :] + coef[...] * ref[pl.ds(i * CHUNK, CHUNK), :].astype(FULL)
            cot[part, :] = grad
            dffn[part, :] = (grad * valid_at(part)).astype(LOW)
    dffn_t[...] = dffn[...].T
    h2_t[...] = h2[...].T
    acc[...] = jnp.zeros_like(acc)
    dacc[...] = jnp.zeros_like(dacc)
    wait_whole(w_up, sem_up)
    wait_whole(d_held, sem_down)
    if not downs.aligned:
        merge_tiles(d_held, w_down, downs)
    down = d_held if downs.aligned else w_down
    c0, c1 = 0.7978845608028654, 0.044715

    @pl.loop(0, hidden // block)
    def _(f):
        cols = pl.ds(pl.multiple_of(f * block, LANES), block)
        pre = matmul(h2[...], w_up[:, cols])
        dact = matmul(dffn[...], down[:, cols])
        square = pre * pre
        flat = jnp.tanh(c0 * (pre + c1 * square * pre))
        cdf = 0.5 * (1.0 + flat)
        slope = cdf + pre * (0.5 * (1.0 - flat * flat)) * (c0 * (1.0 + 3.0 * c1 * square))
        acts[...] = (pre * cdf).astype(LOW)
        dpre[...] = (slope * dact).astype(LOW)
        acc[...] += matmul_nt(acts[...], down[:, cols])
        dacc[...] += matmul_nt(dpre[...], w_up[:, cols])
        g_down[:, cols] = matmul(dffn_t[...], acts[...]).astype(LOW)
        g_up[:, cols] = matmul(h2_t[...], dpre[...]).astype(LOW)

    if downs.room > downs.total:
        g_down[:, downs.total :] = jnp.zeros((width, downs.room - downs.total), LOW)
    store_pieces(
        pos,
        lambda doc, inner: g_down.at[
            pl.ds(pl.multiple_of(doc * down_rows, down_rows), down_rows),
            pl.ds(downs.start_dynamic(inner), downs.wide),
        ],
        sums_c, half, down_targets, (0, downs.wide), sem_gdown,
    )
    store_pieces(
        pos,
        lambda doc, inner: g_up.at[
            pl.ds(pl.multiple_of(inner * rows, rows), rows),
            pl.ds(ups.start_dynamic(doc), ups.wide),
        ],
        sums_b, half, up_targets, (0, ups.wide), sem_gup,
    )
    dgain_ref[...] = jnp.zeros_like(dgain_ref)
    for i in range(parts):
        part = pl.ds(i * CHUNK, CHUNK)
        valid = valid_at(part)
        middle = mid[part, :]
        acc[part, :] = middle + valid * acc[part, :]
        unit, scale = normed(middle)
        grad = dacc[part, :]
        dgain_ref[0:1, :] += jnp.sum(grad * unit, axis=0, keepdims=True)
        dmid = cot[part, :] + norm_back(grad, unit, scale, gain[...])
        dacc[part, :] = dmid
        dbranch[part, :] = (dmid * valid).astype(LOW)
    begin(acc, out_ref, sems.at[0])
    begin(dacc, dmid_ref, sems.at[1])
    h2[...] = matmul_nt(dbranch[...], w_out[...]).astype(LOW)
    begin(h2, datt_ref, sems.at[2])
    g_out[:, : outs.total] = matmul(att_t[...], dbranch[...]).astype(LOW)
    if outs.room > outs.total:
        g_out[:, outs.total :] = jnp.zeros((width, outs.room - outs.total), LOW)
    store_pieces(
        pos,
        lambda doc, inner: g_out.at[
            pl.ds(pl.multiple_of(inner * rows, rows), rows),
            pl.ds(outs.start_dynamic(doc), outs.wide),
        ],
        sums_b, half, up_targets, (ups.wide, outs.wide), sem_gup,
    )
    for i in range(half_rows // CHUNK):
        part = pl.ds(pl.multiple_of((1 - pos[2]) * half_rows + i * CHUNK, CHUNK), CHUNK)
        away_ref[pl.ds(i * CHUNK, CHUNK), :] = acc[part, :].astype(LOW)
    for target in down_targets:
        wait_whole(target, sem_gdown)
    for target in up_targets:
        wait_whole(target, sem_gup)
    finish(acc, out_ref, sems.at[0])
    finish(dacc, dmid_ref, sems.at[1])
    finish(h2, datt_ref, sems.at[2])


def scores_back_kernel(shape, pairs, page_col, page_row, mask_row, q_hbm, k_hbm, v_hbm, att_hbm, datt_hbm, lse_hbm, *refs):
    length, width, factor = shape
    outs, refs = refs[:3], refs[3:]
    (q_ref, k_ref, v_ref, att, datt, lse, dq, dk, dv, allowed, lse_t, dots_t, sems) = refs
    size = width // HEADS
    per = LANES // size
    cols_here = pl.ds(pairs[0] * LANES, (pairs[1] - pairs[0]) * LANES)
    loads = [(source.at[:, cols_here], target) for source, target in
             ((datt_hbm, datt), (att_hbm, att), (q_hbm, q_ref), (k_hbm, k_ref), (v_hbm, v_ref))]
    loads.append((lse_hbm, lse))
    for i, (source, target) in enumerate(loads):
        begin(source, target, sems.at[i])
    mask = jnp.broadcast_to(mask_row[...].astype(FULL), (LANES, length)).T[:, 0:1]
    row = lax.broadcasted_iota(jnp.int32, (length, length), 0)
    col = lax.broadcasted_iota(jnp.int32, (length, length), 1)
    ok = (page_col[...] == page_row[...]) & ((mask == 1.0) | (row == col))
    allowed[...] = jnp.where(ok, 1.0, 0.0)
    here_width = cols_here.size
    head = lax.broadcasted_iota(jnp.int32, (LANES, here_width), 0)
    lane = lax.broadcasted_iota(jnp.int32, (LANES, here_width), 1)
    chosen = jnp.where(lane // size == head, 1.0, 0.0)
    for i, (source, target) in enumerate(loads):
        finish(source, target, sems.at[i])
    dots_t[...] = lax.dot_general(
        chosen, att[...].astype(FULL) * datt[...].astype(FULL), (((1,), (1,)), ((), ())),
        preferred_element_type=FULL, precision=lax.Precision.HIGHEST,
    )
    lse_t[...] = lse[...].T

    @pl.loop(0, pairs[1] - pairs[0])
    def _(pair):
        cols = pl.ds(pl.multiple_of(pair * LANES, LANES), LANES)
        queries, grads = q_ref[:, cols], datt[:, cols]
        keys, values = k_ref[:, cols], v_ref[:, cols]
        lane = lax.broadcasted_iota(jnp.int32, (length, LANES), 1)
        zero = jnp.zeros_like(queries)
        trio = None
        for sub in range(per):
            inside = lane // size == sub
            lse_row = lse_t[pl.ds((pair + pairs[0]) * per + sub, 1), :]
            dot_row = dots_t[pl.ds(pair * per + sub, 1), :]
            scores = matmul_nt(keys, jnp.where(inside, queries, zero))
            scores = jnp.where(allowed[...] > 0.5, scores, NEG)
            probs = jnp.exp(scores - lse_row)
            dprob = matmul_nt(values, jnp.where(inside, grads, zero))
            low = (probs * (dprob - dot_row)).astype(LOW)
            three = (matmul_tn(low, keys), matmul(low, queries), matmul(probs.astype(LOW), grads))
            trio = three if trio is None else [jnp.where(inside, new, old) for new, old in zip(three, trio)]
        dq[:, cols] = (trio[0] * factor).astype(LOW)
        dk[:, cols] = trio[1].astype(LOW)
        dv[:, cols] = trio[2].astype(LOW)

    for i, (source, target) in enumerate(zip((dq, dk, dv), outs)):
        begin(source, target, sems.at[i])
    for i, (source, target) in enumerate(zip((dq, dk, dv), outs)):
        finish(source, target, sems.at[i])


def project_back_kernel(shape, pos, gains, own_hbm, other_hbm, weight_hbm, *refs):
    (sums, half, rows, blocks, length, width, runs) = shape
    given, refs = refs[: 3 * len(runs)], refs[3 * len(runs) :]
    own_out, oth_ref, dgain_ref = refs[:3]
    targets, refs = refs[3:5], refs[5:]
    h_t, flat, own_ref, grad, own, other, weight, sem, sems = refs[:9]
    copies = refs[9:]
    grads = [copies[3 * i : 3 * i + 3] for i in range(len(runs))]
    parts = length // CHUNK
    loads = [(own_hbm, own), (other_hbm, other), *zip(given, copies), (weight_hbm, weight)]
    for i, (source, target) in enumerate(loads):
        begin(source, target, sems.at[i])

    def take(i):
        finish(*loads[i], sems.at[i])

    for which, source in ((0, own), (1, other)):
        take(which)
        for i in range(parts):
            part = pl.ds(i * CHUNK, CHUNK)
            unit, _ = normed(source[part, :].astype(FULL))
            flat[part, :] = unit * gains[which : which + 1, :]
        h_t[which] = flat[...].astype(LOW).T
    for i in range(2, len(loads) - 1):
        take(i)
    for (low, high), trio in zip(runs, grads):
        for block, (which, ref) in enumerate(zip((0, 1, 1), trio)):
            grad[:, block * width + low : block * width + high] = matmul(h_t[which], ref[...]).astype(LOW)
    if blocks.room > blocks.total:
        grad[:, blocks.total :] = jnp.zeros((width, blocks.room - blocks.total), LOW)
    store_pieces(
        pos,
        lambda doc, inner: grad.at[
            pl.ds(pl.multiple_of(inner * rows, rows), rows),
            pl.ds(blocks.start_dynamic(doc), blocks.wide),
        ],
        sums, half, targets, (0, blocks.wide), sem,
    )
    dgain_ref[...] = jnp.zeros_like(dgain_ref)
    take(len(loads) - 1)
    own_ref[...] = sum(
        matmul_nt(trio[0][...], weight[:, low:high]) for (low, high), trio in zip(runs, grads)
    )
    begin(own_ref, own_out, sems.at[0])
    flat[...] = sum(
        matmul_nt(trio[block][...], weight[:, block * width + low : block * width + high])
        for (low, high), trio in zip(runs, grads)
        for block in (1, 2)
    )
    for i in range(parts):
        part = pl.ds(i * CHUNK, CHUNK)
        unit, _ = normed(own[part, :].astype(FULL))
        dgain_ref[0:1, :] += jnp.sum(own_ref[part, :] * unit, axis=0, keepdims=True)
        unit, _ = normed(other[part, :].astype(FULL))
        value = flat[part, :]
        oth_ref[part, :] = value.astype(LOW)
        dgain_ref[1:2, :] += jnp.sum(value * unit, axis=0, keepdims=True)
    finish(own_ref, own_out, sems.at[0])
    for target in targets:
        wait_whole(target, sem)


def tail_kernel(length, own, gain, mine, theirs, dmid, out_ref):
    for i in range(length // CHUNK):
        part = pl.ds(i * CHUNK, CHUNK)
        unit, scale = normed(own[part, :].astype(FULL))
        grad = mine[part, :] + theirs[part, :].astype(FULL)
        out_ref[part, :] = dmid[part, :] + norm_back(grad, unit, scale, gain[...])


VMEM = pl.BlockSpec(memory_space=pltpu.VMEM)
HBM = pl.BlockSpec(memory_space=pltpu.HBM)
SMEM = pl.BlockSpec(memory_space=pltpu.SMEM)


LITTLE = pl.CostEstimate(flops=1_000, bytes_accessed=1_000, transcendentals=0)


def params(mebibytes):
    return pltpu.CompilerParams(vmem_limit_bytes=mebibytes * 1024 * 1024)


def adam_update(weight, first, second, grad, rate, decay):
    first_new = 0.9 * first + 0.1 * grad
    second_new = 0.999 * second + 0.001 * grad * grad
    first_hat = first_new / (1.0 - 0.9**STEP)
    second_hat = second_new / (1.0 - 0.999**STEP)
    weight_new = weight - rate * (first_hat / (jnp.sqrt(second_hat) + 1e-08) + decay * weight)
    return (weight_new, first_new, second_new)


def shards(
    rows, cot_stream, cot_joined, page, key_mask,
    w_qkv, m_qkv, v_qkv, w_out, m_out, v_out, w_up, m_up, v_up, w_down, m_down, v_down,
    gains, m_gains, v_gains,
):
    docs, wide = lax.axis_size("docs"), lax.axis_size("wide")
    half = wide // 2
    doc, place = lax.axis_index("docs"), lax.axis_index("wide")
    stream = place // half
    is_text = stream == 0
    pos = jnp.stack((doc, place % half, stream)).astype(jnp.int32)
    length, width = rows.shape
    half_rows = length // 2
    factor = float(width // HEADS) ** (-0.5)
    piece_rows = w_qkv.shape[1]
    hidden = w_up.shape[2] * docs
    qkvs, outs, ups = Blocks(docs, w_qkv.shape[2]), Blocks(docs, w_out.shape[2]), Blocks(docs, w_up.shape[2])
    downs = Blocks(wide, w_down.shape[1])
    down_rows = w_down.shape[2]

    core = [("wide", 1)]
    along_x = [("docs", 1)]
    along_y = [("docs", 1 << b) for b in range(1, docs.bit_length() - 1)]
    along_z = [("wide", 1 << b) for b in range(1, half.bit_length() - 1)]
    across = ("wide", half)

    def swap(value):
        return flip(value, *across)

    column = doc * w_qkv.shape[2] + lax.iota(jnp.int32, w_qkv.shape[2])
    is_query = (column < width)[None, None, :]
    pair_qkv = jnp.where(is_query, w_qkv, w_qkv[::-1]).astype(LOW)

    def own_first(pair):
        return jnp.where(is_text, pair, pair[::-1])

    unit_a = qkvs.pad(own_first(pair_qkv), doc)
    unit_b = jnp.concatenate(
        (ups.pad(own_first(w_up.astype(LOW)), doc), outs.pad(own_first(w_out.astype(LOW)), doc)), axis=-1
    )
    unit_c = downs.pad(jnp.swapaxes(own_first(w_down.astype(LOW)), 1, 2), place)
    folds = down_rows // piece_rows

    def folded(unit):
        return jnp.concatenate([unit[i * piece_rows : (i + 1) * piece_rows] for i in range(folds)], axis=-1)

    unit_a_oth = swap(unit_a[1])
    unit_b_oth = swap(after(unit_b[1], unit_a_oth)) if FIRST_A else swap(unit_b[1])
    if downs.aligned:
        unit_c_oth = swap(after(unit_c[1], unit_a_oth))
    else:
        raw = jnp.swapaxes(own_first(w_down.astype(LOW)), 1, 2)
        unit_c_oth = downs.pad(swap(raw[1]), (place + half) % wide)
    zxy, zyx = along_z + along_x + along_y, along_z + along_y + along_x
    a_own, a_oth = Doubling(unit_a[0], 0, zxy), Doubling(unit_a_oth, 1, zyx)
    b_own = Doubling(unit_b[0], 0, along_y + along_x + along_z)
    c_own = Doubling(folded(unit_c[0]), 0, along_x + along_z + along_y)
    b_oth, c_oth = Doubling(unit_b_oth, 1, zxy), Doubling(folded(unit_c_oth), 1, zyx)
    steps_y, steps_x = len(along_y), len(along_x)
    chunks, begin = [], 0
    for size in [length * part // sum(ROW_PARTS) for part in ROW_PARTS]:
        some = rows[begin : begin + size]
        chunks.append(swap(after(some, chunks[-1] if chunks else unit_a_oth)))
        begin += size
    for _ in range(steps_y):
        b_own.send()
    for _ in range(steps_x):
        c_own.send()
    for _ in range(steps_x):
        b_own.send(unit_a_oth)
    for _ in along_z:
        c_own.send(unit_a_oth)
    a_own.send_all()
    a_oth.send_all()
    first = (a_oth.arrays[len(along_z) + steps_y], a_own.arrays[len(along_z) + steps_x])
    rest = (a_oth.arrays[-1], a_own.arrays[-1])
    for one in (b_oth, c_oth):
        for _ in along_z:
            one.send(*first)
    met = b_oth.last + c_oth.last
    for one in (b_own, c_own):
        while one.step < len(one.order):
            one.send(*met)
    for one, steps in ((b_oth, steps_x), (c_oth, steps_y)):
        for _ in range(steps):
            one.send(*rest, chunks[1])
    for one in (b_oth, c_oth):
        while one.step < len(one.order):
            one.send(chunks[-1])
    pieces_a, codes_a = [], []
    for one in (a_own, a_oth):
        for value, known in one.split_newest():
            one.add(value, known, *core[0])
        pieces_a += one.arrays
        codes_a += one.slotted()
    waiting, passed = [], []
    for one in (b_own, b_oth, c_own, c_oth):
        early, late = one.split_newest()
        passed.append(one.add(after(early[0], chunks[-1]), early[1], *core[0]))
        waiting.append((one, *late))
    other_joined = swap(after(cot_joined.astype(LOW), chunks[-1], *passed))

    page_col, page_row = page[:, None], page[None, :]
    mask_row = key_mask[None, :]
    gain_own = lax.dynamic_index_in_dim(gains, stream, 0, keepdims=True)
    gain_oth = lax.dynamic_index_in_dim(gains, 1 - stream, 0, keepdims=True)
    gain_one = jnp.concatenate((gain_own, gain_oth), axis=0)
    gain_two = lax.dynamic_index_in_dim(gains, 2 + stream, 0, keepdims=True)
    mix = jax.nn.sigmoid(gains[4])[None, :]
    coef = jnp.where(is_text, mix, 1.0 - mix)

    low_rows = jax.ShapeDtypeStruct((length, width), LOW)
    full_rows = jax.ShapeDtypeStruct((length, width), FULL)

    sizes = tuple(chunk.shape[0] for chunk in chunks)
    shape = (codes_a, half, piece_rows, qkvs, length, width, factor, sizes)
    made = (low_rows, low_rows, low_rows, low_rows, jax.ShapeDtypeStruct((length, LANES), FULL),
            jax.ShapeDtypeStruct((width, 3 * width), LOW), low_rows)
    queries, keys, values, attended, lse, weight_qkv, other_rows = pl.pallas_call(
        functools.partial(project_kernel, shape),
        out_shape=made,
        in_specs=[SMEM] + [VMEM] * 4 + [HBM] * (1 + len(chunks) + len(pieces_a)),
        out_specs=(HBM,) * 7,
        scratch_shapes=[pltpu.VMEM(one.shape, one.dtype) for one in made] + [
            pltpu.VMEM((length, width), LOW),
            pltpu.VMEM((docs, width, qkvs.wide), LOW),
            pltpu.VMEM((length, width), LOW),
            pltpu.VMEM((length, width), LOW),
            pltpu.VMEM((length, length), FULL),
            pltpu.SemaphoreType.DMA,
            pltpu.SemaphoreType.DMA((7,)),
            pltpu.SemaphoreType.DMA((1 + len(chunks),)),
        ],
        compiler_params=params(60),
        cost_estimate=LITTLE,
        name="project_attend",
    )(pos, gain_one, page_col, page_row, mask_row, rows, *chunks, *pieces_a)

    here = [value for _, value, _ in waiting]
    for one, value, known in waiting:
        one.add(after(value, lse, other_joined, *here), known, *core[0])
    streams = (b_own, b_oth, c_own, c_oth)
    pieces_b = sum((one.arrays for one in streams), [])
    codes_b = sum((one.slotted() for one in streams), [])
    counts = len(b_own.arrays) + len(b_oth.arrays)
    xy, yx = along_x + along_y, along_y + along_x
    steps_b = [core * 2, *zip(xy, yx), *((step, step) for step in along_z)]
    steps_c = [core * 2, *((step, step) for step in along_z + xy)]
    sums_of = [tuple(sum_codes([pair[slot] for pair in steps]) for slot in (0, 1)) for steps in (steps_b, steps_c)]
    sent_count = len(sums_of[0][0])
    block = 6 * LANES
    shape = (codes_b, counts, *sums_of, half, piece_rows, down_rows, ups, outs, downs, length, width, hidden, block)
    shape_b = jax.ShapeDtypeStruct((sent_count, piece_rows, ups.wide + outs.wide), LOW)
    shape_c = jax.ShapeDtypeStruct((sent_count, down_rows, downs.wide), LOW)
    (stream_out, middle_grad, attended_grad, away, dgain_two, kept_b, sent_b, kept_c, sent_c) = pl.pallas_call(
        functools.partial(feed_kernel, shape),
        out_shape=(full_rows, full_rows, low_rows, jax.ShapeDtypeStruct((half_rows, width), LOW),
                   jax.ShapeDtypeStruct((8, width), FULL), shape_b, shape_b, shape_c, shape_c),
        in_specs=[SMEM] + [VMEM] * 3 + [HBM] * (5 + len(pieces_b)),
        out_specs=(HBM,) * 3 + (VMEM,) * 2 + (HBM,) * 4,
        scratch_shapes=[
            pltpu.VMEM((width, hidden), LOW),
            pltpu.VMEM(held_shape(outs, width), LOW),
            pltpu.VMEM((width, width), LOW),
            pltpu.VMEM(held_shape(downs, width), LOW),
            pltpu.VMEM((8, LANES) if downs.aligned else (width, hidden), LOW),
            pltpu.VMEM((width, hidden), LOW),
            pltpu.VMEM((width, outs.room), LOW),
            pltpu.VMEM((width, downs.room), LOW),
            pltpu.VMEM((length, width), LOW),
            pltpu.VMEM((length, width), LOW),
            pltpu.VMEM((length, width), FULL),
            pltpu.VMEM((half_rows, width), FULL),
            pltpu.VMEM((half_rows, width), LOW),
            pltpu.VMEM((length, width), FULL),
            pltpu.VMEM((length, width), LOW),
            pltpu.VMEM((width, length), LOW),
            pltpu.VMEM((length, width), LOW),
            pltpu.VMEM((width, length), LOW),
            pltpu.VMEM((width, length), LOW),
            pltpu.VMEM((length, block), LOW),
            pltpu.VMEM((length, block), LOW),
            pltpu.VMEM((length, width), FULL),
            pltpu.VMEM((length, width), FULL),
            pltpu.VMEM((length, width), LOW),
        ] + [pltpu.SemaphoreType.DMA] * 5 + [pltpu.SemaphoreType.DMA((5,))],
        compiler_params=params(60),
        cost_estimate=LITTLE,
        name="feed_forward_back",
    )(pos, coef, gain_two, page_col, attended, rows, cot_stream, cot_joined, other_joined, *pieces_b)

    def attend_back(pairs, *operands):
        low_cols = jax.ShapeDtypeStruct((length, (pairs[1] - pairs[0]) * LANES), LOW)
        piece = pltpu.VMEM(low_cols.shape, LOW)
        return pl.pallas_call(
            functools.partial(scores_back_kernel, (length, width, factor), pairs),
            out_shape=(low_cols,) * 3,
            in_specs=[VMEM] * 3 + [HBM] * 6,
            out_specs=(HBM,) * 3,
            scratch_shapes=[piece] * 5 + [pltpu.VMEM((length, LANES), FULL)] + [piece] * 3 + [
                pltpu.VMEM((length, length), FULL),
                pltpu.VMEM((LANES, length), FULL),
                pltpu.VMEM((LANES, length), FULL),
                pltpu.SemaphoreType.DMA((6,)),
            ],
            compiler_params=params(60),
            cost_estimate=LITTLE,
            name="attend_back",
        )(page_col, page_row, mask_row, *operands)

    sums_b, sums_c = Halving(kept_b, sent_b, steps_b), Halving(kept_c, sent_c, steps_c)
    sums_b.send()
    sums_c.send()
    quarter = half_rows // 2
    partner_one = swap(away[:quarter])
    pair_count = width // LANES
    cuts = (0, pair_count * 2 // 3, pair_count)
    grads_one = attend_back(cuts[:2], queries, keys, values, attended, attended_grad, lse)
    met = (*sums_b.last, *sums_c.last, partner_one)
    second = after(queries, grads_one[0], *met)
    sums_b.hold(grads_one[0], *met)
    sums_c.hold(grads_one[0], *met)
    sums_b.send()
    sums_c.send()
    partner_two = swap(after(away[quarter:], grads_one[0], *met))
    partner_rows = jnp.concatenate((partner_one, partner_two), axis=0)
    grads_two = attend_back(cuts[1:], second, keys, values, attended, attended_grad, lse)

    runs = tuple((low * LANES, high * LANES) for low, high in zip(cuts[:-1], cuts[1:]))
    shape = (sums_of[0], half, piece_rows, qkvs, length, width, runs)
    shape_a = jax.ShapeDtypeStruct((sent_count, piece_rows, qkvs.wide), LOW)
    own_part, away_part, dgain_one, kept_a, sent_a = pl.pallas_call(
        functools.partial(project_back_kernel, shape),
        out_shape=(full_rows, low_rows, jax.ShapeDtypeStruct((8, width), FULL)) + (shape_a,) * 2,
        in_specs=[SMEM, VMEM] + [HBM] * (3 + 3 * len(runs)),
        out_specs=(HBM,) + (VMEM,) * 2 + (HBM,) * 2,
        scratch_shapes=[
            pltpu.VMEM((2, width, length), LOW),
            pltpu.VMEM((length, width), FULL),
            pltpu.VMEM((length, width), FULL),
            pltpu.VMEM((width, qkvs.room), LOW),
            pltpu.VMEM((length, width), LOW),
            pltpu.VMEM((length, width), LOW),
            pltpu.VMEM((width, 3 * width), LOW),
            pltpu.SemaphoreType.DMA,
            pltpu.SemaphoreType.DMA((3 + 3 * len(runs),)),
        ] + [pltpu.VMEM((length, high - low), LOW) for low, high in runs for _ in range(3)],
        compiler_params=params(60),
        cost_estimate=LITTLE,
        name="project_back",
    )(pos, gain_one, rows, other_rows, weight_qkv, *grads_one, *grads_two)

    sums_a = Halving(kept_a, sent_a, steps_b)
    sums_a.hold(*sums_b.last, *sums_c.last)
    backs, start = [], 0
    for index, part in enumerate(BACK_PARTS):
        size = length * part // sum(BACK_PARTS)
        backs.append(swap(after(away_part[start : start + size], *sums_a.last)))
        start += size
        before = sums_a.last
        if index == 1:
            sums_a.hold(partner_two)
        sums_a.send()
        for one, steps in ((sums_b, (2, 3)), (sums_c, (1, 3))):
            if index in steps and one.left():
                one.hold(*before)
                one.send()
    back_part = jnp.concatenate(backs, axis=0)

    own_rows = lax.dynamic_slice_in_dim(stream_out, stream * half_rows, half_rows, 0)
    partner_rows = partner_rows.astype(FULL)
    text_rows = jnp.where(is_text, own_rows, partner_rows)
    image_rows = jnp.where(is_text, partner_rows, own_rows)
    joined_rows = mix * text_rows + (1.0 - mix) * image_rows
    gate_grad = jnp.sum(cot_joined * (text_rows - image_rows), axis=0, keepdims=True) * mix * (1.0 - mix)

    slot_index = lax.iota(jnp.int32, 5)[:, None]
    small = (
        jnp.where(slot_index == stream, dgain_one[0:1], 0.0)
        + jnp.where(slot_index == 1 - stream, dgain_one[1:2], 0.0)
        + jnp.where(slot_index == 2 + stream, dgain_two[0:1], 0.0)
        + jnp.where(slot_index == 4, gate_grad, 0.0)
    )
    for step in core + along_x + along_y + along_z + [across]:
        small = small + flip(small, *step)
    gains_grad = small
    grad_rows = pl.pallas_call(
        functools.partial(tail_kernel, length),
        out_shape=full_rows,
        in_specs=[VMEM] * 5,
        out_specs=VMEM,
        compiler_params=params(10),
        name="norm_tail",
    )(rows, gain_own, own_part, back_part, after(middle_grad, *sums_a.last))

    def late(pair):
        return tuple(after(value, *sums_a.last) for value in pair)

    total_a, total_b, total_c = sums_a.total(), sums_b.total(), sums_c.total()

    def both(total):
        return total[0], swap(total[1].astype(LOW))

    def placed(mine, theirs):
        theirs = theirs.astype(FULL)
        return jnp.where(is_text, jnp.stack((mine, theirs)), jnp.stack((theirs, mine)))

    mine_b, theirs_b = late(both(total_b))
    grad_b = placed(mine_b, theirs_b)
    grad_up = ups.cut(grad_b[..., : ups.wide], doc)
    grad_out = outs.cut(grad_b[..., ups.wide :], doc)
    if downs.aligned:
        mine_c, theirs_c = late(both(total_c))
    else:
        mine_c = downs.cut(total_c[0], place)
        theirs_c = swap(downs.cut(total_c[1], (place + half) % wide).astype(LOW))
    grad_down = jnp.swapaxes(placed(mine_c, theirs_c), 1, 2)
    mine_a, theirs_a = both(total_a)
    mine_a, theirs_a = qkvs.cut(mine_a, doc), qkvs.cut(theirs_a.astype(FULL), doc)
    query_here = is_query[0]
    grad_qkv = placed(
        jnp.where(query_here, mine_a, theirs_a), jnp.where(query_here, theirs_a, mine_a)
    )

    qkv_new = adam_update(w_qkv, m_qkv, v_qkv, grad_qkv, 0.12, 0.01)
    out_new = adam_update(w_out, m_out, v_out, grad_out, 0.5, 0.01)
    up_new = adam_update(w_up, m_up, v_up, grad_up, 0.12, 0.01)
    down_new = adam_update(w_down, m_down, v_down, grad_down, 0.06, 0.01)
    gains_new = adam_update(gains, m_gains, v_gains, gains_grad, 0.8, 0.0)
    return (stream_out, joined_rows, grad_rows, *qkv_new, *out_new, *up_new, *down_new, *gains_new)


def solution(mesh):
    by_rows = P(("docs", "wide"), None)
    by_row = P(("docs", "wide"))
    weight = P(None, "wide", "docs")
    return jax.shard_map(
        shards,
        mesh=mesh,
        in_specs=(by_rows,) * 3 + (by_row,) * 2 + (weight,) * 12 + (P(),) * 3,
        out_specs=(by_rows,) * 3 + (weight,) * 12 + (P(),) * 3,
        check_vma=False,
    )
```

```python
import functools

import jax
import jax.numpy as jnp
from jax import lax
from jax.experimental import pallas as pl
from jax.experimental.pallas import tpu as pltpu
from jax.sharding import PartitionSpec as P

HEADS = 12
STEP = 10
LANES = 128
CHUNK = 128
ROW_PARTS = (5, 6, 5)
FIRST_A = False
NEG = -1000000000.0
LOW = jnp.bfloat16
FULL = jnp.float32


def flip(value, axis, mask):
    count = lax.axis_size(axis)
    return lax.ppermute(value, axis, [(i, i ^ mask) for i in range(count)])


def flipped(codes, axis, mask):
    d_mask = mask if axis == "docs" else 0
    w_mask = mask if axis == "wide" else 0
    return [(d ^ d_mask, w ^ w_mask) for d, w in codes]


def after(value, *others):
    return lax.optimization_barrier((value, *others))[0]


class Doubling:
    def __init__(self, unit, slot, order):
        self.slot, self.order, self.step = slot, order, 0
        self.arrays, self.codes = [unit[None]], [[(0, 0)]]
        self.last = ()

    def held(self):
        held = self.arrays[0] if len(self.arrays) == 1 else jnp.concatenate(self.arrays, axis=0)
        return held, [code for group in self.codes for code in group]

    def send(self, *others):
        held, known = self.held()
        if others:
            held = after(held, *others)
        axis, mask = self.order[self.step]
        self.arrays.append(flip(held, axis, mask))
        self.codes.append(flipped(known, axis, mask))
        self.step, self.last = self.step + 1, (self.arrays[-1],)

    def send_all(self):
        while self.step < len(self.order):
            self.send()

    def split_newest(self):
        newest, newest_known = self.arrays.pop(), self.codes.pop()
        held, known = self.held()
        self.arrays.append(newest)
        self.codes.append(newest_known)
        return (held, known), (newest, newest_known)

    def add(self, value, known, axis, mask):
        self.arrays.append(flip(value, axis, mask))
        self.codes.append(flipped(known, axis, mask))
        return self.arrays[-1]

    def slotted(self):
        return [(self.slot, group) for group in self.codes]


def sum_codes(order):
    codes = [(0, 0)]
    for axis, mask in reversed(order):
        codes = codes + flipped(codes, axis, mask)
    return codes


def halves_of(value):
    high = lax.reduce_precision(value, 8, 7)
    return high, lax.reduce_precision(value - high, 8, 7)


def with_rider(value, rider):
    lanes = value.shape[-1]
    rows = -(-rider.size // lanes)
    flat = [jnp.pad(part.reshape(-1), (0, rows * lanes - rider.size)) for part in halves_of(rider)]
    tail = jnp.concatenate(flat).astype(LOW).reshape(2 * rows, lanes)
    tail = jnp.pad(tail, ((0, -(2 * rows) % 16), (0, 0)))
    return jnp.concatenate((value.reshape(-1, lanes), tail), axis=0)


def rider_of(message, shape, value_shape):
    count = value_shape[0] * value_shape[1]
    lanes = message.shape[-1]
    rows = -(-(shape[0] * shape[1]) // lanes)
    parts = [
        message[count + i * rows : count + (i + 1) * rows].reshape(-1)[: shape[0] * shape[1]].reshape(shape)
        for i in (0, 1)
    ]
    return message[:count].reshape(value_shape), parts[0].astype(FULL) + parts[1].astype(FULL)


def kept_rider(rider):
    high, low = halves_of(rider)
    return high + low


class Halving:
    def __init__(self, kept, sent, steps):
        self.slots, self.sent, self.steps = split(kept), sent, steps
        self.step, self.last = 0, ()
        self.slots = [[half] for half in self.slots]
        self.outgoing = [None, None]
        self.rider = None

    def carry(self, value, axis, mask):
        if self.rider is None or self.step == 0:
            return flip(value, axis, mask)
        message = flip(with_rider(value, self.rider), axis, mask)
        value, rider = rider_of(message, self.rider.shape, value.shape)
        self.rider = kept_rider(self.rider) + rider
        return value

    def left(self):
        return self.step < len(self.steps)

    def hold(self, *others):
        if self.step == 0:
            self.sent = after(self.sent, *others)
        elif self.left():
            self.outgoing = [after(value, *others) for value in self.outgoing]

    def send(self):
        one, two = self.steps[self.step]
        if one == two:
            whole = self.sent if self.step == 0 else jnp.concatenate(self.outgoing, axis=0)
            arrived = self.carry(whole, *one)
            self.last = (arrived,)
            arrived = split(arrived)
        else:
            arrived = [self.carry(self.outgoing[0], *one), flip(self.outgoing[1], *two)]
            self.last = tuple(arrived)
        self.slots = [parts + [new] for parts, new in zip(self.slots, arrived)]
        self.step += 1
        if self.left():
            for slot, parts in enumerate(self.slots):
                half = parts[0].shape[0] // 2
                self.outgoing[slot] = sum(part[half:].astype(FULL) for part in parts).astype(LOW)
                self.slots[slot] = [part[:half] for part in parts]

    def total(self):
        while self.left():
            self.send()
        return tuple(sum(part[0].astype(FULL) for part in parts) for parts in self.slots)


def split(value):
    middle = value.shape[0] // 2
    return [value[:middle], value[middle:]]


class Blocks:
    def __init__(self, count, size):
        self.count, self.size = count, size
        shifts = [(i * size) % LANES for i in range(count)]
        self.shifts = sorted(set(shifts))
        self.wide = -(-(size + max(shifts)) // LANES) * LANES
        self.aligned = max(shifts) == 0 and size % LANES == 0
        self.total = count * size
        self.room = max(self.start(i) + self.wide for i in range(count))

    def start(self, index):
        return index * self.size // LANES * LANES

    def start_dynamic(self, index):
        return pl.multiple_of(index * self.size // LANES * LANES, LANES)

    def pad(self, value, index):
        result = None
        for shift in self.shifts:
            low = [(0, 0)] * (value.ndim - 1) + [(shift, self.wide - self.size - shift)]
            placed = jnp.pad(value, low)
            here = (index * self.size) % LANES == shift
            result = placed if result is None else jnp.where(here, placed, result)
        return result

    def cut(self, value, index):
        result = None
        for shift in self.shifts:
            piece = value[..., shift : shift + self.size]
            here = (index * self.size) % LANES == shift
            result = piece if result is None else jnp.where(here, piece, result)
        return result

    def tile_owners(self, tile):
        low, high = tile * LANES, (tile + 1) * LANES
        return [
            (i, low - self.start(i))
            for i in range(self.count)
            if i * self.size < high and (i + 1) * self.size > low
        ]


def matmul(left, right):
    return lax.dot_general(left, right, (((1,), (0,)), ((), ())), preferred_element_type=FULL)


def matmul_nt(left, right):
    return lax.dot_general(left, right, (((1,), (1,)), ((), ())), preferred_element_type=FULL)


def matmul_tn(left, right):
    return lax.dot_general(left, right, (((0,), (0,)), ((), ())), preferred_element_type=FULL)


def normed(values):
    centred = values - jnp.mean(values, axis=-1, keepdims=True)
    spread = jnp.mean(centred * centred, axis=-1, keepdims=True)
    scale = lax.rsqrt(spread + 1e-05)
    return centred * scale, scale


def norm_back(grad, unit, scale, gain):
    inner = grad * gain
    mean_inner = jnp.mean(inner, axis=-1, keepdims=True)
    mean_both = jnp.mean(inner * unit, axis=-1, keepdims=True)
    return scale * (inner - mean_inner - unit * mean_both)


def rows_at(index, size=CHUNK):
    return pl.ds(pl.multiple_of(index * size, size), size)


def places(pos, slot, codes, half):
    owner = pos[2] if slot == 0 else 1 - pos[2]
    for index, (d_mask, w_mask) in enumerate(codes):
        yield index, pos[0] ^ d_mask, owner * half + (pos[1] ^ w_mask)


def load_pieces(pos, refs, codes, half, lanes, target, sem):
    for ref, (slot, group) in zip(refs, codes):
        for index, doc, inner in places(pos, slot, group, half):
            pltpu.make_async_copy(
                ref.at[index, :, pl.ds(lanes[0], lanes[1])], target(doc, inner), sem
            ).start()


def load_folded(pos, refs, codes, half, rows, blocks, begin, folds, held, sem):
    for fold in range(folds):
        def target(doc, inner):
            first = pl.ds(pl.multiple_of((doc * folds + fold) * rows, rows), rows)
            if blocks.aligned:
                return held.at[first, pl.ds(blocks.start_dynamic(inner), blocks.wide)]
            return held.at[inner, first, :]

        load_pieces(pos, refs, codes, half, (begin + fold * blocks.wide, blocks.wide), target, sem)


def begin(source, target, sem):
    pltpu.make_async_copy(source, target, sem).start()


def finish(source, target, sem):
    pltpu.make_async_copy(source, target, sem).wait()


def store_pieces(pos, source, sums, half, targets, lanes, sem):
    for slot, codes in enumerate(sums):
        count = len(codes) // 2
        for index, doc, inner in places(pos, slot, codes, half):
            pltpu.make_async_copy(
                source(doc, inner),
                targets[index // count].at[slot * count + index % count, :, pl.ds(lanes[0], lanes[1])],
                sem,
            ).start()


def wait_whole(ref, sem):
    pltpu.make_async_copy(ref, ref, sem).wait()


def row_target(ref, blocks, rows):
    if blocks.aligned:
        return lambda doc, inner: ref.at[
            pl.ds(pl.multiple_of(inner * rows, rows), rows),
            pl.ds(blocks.start_dynamic(doc), blocks.wide),
        ]
    return lambda doc, inner: ref.at[doc, pl.ds(pl.multiple_of(inner * rows, rows), rows), :]


def held_shape(blocks, height):
    return (height, blocks.total) if blocks.aligned else (blocks.count, height, blocks.wide)


def merge_tiles(held, whole, blocks):
    for tile in range(blocks.total // LANES):
        value = None
        for index, offset in blocks.tile_owners(tile):
            piece = held[index, :, offset : offset + LANES]
            value = piece if value is None else value + piece
        whole[:, tile * LANES : (tile + 1) * LANES] = value


def project_kernel(shape, pos, gains, page_col, page_row, mask_row, own_hbm, *refs):
    codes, half, rows, blocks, length, width, factor, chunks = shape
    arrived, refs = refs[: len(chunks)], refs[len(chunks) :]
    pieces, refs = refs[: len(codes)], refs[len(codes) :]
    outs, refs = refs[:7], refs[7:]
    (q_out, k_out, v_out, att_out, lse_out, weight, other) = kept = refs[:7]
    (own, held, h_own, h_oth, allowed, sem, sem_out, sem_in) = refs[7:]
    begin(own_hbm, own, sem_in.at[0])
    load_pieces(pos, pieces, codes, half, (0, blocks.wide), row_target(held, blocks, rows), sem)
    starts = [sum(chunks[:i]) for i in range(len(chunks))]
    places_in = [other.at[pl.ds(start, size), :] for start, size in zip(starts, chunks)]
    for i, (ref, place) in enumerate(zip(arrived, places_in)):
        begin(ref, place, sem_in.at[i + 1])
    finish(own_hbm, own, sem_in.at[0])
    for i, (ref, place) in enumerate(zip(arrived, places_in)):
        finish(ref, place, sem_in.at[i + 1])
    begin(other, outs[6], sem_out.at[6])
    for i in range(length // CHUNK):
        part = pl.ds(i * CHUNK, CHUNK)
        unit, _ = normed(own[part, :].astype(FULL))
        h_own[part, :] = (unit * gains[0:1, :]).astype(LOW)
        unit, _ = normed(other[part, :].astype(FULL))
        h_oth[part, :] = (unit * gains[1:2, :]).astype(LOW)
        row = lax.broadcasted_iota(jnp.int32, (CHUNK, length), 0) + i * CHUNK
        col = lax.broadcasted_iota(jnp.int32, (CHUNK, length), 1)
        ok = (page_col[part, :] == page_row[...]) & ((mask_row[...] == 1) | (row == col))
        allowed[part, :] = jnp.where(ok, 1.0, 0.0)
    wait_whole(held, sem)
    merge_tiles(held, weight, blocks)
    begin(weight, outs[5], sem_out.at[5])
    lse_out[...] = jnp.zeros_like(lse_out)

    q_out[...] = (matmul(h_own[...], weight[:, :width]).astype(LOW) * factor).astype(LOW)
    k_out[...] = matmul(h_oth[...], weight[:, width : 2 * width]).astype(LOW)
    v_out[...] = matmul(h_oth[...], weight[:, 2 * width :]).astype(LOW)
    for i in range(3):
        begin(kept[i], outs[i], sem_out.at[i])
    size = width // HEADS
    per = LANES // size

    @pl.loop(0, width // LANES)
    def _(pair):
        cols = pl.ds(pl.multiple_of(pair * LANES, LANES), LANES)
        keys, values, queries = k_out[:, cols], v_out[:, cols], q_out[:, cols]
        lane = lax.broadcasted_iota(jnp.int32, queries.shape, 1)
        result, sums = None, lse_out[...]
        for sub in range(per):
            inside = lane // size == sub
            scores = matmul_nt(jnp.where(inside, queries, jnp.zeros_like(queries)), keys)
            scores = jnp.where(allowed[...] > 0.5, scores, NEG)
            top = jnp.max(scores, axis=-1, keepdims=True)
            exps = jnp.exp(scores - top)
            total = jnp.sum(exps, axis=-1, keepdims=True)
            out = matmul(exps.astype(LOW), values) * (1.0 / total)
            result = out if result is None else jnp.where(inside, out, result)
            sums = jnp.where(lane == pair * per + sub, top + jnp.log(total), sums)
        lse_out[...] = sums
        att_out[:, cols] = result.astype(LOW)

    for i in (3, 4):
        begin(kept[i], outs[i], sem_out.at[i])
    for i, ref in enumerate(kept):
        finish(ref, outs[i], sem_out.at[i])


def feed_kernel(shape, pos, coef, gain, page_col, att_hbm, own_hbm, cot_hbm, cotj_hbm, arrived_hbm, *refs):
    (codes, counts, sums_b, sums_c, half, rows, down_rows, ups, outs, downs, length, width, hidden, block) = shape
    pieces, refs = refs[: len(codes)], refs[len(codes) :]
    out_ref, dmid_ref, datt_ref, away_ref, dgain_ref = refs[:5]
    up_targets, down_targets = refs[5:7], refs[7:9]
    (w_up, o_held, w_out, d_held, w_down, g_up, g_out, g_down, att, own, cot, cotj_own, cotj_oth, mid, h2, h2_t, dffn, dffn_t,
     att_t, acts, dpre, acc, dacc, dbranch, sem_up, sem_out, sem_down, sem_gup, sem_gdown, sems) = refs[9:]
    begin(att_hbm, att, sems.at[0])
    last = counts
    load_pieces(pos, pieces[:last], codes[:last], half, (ups.wide, outs.wide), row_target(o_held, outs, rows), sem_out)
    begin(own_hbm, own, sems.at[1])
    begin(cot_hbm, cot, sems.at[2])
    begin(cotj_hbm, cotj_own, sems.at[3])
    begin(arrived_hbm, cotj_oth, sems.at[4])
    load_pieces(pos, pieces[:last], codes[:last], half, (0, ups.wide), row_target(w_up, ups, rows), sem_up)
    folds = down_rows // rows
    load_folded(pos, pieces[last:], codes[last:], half, rows, downs, 0, folds, d_held, sem_down)
    half_rows = length // 2
    parts = length // CHUNK

    def valid_at(part):
        return jnp.where(page_col[part, :] >= 0, 1.0, 0.0)

    finish(att_hbm, att, sems.at[0])
    wait_whole(o_held, sem_out)
    merge_tiles(o_held, w_out, outs)
    mid[...] = matmul(att[...], w_out[...])
    att_t[...] = att[...].T
    finish(own_hbm, own, sems.at[1])
    for i in range(parts):
        part = pl.ds(i * CHUNK, CHUNK)
        middle = own[part, :].astype(FULL) + valid_at(part) * mid[part, :]
        mid[part, :] = middle
        unit, _ = normed(middle)
        h2[part, :] = (unit * gain[...]).astype(LOW)
    finish(cot_hbm, cot, sems.at[2])
    finish(cotj_hbm, cotj_own, sems.at[3])
    finish(arrived_hbm, cotj_oth, sems.at[4])
    for which, ref in ((pos[2], cotj_own), (1 - pos[2], cotj_oth)):
        for i in range(half_rows // CHUNK):
            part = pl.ds(pl.multiple_of(which * half_rows + i * CHUNK, CHUNK), CHUNK)
            grad = cot[part, :] + coef[...] * ref[pl.ds(i * CHUNK, CHUNK), :].astype(FULL)
            cot[part, :] = grad
            dffn[part, :] = (grad * valid_at(part)).astype(LOW)
    dffn_t[...] = dffn[...].T
    h2_t[...] = h2[...].T
    acc[...] = jnp.zeros_like(acc)
    dacc[...] = jnp.zeros_like(dacc)
    wait_whole(w_up, sem_up)
    wait_whole(d_held, sem_down)
    if not downs.aligned:
        merge_tiles(d_held, w_down, downs)
    down = d_held if downs.aligned else w_down
    c0, c1 = 0.7978845608028654, 0.044715

    @pl.loop(0, hidden // block)
    def _(f):
        cols = pl.ds(pl.multiple_of(f * block, LANES), block)
        pre = matmul(h2[...], w_up[:, cols])
        dact = matmul(dffn[...], down[:, cols])
        square = pre * pre
        flat = jnp.tanh(c0 * (pre + c1 * square * pre))
        cdf = 0.5 * (1.0 + flat)
        slope = cdf + pre * (0.5 * (1.0 - flat * flat)) * (c0 * (1.0 + 3.0 * c1 * square))
        acts[...] = (pre * cdf).astype(LOW)
        dpre[...] = (slope * dact).astype(LOW)
        acc[...] += matmul_nt(acts[...], down[:, cols])
        dacc[...] += matmul_nt(dpre[...], w_up[:, cols])
        g_down[:, cols] = matmul(dffn_t[...], acts[...]).astype(LOW)
        g_up[:, cols] = matmul(h2_t[...], dpre[...]).astype(LOW)

    if downs.room > downs.total:
        g_down[:, downs.total :] = jnp.zeros((width, downs.room - downs.total), LOW)
    store_pieces(
        pos,
        lambda doc, inner: g_down.at[
            pl.ds(pl.multiple_of(doc * down_rows, down_rows), down_rows),
            pl.ds(downs.start_dynamic(inner), downs.wide),
        ],
        sums_c, half, down_targets, (0, downs.wide), sem_gdown,
    )
    store_pieces(
        pos,
        lambda doc, inner: g_up.at[
            pl.ds(pl.multiple_of(inner * rows, rows), rows),
            pl.ds(ups.start_dynamic(doc), ups.wide),
        ],
        sums_b, half, up_targets, (0, ups.wide), sem_gup,
    )
    dgain_ref[...] = jnp.zeros_like(dgain_ref)
    for i in range(parts):
        part = pl.ds(i * CHUNK, CHUNK)
        valid = valid_at(part)
        middle = mid[part, :]
        acc[part, :] = middle + valid * acc[part, :]
        unit, scale = normed(middle)
        grad = dacc[part, :]
        dgain_ref[0:1, :] += jnp.sum(grad * unit, axis=0, keepdims=True)
        dmid = cot[part, :] + norm_back(grad, unit, scale, gain[...])
        dacc[part, :] = dmid
        dbranch[part, :] = (dmid * valid).astype(LOW)
    begin(acc, out_ref, sems.at[0])
    begin(dacc, dmid_ref, sems.at[1])
    h2[...] = matmul_nt(dbranch[...], w_out[...]).astype(LOW)
    begin(h2, datt_ref, sems.at[2])
    g_out[:, : outs.total] = matmul(att_t[...], dbranch[...]).astype(LOW)
    if outs.room > outs.total:
        g_out[:, outs.total :] = jnp.zeros((width, outs.room - outs.total), LOW)
    store_pieces(
        pos,
        lambda doc, inner: g_out.at[
            pl.ds(pl.multiple_of(inner * rows, rows), rows),
            pl.ds(outs.start_dynamic(doc), outs.wide),
        ],
        sums_b, half, up_targets, (ups.wide, outs.wide), sem_gup,
    )
    for i in range(half_rows // CHUNK):
        part = pl.ds(pl.multiple_of((1 - pos[2]) * half_rows + i * CHUNK, CHUNK), CHUNK)
        away_ref[pl.ds(i * CHUNK, CHUNK), :] = acc[part, :].astype(LOW)
    for target in down_targets:
        wait_whole(target, sem_gdown)
    for target in up_targets:
        wait_whole(target, sem_gup)
    finish(acc, out_ref, sems.at[0])
    finish(dacc, dmid_ref, sems.at[1])
    finish(h2, datt_ref, sems.at[2])


def scores_back_kernel(shape, pairs, page_col, page_row, mask_row, q_hbm, k_hbm, v_hbm, att_hbm, datt_hbm, lse_hbm, *refs):
    length, width, factor = shape
    outs, refs = refs[:3], refs[3:]
    (q_ref, k_ref, v_ref, att, datt, lse, dq, dk, dv, allowed, lse_t, dots_t, sems) = refs
    size = width // HEADS
    per = LANES // size
    cols_here = pl.ds(pairs[0] * LANES, (pairs[1] - pairs[0]) * LANES)
    loads = [(source.at[:, cols_here], target) for source, target in
             ((datt_hbm, datt), (att_hbm, att), (q_hbm, q_ref), (k_hbm, k_ref), (v_hbm, v_ref))]
    loads.append((lse_hbm, lse))
    for i, (source, target) in enumerate(loads):
        begin(source, target, sems.at[i])
    mask = jnp.broadcast_to(mask_row[...].astype(FULL), (LANES, length)).T[:, 0:1]
    row = lax.broadcasted_iota(jnp.int32, (length, length), 0)
    col = lax.broadcasted_iota(jnp.int32, (length, length), 1)
    ok = (page_col[...] == page_row[...]) & ((mask == 1.0) | (row == col))
    allowed[...] = jnp.where(ok, 1.0, 0.0)
    here_width = cols_here.size
    head = lax.broadcasted_iota(jnp.int32, (LANES, here_width), 0)
    lane = lax.broadcasted_iota(jnp.int32, (LANES, here_width), 1)
    chosen = jnp.where(lane // size == head, 1.0, 0.0)
    for i, (source, target) in enumerate(loads):
        finish(source, target, sems.at[i])
    dots_t[...] = lax.dot_general(
        chosen, att[...].astype(FULL) * datt[...].astype(FULL), (((1,), (1,)), ((), ())),
        preferred_element_type=FULL, precision=lax.Precision.HIGHEST,
    )
    lse_t[...] = lse[...].T

    @pl.loop(0, pairs[1] - pairs[0])
    def _(pair):
        cols = pl.ds(pl.multiple_of(pair * LANES, LANES), LANES)
        queries, grads = q_ref[:, cols], datt[:, cols]
        keys, values = k_ref[:, cols], v_ref[:, cols]
        lane = lax.broadcasted_iota(jnp.int32, (length, LANES), 1)
        zero = jnp.zeros_like(queries)
        trio = None
        for sub in range(per):
            inside = lane // size == sub
            lse_row = lse_t[pl.ds((pair + pairs[0]) * per + sub, 1), :]
            dot_row = dots_t[pl.ds(pair * per + sub, 1), :]
            scores = matmul_nt(keys, jnp.where(inside, queries, zero))
            scores = jnp.where(allowed[...] > 0.5, scores, NEG)
            probs = jnp.exp(scores - lse_row)
            dprob = matmul_nt(values, jnp.where(inside, grads, zero))
            low = (probs * (dprob - dot_row)).astype(LOW)
            three = (matmul_tn(low, keys), matmul(low, queries), matmul(probs.astype(LOW), grads))
            trio = three if trio is None else [jnp.where(inside, new, old) for new, old in zip(three, trio)]
        dq[:, cols] = (trio[0] * factor).astype(LOW)
        dk[:, cols] = trio[1].astype(LOW)
        dv[:, cols] = trio[2].astype(LOW)

    for i, (source, target) in enumerate(zip((dq, dk, dv), outs)):
        begin(source, target, sems.at[i])
    for i, (source, target) in enumerate(zip((dq, dk, dv), outs)):
        finish(source, target, sems.at[i])


def project_back_kernel(shape, pos, gains, own_hbm, other_hbm, weight_hbm, *refs):
    (sums, half, rows, blocks, length, width, runs) = shape
    given, refs = refs[: 3 * len(runs)], refs[3 * len(runs) :]
    own_out, oth_ref, dgain_ref = refs[:3]
    targets, refs = refs[3:5], refs[5:]
    h_t, flat, own_ref, grad, own, other, weight, sem, sems = refs[:9]
    copies = refs[9:]
    grads = [copies[3 * i : 3 * i + 3] for i in range(len(runs))]
    parts = length // CHUNK
    loads = [(own_hbm, own), (other_hbm, other), *zip(given, copies), (weight_hbm, weight)]
    for i, (source, target) in enumerate(loads):
        begin(source, target, sems.at[i])

    def take(i):
        finish(*loads[i], sems.at[i])

    for which, source in ((0, own), (1, other)):
        take(which)
        for i in range(parts):
            part = pl.ds(i * CHUNK, CHUNK)
            unit, _ = normed(source[part, :].astype(FULL))
            flat[part, :] = unit * gains[which : which + 1, :]
        h_t[which] = flat[...].astype(LOW).T
    for i in range(2, len(loads) - 1):
        take(i)
    for (low, high), trio in zip(runs, grads):
        for block, (which, ref) in enumerate(zip((0, 1, 1), trio)):
            grad[:, block * width + low : block * width + high] = matmul(h_t[which], ref[...]).astype(LOW)
    if blocks.room > blocks.total:
        grad[:, blocks.total :] = jnp.zeros((width, blocks.room - blocks.total), LOW)
    store_pieces(
        pos,
        lambda doc, inner: grad.at[
            pl.ds(pl.multiple_of(inner * rows, rows), rows),
            pl.ds(blocks.start_dynamic(doc), blocks.wide),
        ],
        sums, half, targets, (0, blocks.wide), sem,
    )
    dgain_ref[...] = jnp.zeros_like(dgain_ref)
    take(len(loads) - 1)
    own_ref[...] = sum(
        matmul_nt(trio[0][...], weight[:, low:high]) for (low, high), trio in zip(runs, grads)
    )
    begin(own_ref, own_out, sems.at[0])
    flat[...] = sum(
        matmul_nt(trio[block][...], weight[:, block * width + low : block * width + high])
        for (low, high), trio in zip(runs, grads)
        for block in (1, 2)
    )
    for i in range(parts):
        part = pl.ds(i * CHUNK, CHUNK)
        unit, _ = normed(own[part, :].astype(FULL))
        dgain_ref[0:1, :] += jnp.sum(own_ref[part, :] * unit, axis=0, keepdims=True)
        unit, _ = normed(other[part, :].astype(FULL))
        value = flat[part, :]
        oth_ref[part, :] = value.astype(LOW)
        dgain_ref[1:2, :] += jnp.sum(value * unit, axis=0, keepdims=True)
    finish(own_ref, own_out, sems.at[0])
    for target in targets:
        wait_whole(target, sem)


def tail_kernel(length, own, gain, mine, theirs, dmid, out_ref):
    for i in range(length // CHUNK):
        part = pl.ds(i * CHUNK, CHUNK)
        unit, scale = normed(own[part, :].astype(FULL))
        grad = mine[part, :] + theirs[part, :].astype(FULL)
        out_ref[part, :] = dmid[part, :] + norm_back(grad, unit, scale, gain[...])


VMEM = pl.BlockSpec(memory_space=pltpu.VMEM)
HBM = pl.BlockSpec(memory_space=pltpu.HBM)
SMEM = pl.BlockSpec(memory_space=pltpu.SMEM)


LITTLE = pl.CostEstimate(flops=1_000, bytes_accessed=1_000, transcendentals=0)


def params(mebibytes):
    return pltpu.CompilerParams(vmem_limit_bytes=mebibytes * 1024 * 1024)


def adam_update(weight, first, second, grad, rate, decay):
    first_new = 0.9 * first + 0.1 * grad
    second_new = 0.999 * second + 0.001 * grad * grad
    first_hat = first_new / (1.0 - 0.9**STEP)
    second_hat = second_new / (1.0 - 0.999**STEP)
    weight_new = weight - rate * (first_hat / (jnp.sqrt(second_hat) + 1e-08) + decay * weight)
    return (weight_new, first_new, second_new)


def shards(
    rows, cot_stream, cot_joined, page, key_mask,
    w_qkv, m_qkv, v_qkv, w_out, m_out, v_out, w_up, m_up, v_up, w_down, m_down, v_down,
    gains, m_gains, v_gains,
):
    docs, wide = lax.axis_size("docs"), lax.axis_size("wide")
    half = wide // 2
    doc, place = lax.axis_index("docs"), lax.axis_index("wide")
    stream = place // half
    is_text = stream == 0
    pos = jnp.stack((doc, place % half, stream)).astype(jnp.int32)
    length, width = rows.shape
    half_rows = length // 2
    factor = float(width // HEADS) ** (-0.5)
    piece_rows = w_qkv.shape[1]
    hidden = w_up.shape[2] * docs
    qkvs, outs, ups = Blocks(docs, w_qkv.shape[2]), Blocks(docs, w_out.shape[2]), Blocks(docs, w_up.shape[2])
    downs = Blocks(wide, w_down.shape[1])
    down_rows = w_down.shape[2]

    core = [("wide", 1)]
    along_x = [("docs", 1)]
    along_y = [("docs", 1 << b) for b in range(1, docs.bit_length() - 1)]
    along_z = [("wide", 1 << b) for b in range(1, half.bit_length() - 1)]
    across = ("wide", half)

    def swap(value):
        return flip(value, *across)

    column = doc * w_qkv.shape[2] + lax.iota(jnp.int32, w_qkv.shape[2])
    is_query = (column < width)[None, None, :]
    pair_qkv = jnp.where(is_query, w_qkv, w_qkv[::-1]).astype(LOW)

    def own_first(pair):
        return jnp.where(is_text, pair, pair[::-1])

    unit_a = qkvs.pad(own_first(pair_qkv), doc)
    unit_b = jnp.concatenate(
        (ups.pad(own_first(w_up.astype(LOW)), doc), outs.pad(own_first(w_out.astype(LOW)), doc)), axis=-1
    )
    unit_c = downs.pad(jnp.swapaxes(own_first(w_down.astype(LOW)), 1, 2), place)
    folds = down_rows // piece_rows

    def folded(unit):
        return jnp.concatenate([unit[i * piece_rows : (i + 1) * piece_rows] for i in range(folds)], axis=-1)

    unit_a_oth = swap(unit_a[1])
    unit_b_oth = swap(after(unit_b[1], unit_a_oth)) if FIRST_A else swap(unit_b[1])
    if downs.aligned:
        unit_c_oth = swap(after(unit_c[1], unit_a_oth))
    else:
        raw = jnp.swapaxes(own_first(w_down.astype(LOW)), 1, 2)
        unit_c_oth = downs.pad(swap(raw[1]), (place + half) % wide)
    zxy, zyx = along_z + along_x + along_y, along_z + along_y + along_x
    a_own, a_oth = Doubling(unit_a[0], 0, zxy), Doubling(unit_a_oth, 1, zyx)
    b_own = Doubling(unit_b[0], 0, along_y + along_x + along_z)
    c_own = Doubling(folded(unit_c[0]), 0, along_x + along_z + along_y)
    b_oth, c_oth = Doubling(unit_b_oth, 1, zxy), Doubling(folded(unit_c_oth), 1, zyx)
    steps_y, steps_x = len(along_y), len(along_x)
    chunks, begin = [], 0
    for size in [length * part // sum(ROW_PARTS) for part in ROW_PARTS]:
        some = rows[begin : begin + size]
        chunks.append(swap(after(some, chunks[-1] if chunks else unit_a_oth)))
        begin += size
    for _ in range(steps_y):
        b_own.send()
    for _ in range(steps_x):
        c_own.send()
    for _ in range(steps_x):
        b_own.send(unit_a_oth)
    for _ in along_z:
        c_own.send(unit_a_oth)
    a_own.send_all()
    a_oth.send_all()
    first = (a_oth.arrays[len(along_z) + steps_y], a_own.arrays[len(along_z) + steps_x])
    rest = (a_oth.arrays[-1], a_own.arrays[-1])
    for one in (b_oth, c_oth):
        for _ in along_z:
            one.send(*first)
    met = b_oth.last + c_oth.last
    for one in (b_own, c_own):
        while one.step < len(one.order):
            one.send(*met)
    for one, steps in ((b_oth, steps_x), (c_oth, steps_y)):
        for _ in range(steps):
            one.send(*rest, chunks[1])
    for one in (b_oth, c_oth):
        while one.step < len(one.order):
            one.send(chunks[-1])
    pieces_a, codes_a = [], []
    for one in (a_own, a_oth):
        for value, known in one.split_newest():
            one.add(value, known, *core[0])
        pieces_a += one.arrays
        codes_a += one.slotted()
    waiting, passed = [], []
    for one in (b_own, b_oth, c_own, c_oth):
        early, late = one.split_newest()
        passed.append(one.add(after(early[0], chunks[-1]), early[1], *core[0]))
        waiting.append((one, *late))
    other_joined = swap(after(cot_joined.astype(LOW), chunks[-1], *passed))

    page_col, page_row = page[:, None], page[None, :]
    mask_row = key_mask[None, :]
    gain_own = lax.dynamic_index_in_dim(gains, stream, 0, keepdims=True)
    gain_oth = lax.dynamic_index_in_dim(gains, 1 - stream, 0, keepdims=True)
    gain_one = jnp.concatenate((gain_own, gain_oth), axis=0)
    gain_two = lax.dynamic_index_in_dim(gains, 2 + stream, 0, keepdims=True)
    mix = jax.nn.sigmoid(gains[4])[None, :]
    coef = jnp.where(is_text, mix, 1.0 - mix)

    low_rows = jax.ShapeDtypeStruct((length, width), LOW)
    full_rows = jax.ShapeDtypeStruct((length, width), FULL)

    sizes = tuple(chunk.shape[0] for chunk in chunks)
    shape = (codes_a, half, piece_rows, qkvs, length, width, factor, sizes)
    made = (low_rows, low_rows, low_rows, low_rows, jax.ShapeDtypeStruct((length, LANES), FULL),
            jax.ShapeDtypeStruct((width, 3 * width), LOW), low_rows)
    queries, keys, values, attended, lse, weight_qkv, other_rows = pl.pallas_call(
        functools.partial(project_kernel, shape),
        out_shape=made,
        in_specs=[SMEM] + [VMEM] * 4 + [HBM] * (1 + len(chunks) + len(pieces_a)),
        out_specs=(HBM,) * 7,
        scratch_shapes=[pltpu.VMEM(one.shape, one.dtype) for one in made] + [
            pltpu.VMEM((length, width), LOW),
            pltpu.VMEM((docs, width, qkvs.wide), LOW),
            pltpu.VMEM((length, width), LOW),
            pltpu.VMEM((length, width), LOW),
            pltpu.VMEM((length, length), FULL),
            pltpu.SemaphoreType.DMA,
            pltpu.SemaphoreType.DMA((7,)),
            pltpu.SemaphoreType.DMA((1 + len(chunks),)),
        ],
        compiler_params=params(60),
        cost_estimate=LITTLE,
        name="project_attend",
    )(pos, gain_one, page_col, page_row, mask_row, rows, *chunks, *pieces_a)

    here = [value for _, value, _ in waiting]
    for one, value, known in waiting:
        one.add(after(value, lse, other_joined, *here), known, *core[0])
    streams = (b_own, b_oth, c_own, c_oth)
    pieces_b = sum((one.arrays for one in streams), [])
    codes_b = sum((one.slotted() for one in streams), [])
    counts = len(b_own.arrays) + len(b_oth.arrays)
    xy, yx = along_x + along_y, along_y + along_x
    steps_b = [core * 2, *zip(xy, yx), *((step, step) for step in along_z)]
    steps_c = [core * 2, *((step, step) for step in along_z + xy)]
    sums_of = [tuple(sum_codes([pair[slot] for pair in steps]) for slot in (0, 1)) for steps in (steps_b, steps_c)]
    sent_count = len(sums_of[0][0])
    block = 6 * LANES
    shape = (codes_b, counts, *sums_of, half, piece_rows, down_rows, ups, outs, downs, length, width, hidden, block)
    shape_b = jax.ShapeDtypeStruct((sent_count, piece_rows, ups.wide + outs.wide), LOW)
    shape_c = jax.ShapeDtypeStruct((sent_count, down_rows, downs.wide), LOW)
    (stream_out, middle_grad, attended_grad, away, dgain_two, kept_b, sent_b, kept_c, sent_c) = pl.pallas_call(
        functools.partial(feed_kernel, shape),
        out_shape=(full_rows, full_rows, low_rows, jax.ShapeDtypeStruct((half_rows, width), LOW),
                   jax.ShapeDtypeStruct((8, width), FULL), shape_b, shape_b, shape_c, shape_c),
        in_specs=[SMEM] + [VMEM] * 3 + [HBM] * (5 + len(pieces_b)),
        out_specs=(HBM,) * 3 + (VMEM,) * 2 + (HBM,) * 4,
        scratch_shapes=[
            pltpu.VMEM((width, hidden), LOW),
            pltpu.VMEM(held_shape(outs, width), LOW),
            pltpu.VMEM((width, width), LOW),
            pltpu.VMEM(held_shape(downs, width), LOW),
            pltpu.VMEM((8, LANES) if downs.aligned else (width, hidden), LOW),
            pltpu.VMEM((width, hidden), LOW),
            pltpu.VMEM((width, outs.room), LOW),
            pltpu.VMEM((width, downs.room), LOW),
            pltpu.VMEM((length, width), LOW),
            pltpu.VMEM((length, width), LOW),
            pltpu.VMEM((length, width), FULL),
            pltpu.VMEM((half_rows, width), FULL),
            pltpu.VMEM((half_rows, width), LOW),
            pltpu.VMEM((length, width), FULL),
            pltpu.VMEM((length, width), LOW),
            pltpu.VMEM((width, length), LOW),
            pltpu.VMEM((length, width), LOW),
            pltpu.VMEM((width, length), LOW),
            pltpu.VMEM((width, length), LOW),
            pltpu.VMEM((length, block), LOW),
            pltpu.VMEM((length, block), LOW),
            pltpu.VMEM((length, width), FULL),
            pltpu.VMEM((length, width), FULL),
            pltpu.VMEM((length, width), LOW),
        ] + [pltpu.SemaphoreType.DMA] * 5 + [pltpu.SemaphoreType.DMA((5,))],
        compiler_params=params(60),
        cost_estimate=LITTLE,
        name="feed_forward_back",
    )(pos, coef, gain_two, page_col, attended, rows, cot_stream, cot_joined, other_joined, *pieces_b)

    def attend_back(pairs, *operands):
        low_cols = jax.ShapeDtypeStruct((length, (pairs[1] - pairs[0]) * LANES), LOW)
        piece = pltpu.VMEM(low_cols.shape, LOW)
        return pl.pallas_call(
            functools.partial(scores_back_kernel, (length, width, factor), pairs),
            out_shape=(low_cols,) * 3,
            in_specs=[VMEM] * 3 + [HBM] * 6,
            out_specs=(HBM,) * 3,
            scratch_shapes=[piece] * 5 + [pltpu.VMEM((length, LANES), FULL)] + [piece] * 3 + [
                pltpu.VMEM((length, length), FULL),
                pltpu.VMEM((LANES, length), FULL),
                pltpu.VMEM((LANES, length), FULL),
                pltpu.SemaphoreType.DMA((6,)),
            ],
            compiler_params=params(60),
            cost_estimate=LITTLE,
            name="attend_back",
        )(page_col, page_row, mask_row, *operands)

    sums_b, sums_c = Halving(kept_b, sent_b, steps_b), Halving(kept_c, sent_c, steps_c)
    sums_b.send()
    sums_c.send()
    partner_rows = swap(away)
    pair_count = width // LANES
    cuts = (0, pair_count * 2 // 3, pair_count)
    grads_one = attend_back(cuts[:2], queries, keys, values, attended, attended_grad, lse)
    met = (*sums_b.last, *sums_c.last, partner_rows)
    second = after(queries, grads_one[0], *met)
    sums_b.hold(grads_one[0], *met)
    sums_c.hold(grads_one[0], *met)
    sums_b.send()
    sums_c.send()
    grads_two = attend_back(cuts[1:], second, keys, values, attended, attended_grad, lse)

    runs = tuple((low * LANES, high * LANES) for low, high in zip(cuts[:-1], cuts[1:]))
    shape = (sums_of[0], half, piece_rows, qkvs, length, width, runs)
    shape_a = jax.ShapeDtypeStruct((sent_count, piece_rows, qkvs.wide), LOW)
    own_part, away_part, dgain_one, kept_a, sent_a = pl.pallas_call(
        functools.partial(project_back_kernel, shape),
        out_shape=(full_rows, low_rows, jax.ShapeDtypeStruct((8, width), FULL)) + (shape_a,) * 2,
        in_specs=[SMEM, VMEM] + [HBM] * (3 + 3 * len(runs)),
        out_specs=(HBM,) + (VMEM,) * 2 + (HBM,) * 2,
        scratch_shapes=[
            pltpu.VMEM((2, width, length), LOW),
            pltpu.VMEM((length, width), FULL),
            pltpu.VMEM((length, width), FULL),
            pltpu.VMEM((width, qkvs.room), LOW),
            pltpu.VMEM((length, width), LOW),
            pltpu.VMEM((length, width), LOW),
            pltpu.VMEM((width, 3 * width), LOW),
            pltpu.SemaphoreType.DMA,
            pltpu.SemaphoreType.DMA((3 + 3 * len(runs),)),
        ] + [pltpu.VMEM((length, high - low), LOW) for low, high in runs for _ in range(3)],
        compiler_params=params(60),
        cost_estimate=LITTLE,
        name="project_back",
    )(pos, gain_one, rows, other_rows, weight_qkv, *grads_one, *grads_two)

    own_rows = lax.dynamic_slice_in_dim(stream_out, stream * half_rows, half_rows, 0)
    partner_rows = partner_rows.astype(FULL)
    text_rows = jnp.where(is_text, own_rows, partner_rows)
    image_rows = jnp.where(is_text, partner_rows, own_rows)
    joined_rows = mix * text_rows + (1.0 - mix) * image_rows
    gate_grad = jnp.sum(cot_joined * (text_rows - image_rows), axis=0, keepdims=True) * mix * (1.0 - mix)

    slot_index = lax.iota(jnp.int32, 5)[:, None]
    small = (
        jnp.where(slot_index == stream, dgain_one[0:1], 0.0)
        + jnp.where(slot_index == 1 - stream, dgain_one[1:2], 0.0)
        + jnp.where(slot_index == 2 + stream, dgain_two[0:1], 0.0)
        + jnp.where(slot_index == 4, gate_grad, 0.0)
    )
    sums_a = Halving(kept_a, sent_a, steps_b)
    sums_a.hold(*sums_b.last, *sums_c.last)
    sums_a.send()
    sums_a.rider = small + flip(small, *core[0])
    back_part = swap(away_part)
    for one in (sums_b, sums_c):
        one.hold(*[value for value in sums_a.outgoing if value is not None])
    for one in (sums_a, sums_b, sums_c):
        while one.left():
            one.send()

    grad_rows = pl.pallas_call(
        functools.partial(tail_kernel, length),
        out_shape=full_rows,
        in_specs=[VMEM] * 5,
        out_specs=VMEM,
        compiler_params=params(10),
        name="norm_tail",
    )(rows, gain_own, own_part, back_part, after(middle_grad, *sums_a.last))

    def late(pair):
        return tuple(after(value, *sums_a.last) for value in pair)

    total_a, total_b, total_c = sums_a.total(), sums_b.total(), sums_c.total()

    def both(total):
        return total[0], swap(total[1].astype(LOW))

    def placed(mine, theirs):
        theirs = theirs.astype(FULL)
        return jnp.where(is_text, jnp.stack((mine, theirs)), jnp.stack((theirs, mine)))

    mine_b, theirs_b = late(both(total_b))
    grad_b = placed(mine_b, theirs_b)
    grad_up = ups.cut(grad_b[..., : ups.wide], doc)
    grad_out = outs.cut(grad_b[..., ups.wide :], doc)
    if downs.aligned:
        mine_c, theirs_c = late(both(total_c))
    else:
        mine_c = downs.cut(total_c[0], place)
        theirs_c = swap(downs.cut(total_c[1], (place + half) % wide).astype(LOW))
    grad_down = jnp.swapaxes(placed(mine_c, theirs_c), 1, 2)
    last = total_a[1].astype(LOW)[None]
    last, rider = rider_of(swap(with_rider(last, sums_a.rider)), sums_a.rider.shape, last.shape)
    gains_grad = kept_rider(sums_a.rider) + rider
    mine_a, theirs_a = total_a[0], last[0]
    mine_a, theirs_a = qkvs.cut(mine_a, doc), qkvs.cut(theirs_a.astype(FULL), doc)
    query_here = is_query[0]
    grad_qkv = placed(
        jnp.where(query_here, mine_a, theirs_a), jnp.where(query_here, theirs_a, mine_a)
    )

    qkv_new = adam_update(w_qkv, m_qkv, v_qkv, grad_qkv, 0.12, 0.01)
    out_new = adam_update(w_out, m_out, v_out, grad_out, 0.5, 0.01)
    up_new = adam_update(w_up, m_up, v_up, grad_up, 0.12, 0.01)
    down_new = adam_update(w_down, m_down, v_down, grad_down, 0.06, 0.01)
    gains_new = adam_update(gains, m_gains, v_gains, gains_grad, 0.8, 0.0)
    return (stream_out, joined_rows, grad_rows, *qkv_new, *out_new, *up_new, *down_new, *gains_new)


def solution(mesh):
    by_rows = P(("docs", "wide"), None)
    by_row = P(("docs", "wide"))
    weight = P(None, "wide", "docs")
    return jax.shard_map(
        shards,
        mesh=mesh,
        in_specs=(by_rows,) * 3 + (by_row,) * 2 + (weight,) * 12 + (P(),) * 3,
        out_specs=(by_rows,) * 3 + (weight,) * 12 + (P(),) * 3,
        check_vma=False,
    )
```

```python
import functools
import math

import jax
import jax.numpy as jnp
from jax import lax
from jax.experimental import pallas as pl
from jax.experimental.pallas import tpu as pltpu
from jax.sharding import PartitionSpec as P

HEADS = 12
STEP = 10
LANES = 128
CHUNK = 128
ROW_PARTS = (5, 6, 5)
FIRST_A = False
NEG = -1000000000.0
LOW = jnp.bfloat16
FULL = jnp.float32


def flip(value, axis, mask):
    count = lax.axis_size(axis)
    return lax.ppermute(value, axis, [(i, i ^ mask) for i in range(count)])


def flipped(codes, axis, mask):
    d_mask = mask if axis == "docs" else 0
    w_mask = mask if axis == "wide" else 0
    return [(d ^ d_mask, w ^ w_mask) for d, w in codes]


def after(value, *others):
    return lax.optimization_barrier((value, *others))[0]


class Doubling:
    def __init__(self, unit, slot, order):
        self.slot, self.order, self.step = slot, order, 0
        self.arrays, self.codes = [unit[None]], [[(0, 0)]]
        self.last = ()

    def held(self):
        held = self.arrays[0] if len(self.arrays) == 1 else jnp.concatenate(self.arrays, axis=0)
        return held, [code for group in self.codes for code in group]

    def send(self, *others):
        held, known = self.held()
        if others:
            held = after(held, *others)
        axis, mask = self.order[self.step]
        self.arrays.append(flip(held, axis, mask))
        self.codes.append(flipped(known, axis, mask))
        self.step, self.last = self.step + 1, (self.arrays[-1],)

    def send_all(self):
        while self.step < len(self.order):
            self.send()

    def split_newest(self):
        newest, newest_known = self.arrays.pop(), self.codes.pop()
        held, known = self.held()
        self.arrays.append(newest)
        self.codes.append(newest_known)
        return (held, known), (newest, newest_known)

    def add(self, value, known, axis, mask):
        self.arrays.append(flip(value, axis, mask))
        self.codes.append(flipped(known, axis, mask))
        return self.arrays[-1]

    def slotted(self):
        return [(self.slot, group) for group in self.codes]


def sum_codes(order):
    codes = [(0, 0)]
    for axis, mask in reversed(order):
        codes = codes + flipped(codes, axis, mask)
    return codes


def halves_of(value):
    high = lax.reduce_precision(value, 8, 7)
    return high, lax.reduce_precision(value - high, 8, 7)


def rider_rows(value, lanes):
    rows, width = value.shape
    runs = [value[:, i : i + lanes] for i in range(0, width, lanes)]
    runs = [jnp.pad(run, ((0, -rows % 8), (0, lanes - run.shape[1]))) for run in runs]
    return jnp.concatenate(runs, axis=0)


def rider_value(laid, shape):
    rows, width = shape
    high = rows + -rows % 8
    runs = [laid[i * high : i * high + rows] for i in range(laid.shape[0] // high)]
    return jnp.concatenate(runs, axis=1)[:, :width]


def with_rider(value, rider):
    lanes = value.shape[-1]
    tail = [part.astype(LOW) for part in halves_of(rider)]
    return jnp.concatenate((value.reshape(-1, lanes), *tail), axis=0)


def rider_of(message, shape, value_shape):
    count, rows = math.prod(value_shape[:-1]), shape[0]
    parts = message[count : count + rows], message[count + rows :]
    return message[:count].reshape(value_shape), parts[0].astype(FULL) + parts[1].astype(FULL)


def kept_rider(rider):
    high, low = halves_of(rider)
    return high + low


class Halving:
    def __init__(self, kept, sent, steps):
        self.slots, self.sent, self.steps = [[half] for half in split(kept)], sent, steps
        self.step, self.last, self.messages, self.waits = 0, (), (), ()
        self.rider = None

    def left(self):
        return self.step < len(self.steps)

    def hold(self, *others):
        self.waits = self.waits + others

    def carry(self, value, axis, mask):
        if self.rider is None or self.step == 0:
            self.messages += (value,)
            return flip(value, axis, mask)
        message = with_rider(value, self.rider)
        self.messages += (message,)
        message = flip(message, axis, mask)
        value, rider = rider_of(message, self.rider.shape, value.shape)
        self.rider = kept_rider(self.rider) + rider
        return value

    def part_sums(self):
        outgoing = []
        for slot, parts in enumerate(self.slots):
            if self.waits:
                parts = parts[:-1] + [after(parts[-1], *self.waits)]
            half = parts[0].shape[0] // 2
            outgoing.append(sum(part[half:].astype(FULL) for part in parts).astype(LOW))
            self.slots[slot] = [part[:half] for part in parts]
        return outgoing

    def send(self, *others):
        one, two = self.steps[self.step]
        self.messages = ()
        if self.step == 0:
            whole = after(self.sent, *self.waits) if self.waits else self.sent
        else:
            outgoing = self.part_sums()
            if others:
                outgoing = [after(value, *others) for value in outgoing]
            whole = jnp.concatenate(outgoing, axis=0) if one == two else None
        if one == two:
            arrived = self.carry(whole, *one)
            self.last = (arrived,)
            arrived = split(arrived)
        else:
            arrived = [self.carry(outgoing[0], *one), flip(outgoing[1], *two)]
            self.messages += (outgoing[1],)
            self.last = tuple(arrived)
        self.slots = [parts + [new] for parts, new in zip(self.slots, arrived)]
        self.step, self.waits = self.step + 1, ()

    def total(self):
        while self.left():
            self.send()
        slots = [parts[:-1] + [after(parts[-1], *self.waits)] if self.waits else parts for parts in self.slots]
        return tuple(sum(part[0].astype(FULL) for part in parts) for parts in slots)


def split(value):
    middle = value.shape[0] // 2
    return [value[:middle], value[middle:]]


class Blocks:
    def __init__(self, count, size):
        self.count, self.size = count, size
        shifts = [(i * size) % LANES for i in range(count)]
        self.shifts = sorted(set(shifts))
        self.wide = -(-(size + max(shifts)) // LANES) * LANES
        self.aligned = max(shifts) == 0 and size % LANES == 0
        self.total = count * size
        self.room = max(self.start(i) + self.wide for i in range(count))

    def start(self, index):
        return index * self.size // LANES * LANES

    def start_dynamic(self, index):
        return pl.multiple_of(index * self.size // LANES * LANES, LANES)

    def pad(self, value, index):
        result = None
        for shift in self.shifts:
            low = [(0, 0)] * (value.ndim - 1) + [(shift, self.wide - self.size - shift)]
            placed = jnp.pad(value, low)
            here = (index * self.size) % LANES == shift
            result = placed if result is None else jnp.where(here, placed, result)
        return result

    def cut(self, value, index):
        result = None
        for shift in self.shifts:
            piece = value[..., shift : shift + self.size]
            here = (index * self.size) % LANES == shift
            result = piece if result is None else jnp.where(here, piece, result)
        return result

    def tile_owners(self, tile):
        low, high = tile * LANES, (tile + 1) * LANES
        return [
            (i, low - self.start(i))
            for i in range(self.count)
            if i * self.size < high and (i + 1) * self.size > low
        ]


def matmul(left, right):
    return lax.dot_general(left, right, (((1,), (0,)), ((), ())), preferred_element_type=FULL)


def matmul_nt(left, right):
    return lax.dot_general(left, right, (((1,), (1,)), ((), ())), preferred_element_type=FULL)


def matmul_tn(left, right):
    return lax.dot_general(left, right, (((0,), (0,)), ((), ())), preferred_element_type=FULL)


def normed(values):
    centred = values - jnp.mean(values, axis=-1, keepdims=True)
    spread = jnp.mean(centred * centred, axis=-1, keepdims=True)
    scale = lax.rsqrt(spread + 1e-05)
    return centred * scale, scale


def norm_back(grad, unit, scale, gain):
    inner = grad * gain
    mean_inner = jnp.mean(inner, axis=-1, keepdims=True)
    mean_both = jnp.mean(inner * unit, axis=-1, keepdims=True)
    return scale * (inner - mean_inner - unit * mean_both)


def rows_at(index, size=CHUNK):
    return pl.ds(pl.multiple_of(index * size, size), size)


def places(pos, slot, codes, half):
    owner = pos[2] if slot == 0 else 1 - pos[2]
    for index, (d_mask, w_mask) in enumerate(codes):
        yield index, pos[0] ^ d_mask, owner * half + (pos[1] ^ w_mask)


def load_pieces(pos, refs, codes, half, lanes, target, sem):
    for ref, (slot, group) in zip(refs, codes):
        for index, doc, inner in places(pos, slot, group, half):
            pltpu.make_async_copy(
                ref.at[index, :, pl.ds(lanes[0], lanes[1])], target(doc, inner), sem
            ).start()


def load_folded(pos, refs, codes, half, rows, blocks, begin, folds, held, sem):
    for fold in range(folds):
        def target(doc, inner):
            first = pl.ds(pl.multiple_of((doc * folds + fold) * rows, rows), rows)
            if blocks.aligned:
                return held.at[first, pl.ds(blocks.start_dynamic(inner), blocks.wide)]
            return held.at[inner, first, :]

        load_pieces(pos, refs, codes, half, (begin + fold * blocks.wide, blocks.wide), target, sem)


def begin(source, target, sem):
    pltpu.make_async_copy(source, target, sem).start()


def finish(source, target, sem):
    pltpu.make_async_copy(source, target, sem).wait()


def store_pieces(pos, source, sums, half, targets, lanes, sem):
    for slot, codes in enumerate(sums):
        count = len(codes) // 2
        for index, doc, inner in places(pos, slot, codes, half):
            pltpu.make_async_copy(
                source(doc, inner),
                targets[index // count].at[slot * count + index % count, :, pl.ds(lanes[0], lanes[1])],
                sem,
            ).start()


def wait_whole(ref, sem):
    pltpu.make_async_copy(ref, ref, sem).wait()


def row_target(ref, blocks, rows):
    if blocks.aligned:
        return lambda doc, inner: ref.at[
            pl.ds(pl.multiple_of(inner * rows, rows), rows),
            pl.ds(blocks.start_dynamic(doc), blocks.wide),
        ]
    return lambda doc, inner: ref.at[doc, pl.ds(pl.multiple_of(inner * rows, rows), rows), :]


def held_shape(blocks, height):
    return (height, blocks.total) if blocks.aligned else (blocks.count, height, blocks.wide)


def merge_tiles(held, whole, blocks):
    for tile in range(blocks.total // LANES):
        value = None
        for index, offset in blocks.tile_owners(tile):
            piece = held[index, :, offset : offset + LANES]
            value = piece if value is None else value + piece
        whole[:, tile * LANES : (tile + 1) * LANES] = value


def project_kernel(shape, pos, gains, page_col, page_row, mask_row, own_hbm, *refs):
    codes, half, rows, blocks, length, width, factor, chunks = shape
    arrived, refs = refs[: len(chunks)], refs[len(chunks) :]
    pieces, refs = refs[: len(codes)], refs[len(codes) :]
    outs, refs = refs[:7], refs[7:]
    (q_out, k_out, v_out, att_out, lse_out, weight, other) = kept = refs[:7]
    (own, held, h_own, h_oth, allowed, sem, sem_out, sem_in) = refs[7:]
    begin(own_hbm, own, sem_in.at[0])
    load_pieces(pos, pieces, codes, half, (0, blocks.wide), row_target(held, blocks, rows), sem)
    starts = [sum(chunks[:i]) for i in range(len(chunks))]
    places_in = [other.at[pl.ds(start, size), :] for start, size in zip(starts, chunks)]
    for i, (ref, place) in enumerate(zip(arrived, places_in)):
        begin(ref, place, sem_in.at[i + 1])
    finish(own_hbm, own, sem_in.at[0])
    for i, (ref, place) in enumerate(zip(arrived, places_in)):
        finish(ref, place, sem_in.at[i + 1])
    begin(other, outs[6], sem_out.at[6])
    for i in range(length // CHUNK):
        part = pl.ds(i * CHUNK, CHUNK)
        unit, _ = normed(own[part, :].astype(FULL))
        h_own[part, :] = (unit * gains[0:1, :]).astype(LOW)
        unit, _ = normed(other[part, :].astype(FULL))
        h_oth[part, :] = (unit * gains[1:2, :]).astype(LOW)
        row = lax.broadcasted_iota(jnp.int32, (CHUNK, length), 0) + i * CHUNK
        col = lax.broadcasted_iota(jnp.int32, (CHUNK, length), 1)
        ok = (page_col[part, :] == page_row[...]) & ((mask_row[...] == 1) | (row == col))
        allowed[part, :] = jnp.where(ok, 1.0, 0.0)
    wait_whole(held, sem)
    merge_tiles(held, weight, blocks)
    begin(weight, outs[5], sem_out.at[5])
    lse_out[...] = jnp.zeros_like(lse_out)

    q_out[...] = (matmul(h_own[...], weight[:, :width]).astype(LOW) * factor).astype(LOW)
    k_out[...] = matmul(h_oth[...], weight[:, width : 2 * width]).astype(LOW)
    v_out[...] = matmul(h_oth[...], weight[:, 2 * width :]).astype(LOW)
    for i in range(3):
        begin(kept[i], outs[i], sem_out.at[i])
    size = width // HEADS
    per = LANES // size

    @pl.loop(0, width // LANES)
    def _(pair):
        cols = pl.ds(pl.multiple_of(pair * LANES, LANES), LANES)
        keys, values, queries = k_out[:, cols], v_out[:, cols], q_out[:, cols]
        lane = lax.broadcasted_iota(jnp.int32, queries.shape, 1)
        result, sums = None, lse_out[...]
        for sub in range(per):
            inside = lane // size == sub
            scores = matmul_nt(jnp.where(inside, queries, jnp.zeros_like(queries)), keys)
            scores = jnp.where(allowed[...] > 0.5, scores, NEG)
            top = jnp.max(scores, axis=-1, keepdims=True)
            exps = jnp.exp(scores - top)
            total = jnp.sum(exps, axis=-1, keepdims=True)
            out = matmul(exps.astype(LOW), values) * (1.0 / total)
            result = out if result is None else jnp.where(inside, out, result)
            sums = jnp.where(lane == pair * per + sub, top + jnp.log(total), sums)
        lse_out[...] = sums
        att_out[:, cols] = result.astype(LOW)

    for i in (3, 4):
        begin(kept[i], outs[i], sem_out.at[i])
    for i, ref in enumerate(kept):
        finish(ref, outs[i], sem_out.at[i])


def feed_kernel(shape, pos, coef, gain, page_col, att_hbm, own_hbm, cot_hbm, cotj_hbm, arrived_hbm, *refs):
    (codes, counts, sums_b, sums_c, half, rows, down_rows, ups, outs, downs, length, width, hidden, block) = shape
    pieces, refs = refs[: len(codes)], refs[len(codes) :]
    out_ref, dmid_ref, datt_ref, away_ref, dgain_ref = refs[:5]
    up_targets, down_targets = refs[5:7], refs[7:9]
    (w_up, o_held, w_out, d_held, w_down, g_up, g_out, g_down, att, own, cot, cotj_own, cotj_oth, mid, h2, h2_t, dffn, dffn_t,
     att_t, acts, dpre, acc, dacc, dbranch, sem_up, sem_out, sem_down, sem_gup, sem_gdown, sems) = refs[9:]
    begin(att_hbm, att, sems.at[0])
    last = counts
    load_pieces(pos, pieces[:last], codes[:last], half, (ups.wide, outs.wide), row_target(o_held, outs, rows), sem_out)
    begin(own_hbm, own, sems.at[1])
    begin(cot_hbm, cot, sems.at[2])
    begin(cotj_hbm, cotj_own, sems.at[3])
    begin(arrived_hbm, cotj_oth, sems.at[4])
    load_pieces(pos, pieces[:last], codes[:last], half, (0, ups.wide), row_target(w_up, ups, rows), sem_up)
    folds = down_rows // rows
    load_folded(pos, pieces[last:], codes[last:], half, rows, downs, 0, folds, d_held, sem_down)
    half_rows = length // 2
    parts = length // CHUNK

    def valid_at(part):
        return jnp.where(page_col[part, :] >= 0, 1.0, 0.0)

    finish(att_hbm, att, sems.at[0])
    wait_whole(o_held, sem_out)
    merge_tiles(o_held, w_out, outs)
    mid[...] = matmul(att[...], w_out[...])
    att_t[...] = att[...].T
    finish(own_hbm, own, sems.at[1])
    for i in range(parts):
        part = pl.ds(i * CHUNK, CHUNK)
        middle = own[part, :].astype(FULL) + valid_at(part) * mid[part, :]
        mid[part, :] = middle
        unit, _ = normed(middle)
        h2[part, :] = (unit * gain[...]).astype(LOW)
    finish(cot_hbm, cot, sems.at[2])
    finish(cotj_hbm, cotj_own, sems.at[3])
    finish(arrived_hbm, cotj_oth, sems.at[4])
    for which, ref in ((pos[2], cotj_own), (1 - pos[2], cotj_oth)):
        for i in range(half_rows // CHUNK):
            part = pl.ds(pl.multiple_of(which * half_rows + i * CHUNK, CHUNK), CHUNK)
            grad = cot[part, :] + coef[...] * ref[pl.ds(i * CHUNK, CHUNK), :].astype(FULL)
            cot[part, :] = grad
            dffn[part, :] = (grad * valid_at(part)).astype(LOW)
    dffn_t[...] = dffn[...].T
    h2_t[...] = h2[...].T
    acc[...] = jnp.zeros_like(acc)
    dacc[...] = jnp.zeros_like(dacc)
    wait_whole(w_up, sem_up)
    wait_whole(d_held, sem_down)
    if not downs.aligned:
        merge_tiles(d_held, w_down, downs)
    down = d_held if downs.aligned else w_down
    c0, c1 = 0.7978845608028654, 0.044715

    @pl.loop(0, hidden // block)
    def _(f):
        cols = pl.ds(pl.multiple_of(f * block, LANES), block)
        pre = matmul(h2[...], w_up[:, cols])
        dact = matmul(dffn[...], down[:, cols])
        square = pre * pre
        flat = jnp.tanh(c0 * (pre + c1 * square * pre))
        cdf = 0.5 * (1.0 + flat)
        slope = cdf + pre * (0.5 * (1.0 - flat * flat)) * (c0 * (1.0 + 3.0 * c1 * square))
        acts[...] = (pre * cdf).astype(LOW)
        dpre[...] = (slope * dact).astype(LOW)
        acc[...] += matmul_nt(acts[...], down[:, cols])
        dacc[...] += matmul_nt(dpre[...], w_up[:, cols])
        g_down[:, cols] = matmul(dffn_t[...], acts[...]).astype(LOW)
        g_up[:, cols] = matmul(h2_t[...], dpre[...]).astype(LOW)

    if downs.room > downs.total:
        g_down[:, downs.total :] = jnp.zeros((width, downs.room - downs.total), LOW)
    store_pieces(
        pos,
        lambda doc, inner: g_down.at[
            pl.ds(pl.multiple_of(doc * down_rows, down_rows), down_rows),
            pl.ds(downs.start_dynamic(inner), downs.wide),
        ],
        sums_c, half, down_targets, (0, downs.wide), sem_gdown,
    )
    store_pieces(
        pos,
        lambda doc, inner: g_up.at[
            pl.ds(pl.multiple_of(inner * rows, rows), rows),
            pl.ds(ups.start_dynamic(doc), ups.wide),
        ],
        sums_b, half, up_targets, (0, ups.wide), sem_gup,
    )
    dgain_ref[...] = jnp.zeros_like(dgain_ref)
    for i in range(parts):
        part = pl.ds(i * CHUNK, CHUNK)
        valid = valid_at(part)
        middle = mid[part, :]
        acc[part, :] = middle + valid * acc[part, :]
        unit, scale = normed(middle)
        grad = dacc[part, :]
        dgain_ref[pl.ds(2 + pos[2], 1), :] += jnp.sum(grad * unit, axis=0, keepdims=True)
        dmid = cot[part, :] + norm_back(grad, unit, scale, gain[...])
        dacc[part, :] = dmid
        dbranch[part, :] = (dmid * valid).astype(LOW)
    begin(acc, out_ref, sems.at[0])
    begin(dacc, dmid_ref, sems.at[1])
    h2[...] = matmul_nt(dbranch[...], w_out[...]).astype(LOW)
    begin(h2, datt_ref, sems.at[2])
    g_out[:, : outs.total] = matmul(att_t[...], dbranch[...]).astype(LOW)
    if outs.room > outs.total:
        g_out[:, outs.total :] = jnp.zeros((width, outs.room - outs.total), LOW)
    store_pieces(
        pos,
        lambda doc, inner: g_out.at[
            pl.ds(pl.multiple_of(inner * rows, rows), rows),
            pl.ds(outs.start_dynamic(doc), outs.wide),
        ],
        sums_b, half, up_targets, (ups.wide, outs.wide), sem_gup,
    )
    for i in range(half_rows // CHUNK):
        part = pl.ds(pl.multiple_of((1 - pos[2]) * half_rows + i * CHUNK, CHUNK), CHUNK)
        away_ref[pl.ds(i * CHUNK, CHUNK), :] = acc[part, :].astype(LOW)
    for target in down_targets:
        wait_whole(target, sem_gdown)
    for target in up_targets:
        wait_whole(target, sem_gup)
    finish(acc, out_ref, sems.at[0])
    finish(dacc, dmid_ref, sems.at[1])
    finish(h2, datt_ref, sems.at[2])


def scores_back_kernel(shape, pairs, page_col, page_row, mask_row, q_hbm, k_hbm, v_hbm, att_hbm, datt_hbm, lse_hbm, *refs):
    length, width, factor = shape
    outs, refs = refs[:3], refs[3:]
    (q_ref, k_ref, v_ref, att, datt, lse, dq, dk, dv, allowed, lse_t, dots_t, sems) = refs
    size = width // HEADS
    per = LANES // size
    cols_here = pl.ds(pairs[0] * LANES, (pairs[1] - pairs[0]) * LANES)
    loads = [(source.at[:, cols_here], target) for source, target in
             ((datt_hbm, datt), (att_hbm, att), (q_hbm, q_ref), (k_hbm, k_ref), (v_hbm, v_ref))]
    loads.append((lse_hbm, lse))
    for i, (source, target) in enumerate(loads):
        begin(source, target, sems.at[i])
    mask = jnp.broadcast_to(mask_row[...].astype(FULL), (LANES, length)).T[:, 0:1]
    row = lax.broadcasted_iota(jnp.int32, (length, length), 0)
    col = lax.broadcasted_iota(jnp.int32, (length, length), 1)
    ok = (page_col[...] == page_row[...]) & ((mask == 1.0) | (row == col))
    allowed[...] = jnp.where(ok, 1.0, 0.0)
    here_width = cols_here.size
    head = lax.broadcasted_iota(jnp.int32, (LANES, here_width), 0)
    lane = lax.broadcasted_iota(jnp.int32, (LANES, here_width), 1)
    chosen = jnp.where(lane // size == head, 1.0, 0.0)
    for i, (source, target) in enumerate(loads):
        finish(source, target, sems.at[i])
    dots_t[...] = lax.dot_general(
        chosen, att[...].astype(FULL) * datt[...].astype(FULL), (((1,), (1,)), ((), ())),
        preferred_element_type=FULL, precision=lax.Precision.HIGHEST,
    )
    lse_t[...] = lse[...].T

    @pl.loop(0, pairs[1] - pairs[0])
    def _(pair):
        cols = pl.ds(pl.multiple_of(pair * LANES, LANES), LANES)
        queries, grads = q_ref[:, cols], datt[:, cols]
        keys, values = k_ref[:, cols], v_ref[:, cols]
        lane = lax.broadcasted_iota(jnp.int32, (length, LANES), 1)
        zero = jnp.zeros_like(queries)
        trio = None
        for sub in range(per):
            inside = lane // size == sub
            lse_row = lse_t[pl.ds((pair + pairs[0]) * per + sub, 1), :]
            dot_row = dots_t[pl.ds(pair * per + sub, 1), :]
            scores = matmul_nt(keys, jnp.where(inside, queries, zero))
            scores = jnp.where(allowed[...] > 0.5, scores, NEG)
            probs = jnp.exp(scores - lse_row)
            dprob = matmul_nt(values, jnp.where(inside, grads, zero))
            low = (probs * (dprob - dot_row)).astype(LOW)
            three = (matmul_tn(low, keys), matmul(low, queries), matmul(probs.astype(LOW), grads))
            trio = three if trio is None else [jnp.where(inside, new, old) for new, old in zip(three, trio)]
        dq[:, cols] = (trio[0] * factor).astype(LOW)
        dk[:, cols] = trio[1].astype(LOW)
        dv[:, cols] = trio[2].astype(LOW)

    for i, (source, target) in enumerate(zip((dq, dk, dv), outs)):
        begin(source, target, sems.at[i])
    for i, (source, target) in enumerate(zip((dq, dk, dv), outs)):
        finish(source, target, sems.at[i])


def project_back_kernel(shape, pos, gains, own_hbm, other_hbm, weight_hbm, *refs):
    (sums, half, rows, blocks, length, width, runs) = shape
    given, refs = refs[: 3 * len(runs)], refs[3 * len(runs) :]
    own_out, oth_ref, dgain_ref = refs[:3]
    targets, refs = refs[3:5], refs[5:]
    h_t, flat, own_ref, grad, own, other, weight, sem, sems = refs[:9]
    copies = refs[9:]
    grads = [copies[3 * i : 3 * i + 3] for i in range(len(runs))]
    parts = length // CHUNK
    loads = [(own_hbm, own), (other_hbm, other), *zip(given, copies), (weight_hbm, weight)]
    for i, (source, target) in enumerate(loads):
        begin(source, target, sems.at[i])

    def take(i):
        finish(*loads[i], sems.at[i])

    for which, source in ((0, own), (1, other)):
        take(which)
        for i in range(parts):
            part = pl.ds(i * CHUNK, CHUNK)
            unit, _ = normed(source[part, :].astype(FULL))
            flat[part, :] = unit * gains[which : which + 1, :]
        h_t[which] = flat[...].astype(LOW).T
    for i in range(2, len(loads) - 1):
        take(i)
    for (low, high), trio in zip(runs, grads):
        for block, (which, ref) in enumerate(zip((0, 1, 1), trio)):
            grad[:, block * width + low : block * width + high] = matmul(h_t[which], ref[...]).astype(LOW)
    if blocks.room > blocks.total:
        grad[:, blocks.total :] = jnp.zeros((width, blocks.room - blocks.total), LOW)
    store_pieces(
        pos,
        lambda doc, inner: grad.at[
            pl.ds(pl.multiple_of(inner * rows, rows), rows),
            pl.ds(blocks.start_dynamic(doc), blocks.wide),
        ],
        sums, half, targets, (0, blocks.wide), sem,
    )
    dgain_ref[...] = jnp.zeros_like(dgain_ref)
    take(len(loads) - 1)
    own_ref[...] = sum(
        matmul_nt(trio[0][...], weight[:, low:high]) for (low, high), trio in zip(runs, grads)
    )
    begin(own_ref, own_out, sems.at[0])
    flat[...] = sum(
        matmul_nt(trio[block][...], weight[:, block * width + low : block * width + high])
        for (low, high), trio in zip(runs, grads)
        for block in (1, 2)
    )
    for i in range(parts):
        part = pl.ds(i * CHUNK, CHUNK)
        unit, _ = normed(own[part, :].astype(FULL))
        dgain_ref[pl.ds(pos[2], 1), :] += jnp.sum(own_ref[part, :] * unit, axis=0, keepdims=True)
        unit, _ = normed(other[part, :].astype(FULL))
        value = flat[part, :]
        oth_ref[part, :] = value.astype(LOW)
        dgain_ref[pl.ds(1 - pos[2], 1), :] += jnp.sum(value * unit, axis=0, keepdims=True)
    finish(own_ref, own_out, sems.at[0])
    for target in targets:
        wait_whole(target, sem)


def tail_kernel(length, own, gain, mine, theirs, dmid, out_ref):
    for i in range(length // CHUNK):
        part = pl.ds(i * CHUNK, CHUNK)
        unit, scale = normed(own[part, :].astype(FULL))
        grad = mine[part, :] + theirs[part, :].astype(FULL)
        out_ref[part, :] = dmid[part, :] + norm_back(grad, unit, scale, gain[...])


VMEM = pl.BlockSpec(memory_space=pltpu.VMEM)
HBM = pl.BlockSpec(memory_space=pltpu.HBM)
SMEM = pl.BlockSpec(memory_space=pltpu.SMEM)


LITTLE = pl.CostEstimate(flops=1_000, bytes_accessed=1_000, transcendentals=0)


def params(mebibytes):
    return pltpu.CompilerParams(vmem_limit_bytes=mebibytes * 1024 * 1024)


def adam_update(weight, first, second, grad, rate, decay):
    first_new = 0.9 * first + 0.1 * grad
    second_new = 0.999 * second + 0.001 * grad * grad
    first_hat = first_new / (1.0 - 0.9**STEP)
    second_hat = second_new / (1.0 - 0.999**STEP)
    weight_new = weight - rate * (first_hat / (jnp.sqrt(second_hat) + 1e-08) + decay * weight)
    return (weight_new, first_new, second_new)


def shards(
    rows, cot_stream, cot_joined, page, key_mask,
    w_qkv, m_qkv, v_qkv, w_out, m_out, v_out, w_up, m_up, v_up, w_down, m_down, v_down,
    gains, m_gains, v_gains,
):
    docs, wide = lax.axis_size("docs"), lax.axis_size("wide")
    half = wide // 2
    doc, place = lax.axis_index("docs"), lax.axis_index("wide")
    stream = place // half
    is_text = stream == 0
    pos = jnp.stack((doc, place % half, stream)).astype(jnp.int32)
    length, width = rows.shape
    half_rows = length // 2
    factor = float(width // HEADS) ** (-0.5)
    piece_rows = w_qkv.shape[1]
    hidden = w_up.shape[2] * docs
    qkvs, outs, ups = Blocks(docs, w_qkv.shape[2]), Blocks(docs, w_out.shape[2]), Blocks(docs, w_up.shape[2])
    downs = Blocks(wide, w_down.shape[1])
    down_rows = w_down.shape[2]

    core = [("wide", 1)]
    along_x = [("docs", 1)]
    along_y = [("docs", 1 << b) for b in range(1, docs.bit_length() - 1)]
    along_z = [("wide", 1 << b) for b in range(1, half.bit_length() - 1)]
    across = ("wide", half)

    def swap(value):
        return flip(value, *across)

    column = doc * w_qkv.shape[2] + lax.iota(jnp.int32, w_qkv.shape[2])
    is_query = (column < width)[None, None, :]
    pair_qkv = jnp.where(is_query, w_qkv, w_qkv[::-1]).astype(LOW)

    def own_first(pair):
        return jnp.where(is_text, pair, pair[::-1])

    unit_a = qkvs.pad(own_first(pair_qkv), doc)
    unit_b = jnp.concatenate(
        (ups.pad(own_first(w_up.astype(LOW)), doc), outs.pad(own_first(w_out.astype(LOW)), doc)), axis=-1
    )
    unit_c = downs.pad(jnp.swapaxes(own_first(w_down.astype(LOW)), 1, 2), place)
    folds = down_rows // piece_rows

    def folded(unit):
        return jnp.concatenate([unit[i * piece_rows : (i + 1) * piece_rows] for i in range(folds)], axis=-1)

    page_col, page_row = page[:, None], page[None, :]
    mask_row = key_mask[None, :]
    gain_own = lax.dynamic_index_in_dim(gains, stream, 0, keepdims=True)
    gain_oth = lax.dynamic_index_in_dim(gains, 1 - stream, 0, keepdims=True)
    gain_one = jnp.concatenate((gain_own, gain_oth), axis=0)
    gain_two = lax.dynamic_index_in_dim(gains, 2 + stream, 0, keepdims=True)
    mix = jax.nn.sigmoid(gains[4])[None, :]
    coef = jnp.where(is_text, mix, 1.0 - mix)

    cot_low = cot_joined.astype(LOW)
    unit_a_oth = swap(unit_a[1])
    unit_b_oth = swap(after(unit_b[1], unit_a_oth)) if FIRST_A else swap(unit_b[1])
    if downs.aligned:
        unit_c_oth = swap(after(unit_c[1], unit_a_oth))
    else:
        raw = jnp.swapaxes(own_first(w_down.astype(LOW)), 1, 2)
        unit_c_oth = downs.pad(swap(raw[1]), (place + half) % wide)
    zxy, zyx = along_z + along_x + along_y, along_z + along_y + along_x
    a_own, a_oth = Doubling(unit_a[0], 0, zxy), Doubling(unit_a_oth, 1, zyx)
    b_own = Doubling(unit_b[0], 0, along_y + along_x + along_z)
    c_own = Doubling(folded(unit_c[0]), 0, along_y + along_z + along_x)
    b_oth, c_oth = Doubling(unit_b_oth, 1, zxy), Doubling(folded(unit_c_oth), 1, zyx)
    steps_y, steps_x = len(along_y), len(along_x)
    chunks, begin = [], 0
    for size in [length * part // sum(ROW_PARTS) for part in ROW_PARTS]:
        some = rows[begin : begin + size]
        chunks.append(swap(after(some, chunks[-1] if chunks else unit_a_oth)))
        begin += size
    for _ in range(steps_y):
        b_own.send()
    for _ in range(steps_y):
        c_own.send()
    for _ in range(steps_x):
        b_own.send(unit_a_oth)
    for _ in along_z:
        c_own.send(unit_a_oth)
    a_own.send_all()
    a_oth.send_all()
    first = (a_oth.arrays[len(along_z) + steps_y], a_own.arrays[len(along_z) + steps_x])
    rest = (a_oth.arrays[-1], a_own.arrays[-1])
    for one in (b_oth, c_oth):
        for _ in along_z:
            one.send(*first, page_col, gain_one, gain_two, coef, cot_low)
    met = b_oth.last + c_oth.last
    for one in (b_own, c_own):
        while one.step < len(one.order):
            one.send(*met)
    for one, steps in ((b_oth, steps_x), (c_oth, steps_y)):
        for _ in range(steps):
            one.send(*rest, chunks[1])
    for one in (b_oth, c_oth):
        while one.step < len(one.order):
            one.send(chunks[-1])
    pieces_a, codes_a = [], []
    for one in (a_own, a_oth):
        for value, known in one.split_newest():
            one.add(value, known, *core[0])
        pieces_a += one.arrays
        codes_a += one.slotted()
    waiting, passed = [], []
    for one in (b_own, b_oth, c_own, c_oth):
        early, late = one.split_newest()
        passed.append(one.add(after(early[0], chunks[-1]), early[1], *core[0]))
        waiting.append((one, *late))
    other_joined = swap(after(cot_low, chunks[-1], *passed))

    low_rows = jax.ShapeDtypeStruct((length, width), LOW)
    full_rows = jax.ShapeDtypeStruct((length, width), FULL)

    sizes = tuple(chunk.shape[0] for chunk in chunks)
    shape = (codes_a, half, piece_rows, qkvs, length, width, factor, sizes)
    made = (low_rows, low_rows, low_rows, low_rows, jax.ShapeDtypeStruct((length, LANES), FULL),
            jax.ShapeDtypeStruct((width, 3 * width), LOW), low_rows)
    queries, keys, values, attended, lse, weight_qkv, other_rows = pl.pallas_call(
        functools.partial(project_kernel, shape),
        out_shape=made,
        in_specs=[SMEM] + [VMEM] * 4 + [HBM] * (1 + len(chunks) + len(pieces_a)),
        out_specs=(HBM,) * 7,
        scratch_shapes=[pltpu.VMEM(one.shape, one.dtype) for one in made] + [
            pltpu.VMEM((length, width), LOW),
            pltpu.VMEM((docs, width, qkvs.wide), LOW),
            pltpu.VMEM((length, width), LOW),
            pltpu.VMEM((length, width), LOW),
            pltpu.VMEM((length, length), FULL),
            pltpu.SemaphoreType.DMA,
            pltpu.SemaphoreType.DMA((7,)),
            pltpu.SemaphoreType.DMA((1 + len(chunks),)),
        ],
        compiler_params=params(60),
        cost_estimate=LITTLE,
        name="project_attend",
    )(pos, gain_one, page_col, page_row, mask_row, rows, *chunks, *pieces_a)

    here = [value for _, value, _ in waiting]
    for one, value, known in waiting:
        one.add(after(value, lse, other_joined, *here), known, *core[0])
    streams = (b_own, b_oth, c_own, c_oth)
    pieces_b = sum((one.arrays for one in streams), [])
    codes_b = sum((one.slotted() for one in streams), [])
    counts = len(b_own.arrays) + len(b_oth.arrays)
    xy, yx = along_x + along_y, along_y + along_x
    steps_b = [core * 2, *zip(xy, yx), *((step, step) for step in along_z)]
    steps_c = [core * 2, *((step, step) for step in along_z), *zip(xy, yx)]
    sums_of = [tuple(sum_codes([pair[slot] for pair in steps]) for slot in (0, 1)) for steps in (steps_b, steps_c)]
    sent_count = len(sums_of[0][0])
    block = 6 * LANES
    shape = (codes_b, counts, *sums_of, half, piece_rows, down_rows, ups, outs, downs, length, width, hidden, block)
    shape_b = jax.ShapeDtypeStruct((sent_count, piece_rows, ups.wide + outs.wide), LOW)
    shape_c = jax.ShapeDtypeStruct((sent_count, down_rows, downs.wide), LOW)
    (stream_out, middle_grad, attended_grad, away, dgain_two, kept_b, sent_b, kept_c, sent_c) = pl.pallas_call(
        functools.partial(feed_kernel, shape),
        out_shape=(full_rows, full_rows, low_rows, jax.ShapeDtypeStruct((half_rows, width), LOW),
                   jax.ShapeDtypeStruct((8, width), FULL), shape_b, shape_b, shape_c, shape_c),
        in_specs=[SMEM] + [VMEM] * 3 + [HBM] * (5 + len(pieces_b)),
        out_specs=(HBM,) * 3 + (VMEM,) * 2 + (HBM,) * 4,
        scratch_shapes=[
            pltpu.VMEM((width, hidden), LOW),
            pltpu.VMEM(held_shape(outs, width), LOW),
            pltpu.VMEM((width, width), LOW),
            pltpu.VMEM(held_shape(downs, width), LOW),
            pltpu.VMEM((8, LANES) if downs.aligned else (width, hidden), LOW),
            pltpu.VMEM((width, hidden), LOW),
            pltpu.VMEM((width, outs.room), LOW),
            pltpu.VMEM((width, downs.room), LOW),
            pltpu.VMEM((length, width), LOW),
            pltpu.VMEM((length, width), LOW),
            pltpu.VMEM((length, width), FULL),
            pltpu.VMEM((half_rows, width), FULL),
            pltpu.VMEM((half_rows, width), LOW),
            pltpu.VMEM((length, width), FULL),
            pltpu.VMEM((length, width), LOW),
            pltpu.VMEM((width, length), LOW),
            pltpu.VMEM((length, width), LOW),
            pltpu.VMEM((width, length), LOW),
            pltpu.VMEM((width, length), LOW),
            pltpu.VMEM((length, block), LOW),
            pltpu.VMEM((length, block), LOW),
            pltpu.VMEM((length, width), FULL),
            pltpu.VMEM((length, width), FULL),
            pltpu.VMEM((length, width), LOW),
        ] + [pltpu.SemaphoreType.DMA] * 5 + [pltpu.SemaphoreType.DMA((5,))],
        compiler_params=params(60),
        cost_estimate=LITTLE,
        name="feed_forward_back",
    )(pos, coef, gain_two, page_col, attended, rows, cot_stream, cot_joined, other_joined, *pieces_b)

    def attend_back(pairs, *operands):
        low_cols = jax.ShapeDtypeStruct((length, (pairs[1] - pairs[0]) * LANES), LOW)
        piece = pltpu.VMEM(low_cols.shape, LOW)
        return pl.pallas_call(
            functools.partial(scores_back_kernel, (length, width, factor), pairs),
            out_shape=(low_cols,) * 3,
            in_specs=[VMEM] * 3 + [HBM] * 6,
            out_specs=(HBM,) * 3,
            scratch_shapes=[piece] * 5 + [pltpu.VMEM((length, LANES), FULL)] + [piece] * 3 + [
                pltpu.VMEM((length, length), FULL),
                pltpu.VMEM((LANES, length), FULL),
                pltpu.VMEM((LANES, length), FULL),
                pltpu.SemaphoreType.DMA((6,)),
            ],
            compiler_params=params(60),
            cost_estimate=LITTLE,
            name="attend_back",
        )(page_col, page_row, mask_row, *operands)

    sums_b, sums_c = Halving(kept_b, sent_b, steps_b), Halving(kept_c, sent_c, steps_c)
    sums_b.send()
    sums_c.send()
    partner_rows = swap(away)
    pair_count = width // LANES
    cuts = (0, pair_count * 2 // 3, pair_count)
    grads_one = attend_back(cuts[:2], queries, keys, values, attended, attended_grad, lse)
    met = (*sums_b.last, *sums_c.last, partner_rows)
    second = after(queries, grads_one[0], *met)
    sums_b.hold(grads_one[0])
    sums_c.hold(grads_one[0])
    sums_b.send(*met)
    sums_c.send(*met)
    grads_two = attend_back(cuts[1:], second, keys, values, attended, attended_grad, lse)

    runs = tuple((low * LANES, high * LANES) for low, high in zip(cuts[:-1], cuts[1:]))
    shape = (sums_of[0], half, piece_rows, qkvs, length, width, runs)
    shape_a = jax.ShapeDtypeStruct((sent_count, piece_rows, qkvs.wide), LOW)
    own_part, away_part, dgain_one, kept_a, sent_a = pl.pallas_call(
        functools.partial(project_back_kernel, shape),
        out_shape=(full_rows, low_rows, jax.ShapeDtypeStruct((8, width), FULL)) + (shape_a,) * 2,
        in_specs=[SMEM, VMEM] + [HBM] * (3 + 3 * len(runs)),
        out_specs=(HBM,) + (VMEM,) * 2 + (HBM,) * 2,
        scratch_shapes=[
            pltpu.VMEM((2, width, length), LOW),
            pltpu.VMEM((length, width), FULL),
            pltpu.VMEM((length, width), FULL),
            pltpu.VMEM((width, qkvs.room), LOW),
            pltpu.VMEM((length, width), LOW),
            pltpu.VMEM((length, width), LOW),
            pltpu.VMEM((width, 3 * width), LOW),
            pltpu.SemaphoreType.DMA,
            pltpu.SemaphoreType.DMA((3 + 3 * len(runs),)),
        ] + [pltpu.VMEM((length, high - low), LOW) for low, high in runs for _ in range(3)],
        compiler_params=params(60),
        cost_estimate=LITTLE,
        name="project_back",
    )(pos, gain_one, rows, other_rows, weight_qkv, *grads_one, *grads_two)

    own_rows = lax.dynamic_slice_in_dim(stream_out, stream * half_rows, half_rows, 0)
    partner_rows = partner_rows.astype(FULL)
    text_rows = jnp.where(is_text, own_rows, partner_rows)
    image_rows = jnp.where(is_text, partner_rows, own_rows)
    joined_rows = mix * text_rows + (1.0 - mix) * image_rows
    gate_grad = jnp.sum(cot_joined * (text_rows - image_rows), axis=0, keepdims=True) * mix * (1.0 - mix)

    slot_index = lax.iota(jnp.int32, 5)[:, None]
    small = dgain_one[:5] + dgain_two[:5] + jnp.where(slot_index == 4, gate_grad, 0.0)
    sums_a = Halving(kept_a, sent_a, steps_b)
    sums_a.hold(*sums_b.last, *sums_c.last)
    sums_a.send()
    sums_a.rider = rider_rows(small + flip(small, *core[0]), qkvs.wide)
    back_part = swap(away_part)
    sums_a.send()
    sums_b.hold(*sums_a.messages)
    sums_b.send()
    sums_a.hold(*sums_b.messages)
    sums_a.send()
    sums_c.hold(*sums_a.messages)
    sums_c.send()
    sums_b.hold(*sums_a.messages)

    total_a, total_b, total_c = sums_a.total(), sums_b.total(), sums_c.total()

    last = total_a[1].astype(LOW)[None]
    packed = with_rider(last, sums_a.rider)
    arrived = swap(packed)
    packed_c = total_c[1].astype(LOW)
    grad_rows = pl.pallas_call(
        functools.partial(tail_kernel, length),
        out_shape=full_rows,
        in_specs=[VMEM] * 5,
        out_specs=VMEM,
        compiler_params=params(10),
        name="norm_tail",
    )(rows, gain_own, own_part, back_part, after(middle_grad, packed, packed_c))

    def both(total):
        return total[0], swap(total[1].astype(LOW))

    def placed(mine, theirs):
        theirs = theirs.astype(FULL)
        return jnp.where(is_text, jnp.stack((mine, theirs)), jnp.stack((theirs, mine)))

    mine_b, theirs_b = both(total_b)
    theirs_b = after(theirs_b, packed, packed_c)
    grad_b = placed(mine_b, theirs_b)
    grad_up = ups.cut(grad_b[..., : ups.wide], doc)
    grad_out = outs.cut(grad_b[..., ups.wide :], doc)
    out_new = adam_update(w_out, m_out, v_out, grad_out, 0.5, 0.01)
    up_new = adam_update(w_up, m_up, v_up, grad_up, 0.12, 0.01)
    if downs.aligned:
        mine_c, theirs_c = total_c[0], swap(packed_c)
    else:
        mine_c = downs.cut(total_c[0], place)
        theirs_c = swap(downs.cut(total_c[1], (place + half) % wide).astype(LOW))
    theirs_c = after(theirs_c, packed, grad_rows, up_new[0], out_new[0])
    grad_down = jnp.swapaxes(placed(mine_c, theirs_c), 1, 2)
    down_new = adam_update(w_down, m_down, v_down, grad_down, 0.06, 0.01)
    arrived = after(arrived, grad_rows, up_new[0], out_new[0], down_new[0])
    last, rider = rider_of(arrived, sums_a.rider.shape, last.shape)
    gains_grad = rider_value(kept_rider(sums_a.rider) + rider, gains.shape)
    mine_a, theirs_a = total_a[0], last[0]
    mine_a, theirs_a = qkvs.cut(mine_a, doc), qkvs.cut(theirs_a.astype(FULL), doc)
    query_here = is_query[0]
    grad_qkv = placed(
        jnp.where(query_here, mine_a, theirs_a), jnp.where(query_here, theirs_a, mine_a)
    )

    qkv_new = adam_update(w_qkv, m_qkv, v_qkv, grad_qkv, 0.12, 0.01)
    gains_new = adam_update(gains, m_gains, v_gains, gains_grad, 0.8, 0.0)
    return (stream_out, joined_rows, grad_rows, *qkv_new, *out_new, *up_new, *down_new, *gains_new)


def solution(mesh):
    by_rows = P(("docs", "wide"), None)
    by_row = P(("docs", "wide"))
    weight = P(None, "wide", "docs")
    return jax.shard_map(
        shards,
        mesh=mesh,
        in_specs=(by_rows,) * 3 + (by_row,) * 2 + (weight,) * 12 + (P(),) * 3,
        out_specs=(by_rows,) * 3 + (weight,) * 12 + (P(),) * 3,
        check_vma=False,
    )
```

```python
import functools
import math

import jax
import jax.numpy as jnp
from jax import lax
from jax.experimental import pallas as pl
from jax.experimental.pallas import tpu as pltpu
from jax.sharding import PartitionSpec as P

HEADS = 12
STEP = 10
LANES = 128
CHUNK = 128
ROW_PARTS = (5, 6, 5)
FIRST_A = False
NEG = -1000000000.0
LOW = jnp.bfloat16
FULL = jnp.float32


def flip(value, axis, mask):
    count = lax.axis_size(axis)
    return lax.ppermute(value, axis, [(i, i ^ mask) for i in range(count)])


def flipped(codes, axis, mask):
    d_mask = mask if axis == "docs" else 0
    w_mask = mask if axis == "wide" else 0
    return [(d ^ d_mask, w ^ w_mask) for d, w in codes]


def after(value, *others):
    return lax.optimization_barrier((value, *others))[0]


class Doubling:
    def __init__(self, unit, slot, order):
        self.slot, self.order, self.step = slot, order, 0
        self.arrays, self.codes = [unit[None]], [[(0, 0)]]
        self.last = ()

    def held(self):
        held = self.arrays[0] if len(self.arrays) == 1 else jnp.concatenate(self.arrays, axis=0)
        return held, [code for group in self.codes for code in group]

    def send(self, *others):
        held, known = self.held()
        if others:
            held = after(held, *others)
        axis, mask = self.order[self.step]
        self.arrays.append(flip(held, axis, mask))
        self.codes.append(flipped(known, axis, mask))
        self.step, self.last = self.step + 1, (self.arrays[-1],)

    def send_all(self):
        while self.step < len(self.order):
            self.send()

    def split_newest(self):
        newest, newest_known = self.arrays.pop(), self.codes.pop()
        held, known = self.held()
        self.arrays.append(newest)
        self.codes.append(newest_known)
        return (held, known), (newest, newest_known)

    def add(self, value, known, axis, mask):
        self.arrays.append(flip(value, axis, mask))
        self.codes.append(flipped(known, axis, mask))
        return self.arrays[-1]

    def slotted(self):
        return [(self.slot, group) for group in self.codes]


def sum_codes(order):
    codes = [(0, 0)]
    for axis, mask in reversed(order):
        codes = codes + flipped(codes, axis, mask)
    return codes


def halves_of(value):
    high = lax.reduce_precision(value, 8, 7)
    return high, lax.reduce_precision(value - high, 8, 7)


def rider_rows(value, lanes):
    rows, width = value.shape
    runs = [value[:, i : i + lanes] for i in range(0, width, lanes)]
    runs = [jnp.pad(run, ((0, -rows % 8), (0, lanes - run.shape[1]))) for run in runs]
    return jnp.concatenate(runs, axis=0)


def rider_value(laid, shape):
    rows, width = shape
    high = rows + -rows % 8
    runs = [laid[i * high : i * high + rows] for i in range(laid.shape[0] // high)]
    return jnp.concatenate(runs, axis=1)[:, :width]


def with_rider(value, rider):
    lanes = value.shape[-1]
    tail = [part.astype(LOW) for part in halves_of(rider)]
    return jnp.concatenate((value.reshape(-1, lanes), *tail), axis=0)


def rider_of(message, shape, value_shape):
    count, rows = math.prod(value_shape[:-1]), shape[0]
    parts = message[count : count + rows], message[count + rows :]
    return message[:count].reshape(value_shape), parts[0].astype(FULL) + parts[1].astype(FULL)


def kept_rider(rider):
    high, low = halves_of(rider)
    return high + low


class Halving:
    def __init__(self, kept, sent, steps):
        self.slots, self.sent, self.steps = [[half] for half in split(kept)], sent, steps
        self.step, self.last, self.messages, self.waits = 0, (), (), ()
        self.rider = None

    def left(self):
        return self.step < len(self.steps)

    def hold(self, *others):
        self.waits = self.waits + others

    def carry(self, value, axis, mask):
        if self.rider is None or self.step == 0:
            self.messages += (value,)
            return flip(value, axis, mask)
        message = with_rider(value, self.rider)
        self.messages += (message,)
        message = flip(message, axis, mask)
        value, rider = rider_of(message, self.rider.shape, value.shape)
        self.rider = kept_rider(self.rider) + rider
        return value

    def part_sums(self):
        outgoing = []
        for slot, parts in enumerate(self.slots):
            if self.waits:
                parts = parts[:-1] + [after(parts[-1], *self.waits)]
            half = parts[0].shape[0] // 2
            outgoing.append(sum(part[half:].astype(FULL) for part in parts).astype(LOW))
            self.slots[slot] = [part[:half] for part in parts]
        return outgoing

    def send(self, *others):
        one, two = self.steps[self.step]
        self.messages = ()
        if self.step == 0:
            whole = after(self.sent, *self.waits) if self.waits else self.sent
        else:
            outgoing = self.part_sums()
            if others:
                outgoing = [after(value, *others) for value in outgoing]
            whole = jnp.concatenate(outgoing, axis=0) if one == two else None
        if one == two:
            arrived = self.carry(whole, *one)
            self.last = (arrived,)
            arrived = split(arrived)
        else:
            arrived = [self.carry(outgoing[0], *one), flip(outgoing[1], *two)]
            self.messages += (outgoing[1],)
            self.last = tuple(arrived)
        self.slots = [parts + [new] for parts, new in zip(self.slots, arrived)]
        self.step, self.waits = self.step + 1, ()

    def total(self):
        while self.left():
            self.send()
        slots = [parts[:-1] + [after(parts[-1], *self.waits)] if self.waits else parts for parts in self.slots]
        return tuple(sum(part[0].astype(FULL) for part in parts) for parts in slots)


def split(value):
    middle = value.shape[0] // 2
    return [value[:middle], value[middle:]]


class Blocks:
    def __init__(self, count, size):
        self.count, self.size = count, size
        shifts = [(i * size) % LANES for i in range(count)]
        self.shifts = sorted(set(shifts))
        self.wide = -(-(size + max(shifts)) // LANES) * LANES
        self.aligned = max(shifts) == 0 and size % LANES == 0
        self.total = count * size
        self.room = max(self.start(i) + self.wide for i in range(count))

    def start(self, index):
        return index * self.size // LANES * LANES

    def start_dynamic(self, index):
        return pl.multiple_of(index * self.size // LANES * LANES, LANES)

    def pad(self, value, index):
        result = None
        for shift in self.shifts:
            low = [(0, 0)] * (value.ndim - 1) + [(shift, self.wide - self.size - shift)]
            placed = jnp.pad(value, low)
            here = (index * self.size) % LANES == shift
            result = placed if result is None else jnp.where(here, placed, result)
        return result

    def cut(self, value, index):
        result = None
        for shift in self.shifts:
            piece = value[..., shift : shift + self.size]
            here = (index * self.size) % LANES == shift
            result = piece if result is None else jnp.where(here, piece, result)
        return result

    def tile_owners(self, tile):
        low, high = tile * LANES, (tile + 1) * LANES
        return [
            (i, low - self.start(i))
            for i in range(self.count)
            if i * self.size < high and (i + 1) * self.size > low
        ]


def matmul(left, right):
    return lax.dot_general(left, right, (((1,), (0,)), ((), ())), preferred_element_type=FULL)


def matmul_nt(left, right):
    return lax.dot_general(left, right, (((1,), (1,)), ((), ())), preferred_element_type=FULL)


def matmul_tn(left, right):
    return lax.dot_general(left, right, (((0,), (0,)), ((), ())), preferred_element_type=FULL)


def normed(values):
    centred = values - jnp.mean(values, axis=-1, keepdims=True)
    spread = jnp.mean(centred * centred, axis=-1, keepdims=True)
    scale = lax.rsqrt(spread + 1e-05)
    return centred * scale, scale


def norm_back(grad, unit, scale, gain):
    inner = grad * gain
    mean_inner = jnp.mean(inner, axis=-1, keepdims=True)
    mean_both = jnp.mean(inner * unit, axis=-1, keepdims=True)
    return scale * (inner - mean_inner - unit * mean_both)


def rows_at(index, size=CHUNK):
    return pl.ds(pl.multiple_of(index * size, size), size)


def places(pos, slot, codes, half):
    owner = pos[2] if slot == 0 else 1 - pos[2]
    for index, (d_mask, w_mask) in enumerate(codes):
        yield index, pos[0] ^ d_mask, owner * half + (pos[1] ^ w_mask)


def load_pieces(pos, refs, codes, half, lanes, target, sem):
    for ref, (slot, group) in zip(refs, codes):
        for index, doc, inner in places(pos, slot, group, half):
            pltpu.make_async_copy(
                ref.at[index, :, pl.ds(lanes[0], lanes[1])], target(doc, inner), sem
            ).start()


def load_folded(pos, refs, codes, half, rows, blocks, begin, folds, held, sem):
    for fold in range(folds):
        def target(doc, inner):
            first = pl.ds(pl.multiple_of((doc * folds + fold) * rows, rows), rows)
            if blocks.aligned:
                return held.at[first, pl.ds(blocks.start_dynamic(inner), blocks.wide)]
            return held.at[inner, first, :]

        load_pieces(pos, refs, codes, half, (begin + fold * blocks.wide, blocks.wide), target, sem)


def begin(source, target, sem):
    pltpu.make_async_copy(source, target, sem).start()


def finish(source, target, sem):
    pltpu.make_async_copy(source, target, sem).wait()


def store_pieces(pos, source, sums, half, targets, lanes, sem):
    for slot, codes in enumerate(sums):
        count = len(codes) // 2
        for index, doc, inner in places(pos, slot, codes, half):
            pltpu.make_async_copy(
                source(doc, inner),
                targets[index // count].at[slot * count + index % count, :, pl.ds(lanes[0], lanes[1])],
                sem,
            ).start()


def wait_whole(ref, sem):
    pltpu.make_async_copy(ref, ref, sem).wait()


def row_target(ref, blocks, rows):
    if blocks.aligned:
        return lambda doc, inner: ref.at[
            pl.ds(pl.multiple_of(inner * rows, rows), rows),
            pl.ds(blocks.start_dynamic(doc), blocks.wide),
        ]
    return lambda doc, inner: ref.at[doc, pl.ds(pl.multiple_of(inner * rows, rows), rows), :]


def held_shape(blocks, height):
    return (height, blocks.total) if blocks.aligned else (blocks.count, height, blocks.wide)


def merge_tiles(held, whole, blocks):
    for tile in range(blocks.total // LANES):
        value = None
        for index, offset in blocks.tile_owners(tile):
            piece = held[index, :, offset : offset + LANES]
            value = piece if value is None else value + piece
        whole[:, tile * LANES : (tile + 1) * LANES] = value


def project_kernel(shape, pos, gains, page_col, page_row, mask_row, own_hbm, *refs):
    codes, half, rows, blocks, length, width, factor, chunks = shape
    arrived, refs = refs[: len(chunks)], refs[len(chunks) :]
    pieces, refs = refs[: len(codes)], refs[len(codes) :]
    outs, refs = refs[:7], refs[7:]
    (q_out, k_out, v_out, att_out, lse_out, weight, other) = kept = refs[:7]
    (own, held, h_own, h_oth, allowed, sem, sem_out, sem_in) = refs[7:]
    begin(own_hbm, own, sem_in.at[0])
    load_pieces(pos, pieces, codes, half, (0, blocks.wide), row_target(held, blocks, rows), sem)
    starts = [sum(chunks[:i]) for i in range(len(chunks))]
    places_in = [other.at[pl.ds(start, size), :] for start, size in zip(starts, chunks)]
    for i, (ref, place) in enumerate(zip(arrived, places_in)):
        begin(ref, place, sem_in.at[i + 1])
    finish(own_hbm, own, sem_in.at[0])
    for i, (ref, place) in enumerate(zip(arrived, places_in)):
        finish(ref, place, sem_in.at[i + 1])
    begin(other, outs[6], sem_out.at[6])
    for i in range(length // CHUNK):
        part = pl.ds(i * CHUNK, CHUNK)
        unit, _ = normed(own[part, :].astype(FULL))
        h_own[part, :] = (unit * gains[0:1, :]).astype(LOW)
        unit, _ = normed(other[part, :].astype(FULL))
        h_oth[part, :] = (unit * gains[1:2, :]).astype(LOW)
        row = lax.broadcasted_iota(jnp.int32, (CHUNK, length), 0) + i * CHUNK
        col = lax.broadcasted_iota(jnp.int32, (CHUNK, length), 1)
        ok = (page_col[part, :] == page_row[...]) & ((mask_row[...] == 1) | (row == col))
        allowed[part, :] = jnp.where(ok, 1.0, 0.0)
    wait_whole(held, sem)
    merge_tiles(held, weight, blocks)
    begin(weight, outs[5], sem_out.at[5])
    lse_out[...] = jnp.zeros_like(lse_out)

    q_out[...] = (matmul(h_own[...], weight[:, :width]).astype(LOW) * factor).astype(LOW)
    k_out[...] = matmul(h_oth[...], weight[:, width : 2 * width]).astype(LOW)
    v_out[...] = matmul(h_oth[...], weight[:, 2 * width :]).astype(LOW)
    for i in range(3):
        begin(kept[i], outs[i], sem_out.at[i])
    size = width // HEADS
    per = LANES // size

    @pl.loop(0, width // LANES)
    def _(pair):
        cols = pl.ds(pl.multiple_of(pair * LANES, LANES), LANES)
        keys, values, queries = k_out[:, cols], v_out[:, cols], q_out[:, cols]
        lane = lax.broadcasted_iota(jnp.int32, queries.shape, 1)
        result, sums = None, lse_out[...]
        for sub in range(per):
            inside = lane // size == sub
            scores = matmul_nt(jnp.where(inside, queries, jnp.zeros_like(queries)), keys)
            scores = jnp.where(allowed[...] > 0.5, scores, NEG)
            top = jnp.max(scores, axis=-1, keepdims=True)
            exps = jnp.exp(scores - top)
            total = jnp.sum(exps, axis=-1, keepdims=True)
            out = matmul(exps.astype(LOW), values) * (1.0 / total)
            result = out if result is None else jnp.where(inside, out, result)
            sums = jnp.where(lane == pair * per + sub, top + jnp.log(total), sums)
        lse_out[...] = sums
        att_out[:, cols] = result.astype(LOW)

    for i in (3, 4):
        begin(kept[i], outs[i], sem_out.at[i])
    for i, ref in enumerate(kept):
        finish(ref, outs[i], sem_out.at[i])


def feed_kernel(shape, pos, coef, gain, page_col, att_hbm, own_hbm, cot_hbm, cotj_hbm, arrived_hbm, *refs):
    (codes, counts, sums_b, sums_c, half, rows, down_rows, ups, outs, downs, length, width, hidden, block) = shape
    pieces, refs = refs[: len(codes)], refs[len(codes) :]
    out_ref, dmid_ref, datt_ref, away_ref, dgain_ref = refs[:5]
    up_targets, down_targets = refs[5:7], refs[7:9]
    (w_up, o_held, w_out, d_held, w_down, g_up, g_out, g_down, att, own, cot, cotj_own, cotj_oth, mid, h2, h2_t, dffn, dffn_t,
     att_t, acts, dpre, acc, dacc, dbranch, sem_up, sem_out, sem_down, sem_gup, sem_gdown, sems) = refs[9:]
    begin(att_hbm, att, sems.at[0])
    last = counts
    load_pieces(pos, pieces[:last], codes[:last], half, (ups.wide, outs.wide), row_target(o_held, outs, rows), sem_out)
    begin(own_hbm, own, sems.at[1])
    begin(cot_hbm, cot, sems.at[2])
    begin(cotj_hbm, cotj_own, sems.at[3])
    begin(arrived_hbm, cotj_oth, sems.at[4])
    load_pieces(pos, pieces[:last], codes[:last], half, (0, ups.wide), row_target(w_up, ups, rows), sem_up)
    folds = down_rows // rows
    load_folded(pos, pieces[last:], codes[last:], half, rows, downs, 0, folds, d_held, sem_down)
    half_rows = length // 2
    parts = length // CHUNK

    def valid_at(part):
        return jnp.where(page_col[part, :] >= 0, 1.0, 0.0)

    finish(att_hbm, att, sems.at[0])
    wait_whole(o_held, sem_out)
    merge_tiles(o_held, w_out, outs)
    mid[...] = matmul(att[...], w_out[...])
    att_t[...] = att[...].T
    finish(own_hbm, own, sems.at[1])
    for i in range(parts):
        part = pl.ds(i * CHUNK, CHUNK)
        middle = own[part, :].astype(FULL) + valid_at(part) * mid[part, :]
        mid[part, :] = middle
        unit, _ = normed(middle)
        h2[part, :] = (unit * gain[...]).astype(LOW)
    finish(cot_hbm, cot, sems.at[2])
    finish(cotj_hbm, cotj_own, sems.at[3])
    finish(arrived_hbm, cotj_oth, sems.at[4])
    for which, ref in ((pos[2], cotj_own), (1 - pos[2], cotj_oth)):
        for i in range(half_rows // CHUNK):
            part = pl.ds(pl.multiple_of(which * half_rows + i * CHUNK, CHUNK), CHUNK)
            grad = cot[part, :] + coef[...] * ref[pl.ds(i * CHUNK, CHUNK), :].astype(FULL)
            cot[part, :] = grad
            dffn[part, :] = (grad * valid_at(part)).astype(LOW)
    dffn_t[...] = dffn[...].T
    h2_t[...] = h2[...].T
    acc[...] = jnp.zeros_like(acc)
    dacc[...] = jnp.zeros_like(dacc)
    wait_whole(w_up, sem_up)
    wait_whole(d_held, sem_down)
    if not downs.aligned:
        merge_tiles(d_held, w_down, downs)
    down = d_held if downs.aligned else w_down
    c0, c1 = 0.7978845608028654, 0.044715

    @pl.loop(0, hidden // block)
    def _(f):
        cols = pl.ds(pl.multiple_of(f * block, LANES), block)
        pre = matmul(h2[...], w_up[:, cols])
        dact = matmul(dffn[...], down[:, cols])
        square = pre * pre
        flat = jnp.tanh(c0 * (pre + c1 * square * pre))
        cdf = 0.5 * (1.0 + flat)
        slope = cdf + pre * (0.5 * (1.0 - flat * flat)) * (c0 * (1.0 + 3.0 * c1 * square))
        acts[...] = (pre * cdf).astype(LOW)
        dpre[...] = (slope * dact).astype(LOW)
        acc[...] += matmul_nt(acts[...], down[:, cols])
        dacc[...] += matmul_nt(dpre[...], w_up[:, cols])
        g_down[:, cols] = matmul(dffn_t[...], acts[...]).astype(LOW)
        g_up[:, cols] = matmul(h2_t[...], dpre[...]).astype(LOW)

    if downs.room > downs.total:
        g_down[:, downs.total :] = jnp.zeros((width, downs.room - downs.total), LOW)
    store_pieces(
        pos,
        lambda doc, inner: g_down.at[
            pl.ds(pl.multiple_of(doc * down_rows, down_rows), down_rows),
            pl.ds(downs.start_dynamic(inner), downs.wide),
        ],
        sums_c, half, down_targets, (0, downs.wide), sem_gdown,
    )
    store_pieces(
        pos,
        lambda doc, inner: g_up.at[
            pl.ds(pl.multiple_of(inner * rows, rows), rows),
            pl.ds(ups.start_dynamic(doc), ups.wide),
        ],
        sums_b, half, up_targets, (0, ups.wide), sem_gup,
    )
    dgain_ref[...] = jnp.zeros_like(dgain_ref)
    for i in range(parts):
        part = pl.ds(i * CHUNK, CHUNK)
        valid = valid_at(part)
        middle = mid[part, :]
        acc[part, :] = middle + valid * acc[part, :]
        unit, scale = normed(middle)
        grad = dacc[part, :]
        dgain_ref[pl.ds(2 + pos[2], 1), :] += jnp.sum(grad * unit, axis=0, keepdims=True)
        dmid = cot[part, :] + norm_back(grad, unit, scale, gain[...])
        dacc[part, :] = dmid
        dbranch[part, :] = (dmid * valid).astype(LOW)
    begin(acc, out_ref, sems.at[0])
    begin(dacc, dmid_ref, sems.at[1])
    h2[...] = matmul_nt(dbranch[...], w_out[...]).astype(LOW)
    begin(h2, datt_ref, sems.at[2])
    g_out[:, : outs.total] = matmul(att_t[...], dbranch[...]).astype(LOW)
    if outs.room > outs.total:
        g_out[:, outs.total :] = jnp.zeros((width, outs.room - outs.total), LOW)
    store_pieces(
        pos,
        lambda doc, inner: g_out.at[
            pl.ds(pl.multiple_of(inner * rows, rows), rows),
            pl.ds(outs.start_dynamic(doc), outs.wide),
        ],
        sums_b, half, up_targets, (ups.wide, outs.wide), sem_gup,
    )
    for i in range(half_rows // CHUNK):
        part = pl.ds(pl.multiple_of((1 - pos[2]) * half_rows + i * CHUNK, CHUNK), CHUNK)
        away_ref[pl.ds(i * CHUNK, CHUNK), :] = acc[part, :].astype(LOW)
    for target in down_targets:
        wait_whole(target, sem_gdown)
    for target in up_targets:
        wait_whole(target, sem_gup)
    finish(acc, out_ref, sems.at[0])
    finish(dacc, dmid_ref, sems.at[1])
    finish(h2, datt_ref, sems.at[2])


def scores_back(shape, pairs, page_col, page_row, mask_row, sources, scratch, more_loads):
    length, width, factor = shape
    q_hbm, k_hbm, v_hbm, att_hbm, datt_hbm, lse_hbm = sources
    (q_ref, k_ref, v_ref, att, datt, lse, dq, dk, dv, allowed, lse_t, dots_t, sems) = scratch
    size = width // HEADS
    per = LANES // size
    cols_here = pl.ds(pairs[0] * LANES, (pairs[1] - pairs[0]) * LANES)
    loads = [(source.at[:, cols_here], target) for source, target in
             ((datt_hbm, datt), (att_hbm, att), (q_hbm, q_ref), (k_hbm, k_ref), (v_hbm, v_ref))]
    loads.append((lse_hbm, lse))
    for i, (source, target) in enumerate(loads):
        begin(source, target, sems.at[i])
    more_loads()
    mask = jnp.broadcast_to(mask_row[...].astype(FULL), (LANES, length)).T[:, 0:1]
    row = lax.broadcasted_iota(jnp.int32, (length, length), 0)
    col = lax.broadcasted_iota(jnp.int32, (length, length), 1)
    ok = (page_col[...] == page_row[...]) & ((mask == 1.0) | (row == col))
    allowed[...] = jnp.where(ok, 1.0, 0.0)
    here_width = cols_here.size
    head = lax.broadcasted_iota(jnp.int32, (LANES, here_width), 0)
    lane = lax.broadcasted_iota(jnp.int32, (LANES, here_width), 1)
    chosen = jnp.where(lane // size == head, 1.0, 0.0)
    for i, (source, target) in enumerate(loads):
        finish(source, target, sems.at[i])
    dots_t[...] = lax.dot_general(
        chosen, att[...].astype(FULL) * datt[...].astype(FULL), (((1,), (1,)), ((), ())),
        preferred_element_type=FULL, precision=lax.Precision.HIGHEST,
    )
    lse_t[...] = lse[...].T

    @pl.loop(0, pairs[1] - pairs[0])
    def _(pair):
        cols = pl.ds(pl.multiple_of(pair * LANES, LANES), LANES)
        queries, grads = q_ref[:, cols], datt[:, cols]
        keys, values = k_ref[:, cols], v_ref[:, cols]
        lane = lax.broadcasted_iota(jnp.int32, (length, LANES), 1)
        zero = jnp.zeros_like(queries)
        trio = None
        for sub in range(per):
            inside = lane // size == sub
            lse_row = lse_t[pl.ds((pair + pairs[0]) * per + sub, 1), :]
            dot_row = dots_t[pl.ds(pair * per + sub, 1), :]
            scores = matmul_nt(keys, jnp.where(inside, queries, zero))
            scores = jnp.where(allowed[...] > 0.5, scores, NEG)
            probs = jnp.exp(scores - lse_row)
            dprob = matmul_nt(values, jnp.where(inside, grads, zero))
            low = (probs * (dprob - dot_row)).astype(LOW)
            three = (matmul_tn(low, keys), matmul(low, queries), matmul(probs.astype(LOW), grads))
            trio = three if trio is None else [jnp.where(inside, new, old) for new, old in zip(three, trio)]
        dq[:, cols] = (trio[0] * factor).astype(LOW)
        dk[:, cols] = trio[1].astype(LOW)
        dv[:, cols] = trio[2].astype(LOW)


def scores_back_kernel(shape, pairs, page_col, page_row, mask_row, *refs):
    sources, outs, scratch = refs[:6], refs[6:9], refs[9:]
    scores_back(shape, pairs, page_col, page_row, mask_row, sources, scratch, lambda: None)
    made, sems = scratch[6:9], scratch[-1]
    for i, (source, target) in enumerate(zip(made, outs)):
        begin(source, target, sems.at[i])
    for i, (source, target) in enumerate(zip(made, outs)):
        finish(source, target, sems.at[i])


def project_back_kernel(
    shape, pairs, factor, pos, gains, page_col, page_row, mask_row, own_hbm, other_hbm, weight_hbm, *refs
):
    (sums, half, rows, blocks, length, width, runs) = shape
    sources, refs = refs[:6], refs[6:]
    given, refs = refs[: 3 * (len(runs) - 1)], refs[3 * (len(runs) - 1) :]
    own_out, oth_ref, dgain_ref = refs[:3]
    targets, refs = refs[3:5], refs[5:]
    h_t, flat, own_ref, grad, own, other, weight, sem, sems = refs[:9]
    copies, scratch = refs[9 : 9 + len(given)], refs[9 + len(given) :]
    grads = [copies[3 * i : 3 * i + 3] for i in range(len(runs) - 1)] + [scratch[6:9]]
    parts = length // CHUNK
    loads = [(own_hbm, own), (other_hbm, other), *zip(given, copies), (weight_hbm, weight)]

    def begin_loads():
        for i, (source, target) in enumerate(loads):
            begin(source, target, sems.at[i])

    scores_back((length, width, factor), pairs, page_col, page_row, mask_row, sources, scratch, begin_loads)

    def take(i):
        finish(*loads[i], sems.at[i])

    for which, source in ((0, own), (1, other)):
        take(which)
        for i in range(parts):
            part = pl.ds(i * CHUNK, CHUNK)
            unit, _ = normed(source[part, :].astype(FULL))
            flat[part, :] = unit * gains[which : which + 1, :]
        h_t[which] = flat[...].astype(LOW).T
    for i in range(2, len(loads) - 1):
        take(i)
    for (low, high), trio in zip(runs, grads):
        for block, (which, ref) in enumerate(zip((0, 1, 1), trio)):
            grad[:, block * width + low : block * width + high] = matmul(h_t[which], ref[...]).astype(LOW)
    if blocks.room > blocks.total:
        grad[:, blocks.total :] = jnp.zeros((width, blocks.room - blocks.total), LOW)
    store_pieces(
        pos,
        lambda doc, inner: grad.at[
            pl.ds(pl.multiple_of(inner * rows, rows), rows),
            pl.ds(blocks.start_dynamic(doc), blocks.wide),
        ],
        sums, half, targets, (0, blocks.wide), sem,
    )
    dgain_ref[...] = jnp.zeros_like(dgain_ref)
    take(len(loads) - 1)
    own_ref[...] = sum(
        matmul_nt(trio[0][...], weight[:, low:high]) for (low, high), trio in zip(runs, grads)
    )
    begin(own_ref, own_out, sems.at[0])
    flat[...] = sum(
        matmul_nt(trio[block][...], weight[:, block * width + low : block * width + high])
        for (low, high), trio in zip(runs, grads)
        for block in (1, 2)
    )
    for i in range(parts):
        part = pl.ds(i * CHUNK, CHUNK)
        unit, _ = normed(own[part, :].astype(FULL))
        dgain_ref[pl.ds(pos[2], 1), :] += jnp.sum(own_ref[part, :] * unit, axis=0, keepdims=True)
        unit, _ = normed(other[part, :].astype(FULL))
        value = flat[part, :]
        oth_ref[part, :] = value.astype(LOW)
        dgain_ref[pl.ds(1 - pos[2], 1), :] += jnp.sum(value * unit, axis=0, keepdims=True)
    finish(own_ref, own_out, sems.at[0])
    for target in targets:
        wait_whole(target, sem)


def tail_kernel(length, own, gain, mine, theirs, dmid, out_ref):
    for i in range(length // CHUNK):
        part = pl.ds(i * CHUNK, CHUNK)
        unit, scale = normed(own[part, :].astype(FULL))
        grad = mine[part, :] + theirs[part, :].astype(FULL)
        out_ref[part, :] = dmid[part, :] + norm_back(grad, unit, scale, gain[...])


VMEM = pl.BlockSpec(memory_space=pltpu.VMEM)
HBM = pl.BlockSpec(memory_space=pltpu.HBM)
SMEM = pl.BlockSpec(memory_space=pltpu.SMEM)


LITTLE = pl.CostEstimate(flops=1_000, bytes_accessed=1_000, transcendentals=0)


def params(mebibytes):
    return pltpu.CompilerParams(vmem_limit_bytes=mebibytes * 1024 * 1024)


def adam_update(weight, first, second, grad, rate, decay):
    first_new = 0.9 * first + 0.1 * grad
    second_new = 0.999 * second + 0.001 * grad * grad
    first_hat = first_new / (1.0 - 0.9**STEP)
    second_hat = second_new / (1.0 - 0.999**STEP)
    weight_new = weight - rate * (first_hat / (jnp.sqrt(second_hat) + 1e-08) + decay * weight)
    return (weight_new, first_new, second_new)


def shards(
    rows, cot_stream, cot_joined, page, key_mask,
    w_qkv, m_qkv, v_qkv, w_out, m_out, v_out, w_up, m_up, v_up, w_down, m_down, v_down,
    gains, m_gains, v_gains,
):
    docs, wide = lax.axis_size("docs"), lax.axis_size("wide")
    half = wide // 2
    doc, place = lax.axis_index("docs"), lax.axis_index("wide")
    stream = place // half
    is_text = stream == 0
    pos = jnp.stack((doc, place % half, stream)).astype(jnp.int32)
    length, width = rows.shape
    half_rows = length // 2
    factor = float(width // HEADS) ** (-0.5)
    piece_rows = w_qkv.shape[1]
    hidden = w_up.shape[2] * docs
    qkvs, outs, ups = Blocks(docs, w_qkv.shape[2]), Blocks(docs, w_out.shape[2]), Blocks(docs, w_up.shape[2])
    downs = Blocks(wide, w_down.shape[1])
    down_rows = w_down.shape[2]

    core = [("wide", 1)]
    along_x = [("docs", 1)]
    along_y = [("docs", 1 << b) for b in range(1, docs.bit_length() - 1)]
    along_z = [("wide", 1 << b) for b in range(1, half.bit_length() - 1)]
    across = ("wide", half)

    def swap(value):
        return flip(value, *across)

    column = doc * w_qkv.shape[2] + lax.iota(jnp.int32, w_qkv.shape[2])
    is_query = (column < width)[None, None, :]
    pair_qkv = jnp.where(is_query, w_qkv, w_qkv[::-1]).astype(LOW)

    def own_first(pair):
        return jnp.where(is_text, pair, pair[::-1])

    unit_a = qkvs.pad(own_first(pair_qkv), doc)
    unit_b = jnp.concatenate(
        (ups.pad(own_first(w_up.astype(LOW)), doc), outs.pad(own_first(w_out.astype(LOW)), doc)), axis=-1
    )
    unit_c = downs.pad(jnp.swapaxes(own_first(w_down.astype(LOW)), 1, 2), place)
    folds = down_rows // piece_rows

    def folded(unit):
        return jnp.concatenate([unit[i * piece_rows : (i + 1) * piece_rows] for i in range(folds)], axis=-1)

    page_col, page_row = page[:, None], page[None, :]
    mask_row = key_mask[None, :]
    gain_own = lax.dynamic_index_in_dim(gains, stream, 0, keepdims=True)
    gain_oth = lax.dynamic_index_in_dim(gains, 1 - stream, 0, keepdims=True)
    gain_one = jnp.concatenate((gain_own, gain_oth), axis=0)
    gain_two = lax.dynamic_index_in_dim(gains, 2 + stream, 0, keepdims=True)
    mix = jax.nn.sigmoid(gains[4])[None, :]
    coef = jnp.where(is_text, mix, 1.0 - mix)

    cot_low = cot_joined.astype(LOW)
    unit_a_oth = swap(unit_a[1])
    unit_b_oth = swap(after(unit_b[1], unit_a_oth)) if FIRST_A else swap(unit_b[1])
    if downs.aligned:
        unit_c_oth = swap(after(unit_c[1], unit_a_oth))
    else:
        raw = jnp.swapaxes(own_first(w_down.astype(LOW)), 1, 2)
        unit_c_oth = downs.pad(swap(raw[1]), (place + half) % wide)
    zxy, zyx = along_z + along_x + along_y, along_z + along_y + along_x
    a_own, a_oth = Doubling(unit_a[0], 0, zxy), Doubling(unit_a_oth, 1, zyx)
    b_own = Doubling(unit_b[0], 0, along_y + along_x + along_z)
    c_own = Doubling(folded(unit_c[0]), 0, along_y + along_z + along_x)
    b_oth, c_oth = Doubling(unit_b_oth, 1, zxy), Doubling(folded(unit_c_oth), 1, zyx)
    steps_y, steps_x = len(along_y), len(along_x)
    chunks, begin = [], 0
    for size in [length * part // sum(ROW_PARTS) for part in ROW_PARTS]:
        some = rows[begin : begin + size]
        chunks.append(swap(after(some, chunks[-1] if chunks else unit_a_oth)))
        begin += size
    for _ in range(steps_y):
        b_own.send()
    for _ in range(steps_y):
        c_own.send()
    for _ in range(steps_x):
        b_own.send(unit_a_oth)
    for _ in along_z:
        c_own.send(unit_a_oth)
    a_own.send_all()
    a_oth.send_all()
    first = (a_oth.arrays[len(along_z) + steps_y], a_own.arrays[len(along_z) + steps_x])
    rest = (a_oth.arrays[-1], a_own.arrays[-1])
    for one in (b_oth, c_oth):
        for _ in along_z:
            one.send(*first, page_col, gain_one, gain_two, coef, cot_low)
    met = b_oth.last + c_oth.last
    for one in (b_own, c_own):
        while one.step < len(one.order):
            one.send(*met)
    for one, steps in ((b_oth, steps_x), (c_oth, steps_y)):
        for _ in range(steps):
            one.send(*rest, chunks[1])
    for one in (b_oth, c_oth):
        while one.step < len(one.order):
            one.send(chunks[-1])
    pieces_a, codes_a = [], []
    for one in (a_own, a_oth):
        for value, known in one.split_newest():
            one.add(value, known, *core[0])
        pieces_a += one.arrays
        codes_a += one.slotted()
    waiting, passed = [], []
    for one in (b_own, b_oth, c_own, c_oth):
        early, late = one.split_newest()
        passed.append(one.add(after(early[0], chunks[-1]), early[1], *core[0]))
        waiting.append((one, *late))
    other_joined = swap(after(cot_low, chunks[-1], *passed))

    low_rows = jax.ShapeDtypeStruct((length, width), LOW)
    full_rows = jax.ShapeDtypeStruct((length, width), FULL)

    sizes = tuple(chunk.shape[0] for chunk in chunks)
    shape = (codes_a, half, piece_rows, qkvs, length, width, factor, sizes)
    made = (low_rows, low_rows, low_rows, low_rows, jax.ShapeDtypeStruct((length, LANES), FULL),
            jax.ShapeDtypeStruct((width, 3 * width), LOW), low_rows)
    queries, keys, values, attended, lse, weight_qkv, other_rows = pl.pallas_call(
        functools.partial(project_kernel, shape),
        out_shape=made,
        in_specs=[SMEM] + [VMEM] * 4 + [HBM] * (1 + len(chunks) + len(pieces_a)),
        out_specs=(HBM,) * 7,
        scratch_shapes=[pltpu.VMEM(one.shape, one.dtype) for one in made] + [
            pltpu.VMEM((length, width), LOW),
            pltpu.VMEM((docs, width, qkvs.wide), LOW),
            pltpu.VMEM((length, width), LOW),
            pltpu.VMEM((length, width), LOW),
            pltpu.VMEM((length, length), FULL),
            pltpu.SemaphoreType.DMA,
            pltpu.SemaphoreType.DMA((7,)),
            pltpu.SemaphoreType.DMA((1 + len(chunks),)),
        ],
        compiler_params=params(60),
        cost_estimate=LITTLE,
        name="project_attend",
    )(pos, gain_one, page_col, page_row, mask_row, rows, *chunks, *pieces_a)

    here = [value for _, value, _ in waiting]
    for one, value, known in waiting:
        one.add(after(value, lse, other_joined, *here), known, *core[0])
    streams = (b_own, b_oth, c_own, c_oth)
    pieces_b = sum((one.arrays for one in streams), [])
    codes_b = sum((one.slotted() for one in streams), [])
    counts = len(b_own.arrays) + len(b_oth.arrays)
    xy, yx = along_x + along_y, along_y + along_x
    steps_b = [core * 2, *zip(xy, yx), *((step, step) for step in along_z)]
    steps_c = [core * 2, *((step, step) for step in along_z), *zip(xy, yx)]
    sums_of = [tuple(sum_codes([pair[slot] for pair in steps]) for slot in (0, 1)) for steps in (steps_b, steps_c)]
    sent_count = len(sums_of[0][0])
    block = 8 * LANES
    shape = (codes_b, counts, *sums_of, half, piece_rows, down_rows, ups, outs, downs, length, width, hidden, block)
    shape_b = jax.ShapeDtypeStruct((sent_count, piece_rows, ups.wide + outs.wide), LOW)
    shape_c = jax.ShapeDtypeStruct((sent_count, down_rows, downs.wide), LOW)
    (stream_out, middle_grad, attended_grad, away, dgain_two, kept_b, sent_b, kept_c, sent_c) = pl.pallas_call(
        functools.partial(feed_kernel, shape),
        out_shape=(full_rows, full_rows, low_rows, jax.ShapeDtypeStruct((half_rows, width), LOW),
                   jax.ShapeDtypeStruct((8, width), FULL), shape_b, shape_b, shape_c, shape_c),
        in_specs=[SMEM] + [VMEM] * 3 + [HBM] * (5 + len(pieces_b)),
        out_specs=(HBM,) * 3 + (VMEM,) * 2 + (HBM,) * 4,
        scratch_shapes=[
            pltpu.VMEM((width, hidden), LOW),
            pltpu.VMEM(held_shape(outs, width), LOW),
            pltpu.VMEM((width, width), LOW),
            pltpu.VMEM(held_shape(downs, width), LOW),
            pltpu.VMEM((8, LANES) if downs.aligned else (width, hidden), LOW),
            pltpu.VMEM((width, hidden), LOW),
            pltpu.VMEM((width, outs.room), LOW),
            pltpu.VMEM((width, downs.room), LOW),
            pltpu.VMEM((length, width), LOW),
            pltpu.VMEM((length, width), LOW),
            pltpu.VMEM((length, width), FULL),
            pltpu.VMEM((half_rows, width), FULL),
            pltpu.VMEM((half_rows, width), LOW),
            pltpu.VMEM((length, width), FULL),
            pltpu.VMEM((length, width), LOW),
            pltpu.VMEM((width, length), LOW),
            pltpu.VMEM((length, width), LOW),
            pltpu.VMEM((width, length), LOW),
            pltpu.VMEM((width, length), LOW),
            pltpu.VMEM((length, block), LOW),
            pltpu.VMEM((length, block), LOW),
            pltpu.VMEM((length, width), FULL),
            pltpu.VMEM((length, width), FULL),
            pltpu.VMEM((length, width), LOW),
        ] + [pltpu.SemaphoreType.DMA] * 5 + [pltpu.SemaphoreType.DMA((5,))],
        compiler_params=params(60),
        cost_estimate=LITTLE,
        name="feed_forward_back",
    )(pos, coef, gain_two, page_col, attended, rows, cot_stream, cot_joined, other_joined, *pieces_b)

    def attend_scratch(pairs):
        piece = pltpu.VMEM((length, (pairs[1] - pairs[0]) * LANES), LOW)
        return [piece] * 5 + [pltpu.VMEM((length, LANES), FULL)] + [piece] * 3 + [
            pltpu.VMEM((length, length), FULL),
            pltpu.VMEM((LANES, length), FULL),
            pltpu.VMEM((LANES, length), FULL),
            pltpu.SemaphoreType.DMA((6,)),
        ]

    def attend_back(pairs, *operands):
        low_cols = jax.ShapeDtypeStruct((length, (pairs[1] - pairs[0]) * LANES), LOW)
        return pl.pallas_call(
            functools.partial(scores_back_kernel, (length, width, factor), pairs),
            out_shape=(low_cols,) * 3,
            in_specs=[VMEM] * 3 + [HBM] * 6,
            out_specs=(HBM,) * 3,
            scratch_shapes=attend_scratch(pairs),
            compiler_params=params(60),
            cost_estimate=LITTLE,
            name="attend_back",
        )(page_col, page_row, mask_row, *operands)

    sums_b, sums_c = Halving(kept_b, sent_b, steps_b), Halving(kept_c, sent_c, steps_c)
    sums_b.send()
    sums_c.send()
    partner_rows = swap(away)
    pair_count = width // LANES
    cuts = (0, pair_count * 2 // 3, pair_count)
    grads_one = attend_back(cuts[:2], queries, keys, values, attended, attended_grad, lse)
    met = (*sums_b.last, *sums_c.last, partner_rows)
    second = after(queries, grads_one[0], *met)
    sums_b.hold(grads_one[0])
    sums_c.hold(grads_one[0])
    sums_b.send(*met)
    sums_c.send(*met[:-1])
    runs = tuple((low * LANES, high * LANES) for low, high in zip(cuts[:-1], cuts[1:]))
    shape = (sums_of[0], half, piece_rows, qkvs, length, width, runs)
    shape_a = jax.ShapeDtypeStruct((sent_count, piece_rows, qkvs.wide), LOW)
    own_part, away_part, dgain_one, kept_a, sent_a = pl.pallas_call(
        functools.partial(project_back_kernel, shape, cuts[1:], factor),
        out_shape=(full_rows, low_rows, jax.ShapeDtypeStruct((8, width), FULL)) + (shape_a,) * 2,
        in_specs=[SMEM] + [VMEM] * 4 + [HBM] * (6 + 3 * len(runs)),
        out_specs=(HBM,) + (VMEM,) * 2 + (HBM,) * 2,
        scratch_shapes=[
            pltpu.VMEM((2, width, length), LOW),
            pltpu.VMEM((length, width), FULL),
            pltpu.VMEM((length, width), FULL),
            pltpu.VMEM((width, qkvs.room), LOW),
            pltpu.VMEM((length, width), LOW),
            pltpu.VMEM((length, width), LOW),
            pltpu.VMEM((width, 3 * width), LOW),
            pltpu.SemaphoreType.DMA,
            pltpu.SemaphoreType.DMA((3 * len(runs),)),
        ] + [pltpu.VMEM((length, high - low), LOW) for low, high in runs[:-1] for _ in range(3)] + attend_scratch(cuts[1:]),
        compiler_params=params(60),
        cost_estimate=LITTLE,
        name="project_back",
    )(pos, gain_one, page_col, page_row, mask_row, rows, other_rows, weight_qkv,
      second, keys, values, attended, attended_grad, lse, *grads_one)

    own_rows = lax.dynamic_slice_in_dim(stream_out, stream * half_rows, half_rows, 0)
    partner_rows = partner_rows.astype(FULL)
    text_rows = jnp.where(is_text, own_rows, partner_rows)
    image_rows = jnp.where(is_text, partner_rows, own_rows)
    joined_rows = mix * text_rows + (1.0 - mix) * image_rows
    gate_grad = jnp.sum(cot_joined * (text_rows - image_rows), axis=0, keepdims=True) * mix * (1.0 - mix)

    slot_index = lax.iota(jnp.int32, 5)[:, None]
    small = dgain_one[:5] + dgain_two[:5] + jnp.where(slot_index == 4, gate_grad, 0.0)
    sums_a = Halving(kept_a, sent_a, steps_b)
    sums_a.hold(*sums_b.last, *sums_c.last)
    sums_a.send()
    sums_a.rider = rider_rows(small + flip(small, *core[0]), qkvs.wide)
    back_part = swap(away_part)
    sums_a.send()
    sums_b.hold(*sums_a.messages)
    sums_b.send()
    sums_a.hold(*sums_b.messages)
    sums_a.send()
    sums_c.hold(*sums_a.messages)
    sums_c.send()
    sums_b.hold(*sums_a.messages)

    total_a, total_b, total_c = sums_a.total(), sums_b.total(), sums_c.total()

    last = total_a[1].astype(LOW)[None]
    packed = with_rider(last, sums_a.rider)
    arrived = swap(packed)
    packed_c = total_c[1].astype(LOW)
    grad_rows = pl.pallas_call(
        functools.partial(tail_kernel, length),
        out_shape=full_rows,
        in_specs=[VMEM] * 5,
        out_specs=VMEM,
        compiler_params=params(10),
        name="norm_tail",
    )(rows, gain_own, own_part, back_part, after(middle_grad, packed, packed_c))

    def both(total):
        return total[0], swap(total[1].astype(LOW))

    def placed(mine, theirs):
        theirs = theirs.astype(FULL)
        return jnp.where(is_text, jnp.stack((mine, theirs)), jnp.stack((theirs, mine)))

    mine_b, theirs_b = both(total_b)
    theirs_b = after(theirs_b, packed, packed_c)
    grad_b = placed(mine_b, theirs_b)
    grad_up = ups.cut(grad_b[..., : ups.wide], doc)
    grad_out = outs.cut(grad_b[..., ups.wide :], doc)
    out_new = adam_update(w_out, m_out, v_out, grad_out, 0.5, 0.01)
    up_new = adam_update(w_up, m_up, v_up, grad_up, 0.12, 0.01)
    if downs.aligned:
        mine_c, theirs_c = total_c[0], swap(packed_c)
    else:
        mine_c = downs.cut(total_c[0], place)
        theirs_c = swap(downs.cut(total_c[1], (place + half) % wide).astype(LOW))
    theirs_c = after(theirs_c, packed, grad_rows, up_new[0], out_new[0])
    grad_down = jnp.swapaxes(placed(mine_c, theirs_c), 1, 2)
    down_new = adam_update(w_down, m_down, v_down, grad_down, 0.06, 0.01)
    arrived = after(arrived, grad_rows, up_new[0], out_new[0], down_new[0])
    last, rider = rider_of(arrived, sums_a.rider.shape, last.shape)
    gains_grad = rider_value(kept_rider(sums_a.rider) + rider, gains.shape)
    mine_a, theirs_a = total_a[0], last[0]
    mine_a, theirs_a = qkvs.cut(mine_a, doc), qkvs.cut(theirs_a.astype(FULL), doc)
    query_here = is_query[0]
    grad_qkv = placed(
        jnp.where(query_here, mine_a, theirs_a), jnp.where(query_here, theirs_a, mine_a)
    )

    qkv_new = adam_update(w_qkv, m_qkv, v_qkv, grad_qkv, 0.12, 0.01)
    gains_new = adam_update(gains, m_gains, v_gains, gains_grad, 0.8, 0.0)
    return (stream_out, joined_rows, grad_rows, *qkv_new, *out_new, *up_new, *down_new, *gains_new)


def solution(mesh):
    by_rows = P(("docs", "wide"), None)
    by_row = P(("docs", "wide"))
    weight = P(None, "wide", "docs")
    return jax.shard_map(
        shards,
        mesh=mesh,
        in_specs=(by_rows,) * 3 + (by_row,) * 2 + (weight,) * 12 + (P(),) * 3,
        out_specs=(by_rows,) * 3 + (weight,) * 12 + (P(),) * 3,
        check_vma=False,
    )
```

```python
import functools
import math

import jax
import jax.numpy as jnp
from jax import lax
from jax.experimental import pallas as pl
from jax.experimental.pallas import tpu as pltpu
from jax.sharding import PartitionSpec as P

HEADS = 12
STEP = 10
LANES = 128
CHUNK = 128
ROW_PARTS = (5, 6, 5)
FIRST_A = False
NEG = -1000000000.0
LOW = jnp.bfloat16
FULL = jnp.float32


def flip(value, axis, mask):
    count = lax.axis_size(axis)
    return lax.ppermute(value, axis, [(i, i ^ mask) for i in range(count)])


def flipped(codes, axis, mask):
    d_mask = mask if axis == "docs" else 0
    w_mask = mask if axis == "wide" else 0
    return [(d ^ d_mask, w ^ w_mask) for d, w in codes]


def after(value, *others):
    return lax.optimization_barrier((value, *others))[0]


class Doubling:
    def __init__(self, unit, slot, order):
        self.slot, self.order, self.step = slot, order, 0
        self.arrays, self.codes = [unit[None]], [[(0, 0)]]
        self.last = ()

    def held(self):
        held = self.arrays[0] if len(self.arrays) == 1 else jnp.concatenate(self.arrays, axis=0)
        return held, [code for group in self.codes for code in group]

    def send(self, *others):
        held, known = self.held()
        if others:
            held = after(held, *others)
        axis, mask = self.order[self.step]
        self.arrays.append(flip(held, axis, mask))
        self.codes.append(flipped(known, axis, mask))
        self.step, self.last = self.step + 1, (self.arrays[-1],)

    def send_all(self):
        while self.step < len(self.order):
            self.send()

    def split_newest(self):
        newest, newest_known = self.arrays.pop(), self.codes.pop()
        held, known = self.held()
        self.arrays.append(newest)
        self.codes.append(newest_known)
        return (held, known), (newest, newest_known)

    def add(self, value, known, axis, mask):
        self.arrays.append(flip(value, axis, mask))
        self.codes.append(flipped(known, axis, mask))
        return self.arrays[-1]

    def slotted(self):
        return [(self.slot, group) for group in self.codes]


def sum_codes(order):
    codes = [(0, 0)]
    for axis, mask in reversed(order):
        codes = codes + flipped(codes, axis, mask)
    return codes


def halves_of(value):
    high = lax.reduce_precision(value, 8, 7)
    return high, lax.reduce_precision(value - high, 8, 7)


def rider_rows(value, lanes):
    rows, width = value.shape
    runs = [value[:, i : i + lanes] for i in range(0, width, lanes)]
    runs = [jnp.pad(run, ((0, -rows % 8), (0, lanes - run.shape[1]))) for run in runs]
    return jnp.concatenate(runs, axis=0)


def rider_value(laid, shape):
    rows, width = shape
    high = rows + -rows % 8
    runs = [laid[i * high : i * high + rows] for i in range(laid.shape[0] // high)]
    return jnp.concatenate(runs, axis=1)[:, :width]


def with_rider(value, rider):
    lanes = value.shape[-1]
    tail = [part.astype(LOW) for part in halves_of(rider)]
    return jnp.concatenate((value.reshape(-1, lanes), *tail), axis=0)


def rider_of(message, shape, value_shape):
    count, rows = math.prod(value_shape[:-1]), shape[0]
    parts = message[count : count + rows], message[count + rows :]
    return message[:count].reshape(value_shape), parts[0].astype(FULL) + parts[1].astype(FULL)


def kept_rider(rider):
    high, low = halves_of(rider)
    return high + low


class Halving:
    def __init__(self, kept, sent, steps):
        self.slots, self.sent, self.steps = [[half] for half in split(kept)], sent, steps
        self.step, self.last, self.messages, self.waits = 0, (), (), ()
        self.rider = None

    def left(self):
        return self.step < len(self.steps)

    def hold(self, *others):
        self.waits = self.waits + others

    def carry(self, value, axis, mask):
        if self.rider is None or self.step == 0:
            self.messages += (value,)
            return flip(value, axis, mask)
        message = with_rider(value, self.rider)
        self.messages += (message,)
        message = flip(message, axis, mask)
        value, rider = rider_of(message, self.rider.shape, value.shape)
        self.rider = kept_rider(self.rider) + rider
        return value

    def part_sums(self):
        outgoing = []
        for slot, parts in enumerate(self.slots):
            if self.waits:
                parts = parts[:-1] + [after(parts[-1], *self.waits)]
            half = parts[0].shape[0] // 2
            outgoing.append(sum(part[half:].astype(FULL) for part in parts).astype(LOW))
            self.slots[slot] = [part[:half] for part in parts]
        return outgoing

    def send(self, *others):
        one, two = self.steps[self.step]
        self.messages = ()
        if self.step == 0:
            whole = after(self.sent, *self.waits) if self.waits else self.sent
        else:
            outgoing = self.part_sums()
            if others:
                outgoing = [after(value, *others) for value in outgoing]
            whole = jnp.concatenate(outgoing, axis=0) if one == two else None
        if one == two:
            arrived = self.carry(whole, *one)
            self.last = (arrived,)
            arrived = split(arrived)
        else:
            arrived = [self.carry(outgoing[0], *one), flip(outgoing[1], *two)]
            self.messages += (outgoing[1],)
            self.last = tuple(arrived)
        self.slots = [parts + [new] for parts, new in zip(self.slots, arrived)]
        self.step, self.waits = self.step + 1, ()

    def total(self):
        while self.left():
            self.send()
        slots = [parts[:-1] + [after(parts[-1], *self.waits)] if self.waits else parts for parts in self.slots]
        return tuple(sum(part[0].astype(FULL) for part in parts) for parts in slots)


def split(value):
    middle = value.shape[0] // 2
    return [value[:middle], value[middle:]]


class Blocks:
    def __init__(self, count, size):
        self.count, self.size = count, size
        shifts = [(i * size) % LANES for i in range(count)]
        self.shifts = sorted(set(shifts))
        self.wide = -(-(size + max(shifts)) // LANES) * LANES
        self.aligned = max(shifts) == 0 and size % LANES == 0
        self.total = count * size
        self.room = max(self.start(i) + self.wide for i in range(count))

    def start(self, index):
        return index * self.size // LANES * LANES

    def start_dynamic(self, index):
        return pl.multiple_of(index * self.size // LANES * LANES, LANES)

    def pad(self, value, index):
        result = None
        for shift in self.shifts:
            low = [(0, 0)] * (value.ndim - 1) + [(shift, self.wide - self.size - shift)]
            placed = jnp.pad(value, low)
            here = (index * self.size) % LANES == shift
            result = placed if result is None else jnp.where(here, placed, result)
        return result

    def cut(self, value, index):
        result = None
        for shift in self.shifts:
            piece = value[..., shift : shift + self.size]
            here = (index * self.size) % LANES == shift
            result = piece if result is None else jnp.where(here, piece, result)
        return result

    def tile_owners(self, tile):
        low, high = tile * LANES, (tile + 1) * LANES
        return [
            (i, low - self.start(i))
            for i in range(self.count)
            if i * self.size < high and (i + 1) * self.size > low
        ]


def matmul(left, right):
    return lax.dot_general(left, right, (((1,), (0,)), ((), ())), preferred_element_type=FULL)


def matmul_nt(left, right):
    return lax.dot_general(left, right, (((1,), (1,)), ((), ())), preferred_element_type=FULL)


def matmul_tn(left, right):
    return lax.dot_general(left, right, (((0,), (0,)), ((), ())), preferred_element_type=FULL)


def normed(values):
    centred = values - jnp.mean(values, axis=-1, keepdims=True)
    spread = jnp.mean(centred * centred, axis=-1, keepdims=True)
    scale = lax.rsqrt(spread + 1e-05)
    return centred * scale, scale


def norm_back(grad, unit, scale, gain):
    inner = grad * gain
    mean_inner = jnp.mean(inner, axis=-1, keepdims=True)
    mean_both = jnp.mean(inner * unit, axis=-1, keepdims=True)
    return scale * (inner - mean_inner - unit * mean_both)


def rows_at(index, size=CHUNK):
    return pl.ds(pl.multiple_of(index * size, size), size)


def places(pos, slot, codes, half):
    owner = pos[2] if slot == 0 else 1 - pos[2]
    for index, (d_mask, w_mask) in enumerate(codes):
        yield index, pos[0] ^ d_mask, owner * half + (pos[1] ^ w_mask)


def load_pieces(pos, refs, codes, half, lanes, target, sem):
    for ref, (slot, group) in zip(refs, codes):
        for index, doc, inner in places(pos, slot, group, half):
            pltpu.make_async_copy(
                ref.at[index, :, pl.ds(lanes[0], lanes[1])], target(doc, inner), sem
            ).start()


def load_folded(pos, refs, codes, half, rows, blocks, begin, folds, held, sem):
    for fold in range(folds):
        def target(doc, inner):
            first = pl.ds(pl.multiple_of((doc * folds + fold) * rows, rows), rows)
            if blocks.aligned:
                return held.at[first, pl.ds(blocks.start_dynamic(inner), blocks.wide)]
            return held.at[inner, first, :]

        load_pieces(pos, refs, codes, half, (begin + fold * blocks.wide, blocks.wide), target, sem)


def begin(source, target, sem):
    pltpu.make_async_copy(source, target, sem).start()


def finish(source, target, sem):
    pltpu.make_async_copy(source, target, sem).wait()


def store_pieces(pos, source, sums, half, targets, lanes, sem):
    for slot, codes in enumerate(sums):
        count = len(codes) // 2
        for index, doc, inner in places(pos, slot, codes, half):
            pltpu.make_async_copy(
                source(doc, inner),
                targets[index // count].at[slot * count + index % count, :, pl.ds(lanes[0], lanes[1])],
                sem,
            ).start()


def wait_whole(ref, sem):
    pltpu.make_async_copy(ref, ref, sem).wait()


def row_target(ref, blocks, rows):
    if blocks.aligned:
        return lambda doc, inner: ref.at[
            pl.ds(pl.multiple_of(inner * rows, rows), rows),
            pl.ds(blocks.start_dynamic(doc), blocks.wide),
        ]
    return lambda doc, inner: ref.at[doc, pl.ds(pl.multiple_of(inner * rows, rows), rows), :]


def held_shape(blocks, height):
    return (height, blocks.total) if blocks.aligned else (blocks.count, height, blocks.wide)


def merge_tiles(held, whole, blocks):
    for tile in range(blocks.total // LANES):
        value = None
        for index, offset in blocks.tile_owners(tile):
            piece = held[index, :, offset : offset + LANES]
            value = piece if value is None else value + piece
        whole[:, tile * LANES : (tile + 1) * LANES] = value


def project_kernel(shape, pos, gains, page_col, page_row, mask_row, own_hbm, *refs):
    codes, half, rows, blocks, length, width, factor, chunks = shape
    arrived, refs = refs[: len(chunks)], refs[len(chunks) :]
    pieces, refs = refs[: len(codes)], refs[len(codes) :]
    outs, refs = refs[:7], refs[7:]
    (q_out, k_out, v_out, att_out, lse_out, weight, other) = kept = refs[:7]
    (own, held, h_own, h_oth, allowed, sem, sem_out, sem_in) = refs[7:]
    begin(own_hbm, own, sem_in.at[0])
    load_pieces(pos, pieces, codes, half, (0, blocks.wide), row_target(held, blocks, rows), sem)
    starts = [sum(chunks[:i]) for i in range(len(chunks))]
    places_in = [other.at[pl.ds(start, size), :] for start, size in zip(starts, chunks)]
    for i, (ref, place) in enumerate(zip(arrived, places_in)):
        begin(ref, place, sem_in.at[i + 1])
    finish(own_hbm, own, sem_in.at[0])
    for i, (ref, place) in enumerate(zip(arrived, places_in)):
        finish(ref, place, sem_in.at[i + 1])
    begin(other, outs[6], sem_out.at[6])
    for i in range(length // CHUNK):
        part = pl.ds(i * CHUNK, CHUNK)
        unit, _ = normed(own[part, :].astype(FULL))
        h_own[part, :] = (unit * gains[0:1, :]).astype(LOW)
        unit, _ = normed(other[part, :].astype(FULL))
        h_oth[part, :] = (unit * gains[1:2, :]).astype(LOW)
        row = lax.broadcasted_iota(jnp.int32, (CHUNK, length), 0) + i * CHUNK
        col = lax.broadcasted_iota(jnp.int32, (CHUNK, length), 1)
        ok = (page_col[part, :] == page_row[...]) & ((mask_row[...] == 1) | (row == col))
        allowed[part, :] = jnp.where(ok, 1.0, 0.0)
    wait_whole(held, sem)
    merge_tiles(held, weight, blocks)
    begin(weight, outs[5], sem_out.at[5])
    lse_out[...] = jnp.zeros_like(lse_out)

    q_out[...] = (matmul(h_own[...], weight[:, :width]).astype(LOW) * factor).astype(LOW)
    k_out[...] = matmul(h_oth[...], weight[:, width : 2 * width]).astype(LOW)
    v_out[...] = matmul(h_oth[...], weight[:, 2 * width :]).astype(LOW)
    for i in range(3):
        begin(kept[i], outs[i], sem_out.at[i])
    size = width // HEADS
    per = LANES // size

    @pl.loop(0, width // LANES)
    def _(pair):
        cols = pl.ds(pl.multiple_of(pair * LANES, LANES), LANES)
        keys, values, queries = k_out[:, cols], v_out[:, cols], q_out[:, cols]
        lane = lax.broadcasted_iota(jnp.int32, queries.shape, 1)
        result, sums = None, lse_out[...]
        for sub in range(per):
            inside = lane // size == sub
            scores = matmul_nt(jnp.where(inside, queries, jnp.zeros_like(queries)), keys)
            scores = jnp.where(allowed[...] > 0.5, scores, NEG)
            top = jnp.max(scores, axis=-1, keepdims=True)
            exps = jnp.exp(scores - top)
            total = jnp.sum(exps, axis=-1, keepdims=True)
            out = matmul(exps.astype(LOW), values) * (1.0 / total)
            result = out if result is None else jnp.where(inside, out, result)
            sums = jnp.where(lane == pair * per + sub, top + jnp.log(total), sums)
        lse_out[...] = sums
        att_out[:, cols] = result.astype(LOW)

    for i in (3, 4):
        begin(kept[i], outs[i], sem_out.at[i])
    for i, ref in enumerate(kept):
        finish(ref, outs[i], sem_out.at[i])


def feed_kernel(shape, pos, coef, gain, page_col, att_hbm, own_hbm, cot_hbm, cotj_hbm, arrived_hbm, *refs):
    (codes, counts, sums_b, sums_c, half, rows, down_rows, ups, outs, downs, length, width, hidden, block) = shape
    pieces, refs = refs[: len(codes)], refs[len(codes) :]
    out_ref, dmid_ref, datt_ref, away_ref, dgain_ref = refs[:5]
    up_targets, down_targets = refs[5:7], refs[7:9]
    (w_up, o_held, w_out, d_held, w_down, g_up, g_out, g_down, att, own, cot, cotj_own, cotj_oth, mid, h2, h2_t, dffn, dffn_t,
     att_t, acts, dpre, acc, dacc, dbranch, sem_up, sem_out, sem_down, sem_gup, sem_gdown, sems) = refs[9:]
    begin(att_hbm, att, sems.at[0])
    last = counts
    load_pieces(pos, pieces[:last], codes[:last], half, (ups.wide, outs.wide), row_target(o_held, outs, rows), sem_out)
    begin(own_hbm, own, sems.at[1])
    begin(cot_hbm, cot, sems.at[2])
    begin(cotj_hbm, cotj_own, sems.at[3])
    begin(arrived_hbm, cotj_oth, sems.at[4])
    load_pieces(pos, pieces[:last], codes[:last], half, (0, ups.wide), row_target(w_up, ups, rows), sem_up)
    folds = down_rows // rows
    load_folded(pos, pieces[last:], codes[last:], half, rows, downs, 0, folds, d_held, sem_down)
    half_rows = length // 2
    parts = length // CHUNK

    def valid_at(part):
        return jnp.where(page_col[part, :] >= 0, 1.0, 0.0)

    finish(att_hbm, att, sems.at[0])
    wait_whole(o_held, sem_out)
    merge_tiles(o_held, w_out, outs)
    mid[...] = matmul(att[...], w_out[...])
    att_t[...] = att[...].T
    finish(own_hbm, own, sems.at[1])
    for i in range(parts):
        part = pl.ds(i * CHUNK, CHUNK)
        middle = own[part, :].astype(FULL) + valid_at(part) * mid[part, :]
        mid[part, :] = middle
        unit, _ = normed(middle)
        h2[part, :] = (unit * gain[...]).astype(LOW)
    finish(cot_hbm, cot, sems.at[2])
    finish(cotj_hbm, cotj_own, sems.at[3])
    finish(arrived_hbm, cotj_oth, sems.at[4])
    for which, ref in ((pos[2], cotj_own), (1 - pos[2], cotj_oth)):
        for i in range(half_rows // CHUNK):
            part = pl.ds(pl.multiple_of(which * half_rows + i * CHUNK, CHUNK), CHUNK)
            grad = cot[part, :] + coef[...] * ref[pl.ds(i * CHUNK, CHUNK), :].astype(FULL)
            cot[part, :] = grad
            dffn[part, :] = (grad * valid_at(part)).astype(LOW)
    dffn_t[...] = dffn[...].T
    h2_t[...] = h2[...].T
    acc[...] = jnp.zeros_like(acc)
    dacc[...] = jnp.zeros_like(dacc)
    wait_whole(w_up, sem_up)
    wait_whole(d_held, sem_down)
    if not downs.aligned:
        merge_tiles(d_held, w_down, downs)
    down = d_held if downs.aligned else w_down
    c0, c1 = 0.7978845608028654, 0.044715

    @pl.loop(0, hidden // block)
    def _(f):
        cols = pl.ds(pl.multiple_of(f * block, LANES), block)
        pre = matmul(h2[...], w_up[:, cols])
        dact = matmul(dffn[...], down[:, cols])
        square = pre * pre
        flat = jnp.tanh(c0 * (pre + c1 * square * pre))
        cdf = 0.5 * (1.0 + flat)
        slope = cdf + pre * (0.5 * (1.0 - flat * flat)) * (c0 * (1.0 + 3.0 * c1 * square))
        acts[...] = (pre * cdf).astype(LOW)
        dpre[...] = (slope * dact).astype(LOW)
        acc[...] += matmul_nt(acts[...], down[:, cols])
        dacc[...] += matmul_nt(dpre[...], w_up[:, cols])
        g_down[:, cols] = matmul(dffn_t[...], acts[...]).astype(LOW)
        g_up[:, cols] = matmul(h2_t[...], dpre[...]).astype(LOW)

    if downs.room > downs.total:
        g_down[:, downs.total :] = jnp.zeros((width, downs.room - downs.total), LOW)
    store_pieces(
        pos,
        lambda doc, inner: g_down.at[
            pl.ds(pl.multiple_of(doc * down_rows, down_rows), down_rows),
            pl.ds(downs.start_dynamic(inner), downs.wide),
        ],
        sums_c, half, down_targets, (0, downs.wide), sem_gdown,
    )
    store_pieces(
        pos,
        lambda doc, inner: g_up.at[
            pl.ds(pl.multiple_of(inner * rows, rows), rows),
            pl.ds(ups.start_dynamic(doc), ups.wide),
        ],
        sums_b, half, up_targets, (0, ups.wide), sem_gup,
    )
    dgain_ref[...] = jnp.zeros_like(dgain_ref)
    for i in range(parts):
        part = pl.ds(i * CHUNK, CHUNK)
        valid = valid_at(part)
        middle = mid[part, :]
        acc[part, :] = middle + valid * acc[part, :]
        unit, scale = normed(middle)
        grad = dacc[part, :]
        dgain_ref[pl.ds(2 + pos[2], 1), :] += jnp.sum(grad * unit, axis=0, keepdims=True)
        dmid = cot[part, :] + norm_back(grad, unit, scale, gain[...])
        dacc[part, :] = dmid
        dbranch[part, :] = (dmid * valid).astype(LOW)
    begin(acc, out_ref, sems.at[0])
    begin(dacc, dmid_ref, sems.at[1])
    h2[...] = matmul_nt(dbranch[...], w_out[...]).astype(LOW)
    begin(h2, datt_ref, sems.at[2])
    g_out[:, : outs.total] = matmul(att_t[...], dbranch[...]).astype(LOW)
    if outs.room > outs.total:
        g_out[:, outs.total :] = jnp.zeros((width, outs.room - outs.total), LOW)
    store_pieces(
        pos,
        lambda doc, inner: g_out.at[
            pl.ds(pl.multiple_of(inner * rows, rows), rows),
            pl.ds(outs.start_dynamic(doc), outs.wide),
        ],
        sums_b, half, up_targets, (ups.wide, outs.wide), sem_gup,
    )
    for i in range(half_rows // CHUNK):
        part = pl.ds(pl.multiple_of((1 - pos[2]) * half_rows + i * CHUNK, CHUNK), CHUNK)
        away_ref[pl.ds(i * CHUNK, CHUNK), :] = acc[part, :].astype(LOW)
    for target in down_targets:
        wait_whole(target, sem_gdown)
    for target in up_targets:
        wait_whole(target, sem_gup)
    finish(acc, out_ref, sems.at[0])
    finish(dacc, dmid_ref, sems.at[1])
    finish(h2, datt_ref, sems.at[2])


def scores_back(shape, pairs, page_col, page_row, mask_row, sources, scratch, more_loads):
    length, width, factor = shape
    q_hbm, k_hbm, v_hbm, att_hbm, datt_hbm, lse_hbm = sources
    (q_ref, k_ref, v_ref, att, datt, lse, dq, dk, dv, allowed, lse_t, dots_t, sems) = scratch
    size = width // HEADS
    per = LANES // size
    cols_here = pl.ds(pairs[0] * LANES, (pairs[1] - pairs[0]) * LANES)
    loads = [(source.at[:, cols_here], target) for source, target in
             ((datt_hbm, datt), (att_hbm, att), (q_hbm, q_ref), (k_hbm, k_ref), (v_hbm, v_ref))]
    loads.append((lse_hbm, lse))
    for i, (source, target) in enumerate(loads):
        begin(source, target, sems.at[i])
    more_loads()
    mask = jnp.broadcast_to(mask_row[...].astype(FULL), (LANES, length)).T[:, 0:1]
    row = lax.broadcasted_iota(jnp.int32, (length, length), 0)
    col = lax.broadcasted_iota(jnp.int32, (length, length), 1)
    ok = (page_col[...] == page_row[...]) & ((mask == 1.0) | (row == col))
    allowed[...] = jnp.where(ok, 1.0, 0.0)
    here_width = cols_here.size
    head = lax.broadcasted_iota(jnp.int32, (LANES, here_width), 0)
    lane = lax.broadcasted_iota(jnp.int32, (LANES, here_width), 1)
    chosen = jnp.where(lane // size == head, 1.0, 0.0)
    for i, (source, target) in enumerate(loads):
        finish(source, target, sems.at[i])
    dots_t[...] = lax.dot_general(
        chosen, att[...].astype(FULL) * datt[...].astype(FULL), (((1,), (1,)), ((), ())),
        preferred_element_type=FULL, precision=lax.Precision.HIGHEST,
    )
    lse_t[...] = lse[...].T

    @pl.loop(0, pairs[1] - pairs[0])
    def _(pair):
        cols = pl.ds(pl.multiple_of(pair * LANES, LANES), LANES)
        queries, grads = q_ref[:, cols], datt[:, cols]
        keys, values = k_ref[:, cols], v_ref[:, cols]
        lane = lax.broadcasted_iota(jnp.int32, (length, LANES), 1)
        zero = jnp.zeros_like(queries)
        trio = None
        for sub in range(per):
            inside = lane // size == sub
            lse_row = lse_t[pl.ds((pair + pairs[0]) * per + sub, 1), :]
            dot_row = dots_t[pl.ds(pair * per + sub, 1), :]
            scores = matmul_nt(keys, jnp.where(inside, queries, zero))
            scores = jnp.where(allowed[...] > 0.5, scores, NEG)
            probs = jnp.exp(scores - lse_row)
            dprob = matmul_nt(values, jnp.where(inside, grads, zero))
            low = (probs * (dprob - dot_row)).astype(LOW)
            three = (matmul_tn(low, keys), matmul(low, queries), matmul(probs.astype(LOW), grads))
            trio = three if trio is None else [jnp.where(inside, new, old) for new, old in zip(three, trio)]
        dq[:, cols] = (trio[0] * factor).astype(LOW)
        dk[:, cols] = trio[1].astype(LOW)
        dv[:, cols] = trio[2].astype(LOW)


def scores_back_kernel(shape, pairs, page_col, page_row, mask_row, *refs):
    sources, outs, scratch = refs[:6], refs[6:9], refs[9:]
    scores_back(shape, pairs, page_col, page_row, mask_row, sources, scratch, lambda: None)
    made, sems = scratch[6:9], scratch[-1]
    for i, (source, target) in enumerate(zip(made, outs)):
        begin(source, target, sems.at[i])
    for i, (source, target) in enumerate(zip(made, outs)):
        finish(source, target, sems.at[i])


def project_back_kernel(
    shape, pairs, factor, pos, gains, page_col, page_row, mask_row, own_hbm, other_hbm, weight_hbm, *refs
):
    (sums, half, rows, blocks, length, width, runs) = shape
    sources, refs = refs[:6], refs[6:]
    given, refs = refs[: 3 * (len(runs) - 1)], refs[3 * (len(runs) - 1) :]
    own_out, oth_ref, dgain_ref = refs[:3]
    targets, refs = refs[3:5], refs[5:]
    h_t, flat, own_ref, grad, own, other, weight, sem, sems = refs[:9]
    copies, scratch = refs[9 : 9 + len(given)], refs[9 + len(given) :]
    grads = [copies[3 * i : 3 * i + 3] for i in range(len(runs) - 1)] + [scratch[6:9]]
    parts = length // CHUNK
    loads = [(own_hbm, own), (other_hbm, other), *zip(given, copies), (weight_hbm, weight)]

    def begin_loads():
        for i, (source, target) in enumerate(loads):
            begin(source, target, sems.at[i])

    scores_back((length, width, factor), pairs, page_col, page_row, mask_row, sources, scratch, begin_loads)

    def take(i):
        finish(*loads[i], sems.at[i])

    for which, source in ((0, own), (1, other)):
        take(which)
        for i in range(parts):
            part = pl.ds(i * CHUNK, CHUNK)
            unit, _ = normed(source[part, :].astype(FULL))
            flat[part, :] = unit * gains[which : which + 1, :]
        h_t[which] = flat[...].astype(LOW).T
    for i in range(2, len(loads) - 1):
        take(i)
    for (low, high), trio in zip(runs, grads):
        for block, (which, ref) in enumerate(zip((0, 1, 1), trio)):
            grad[:, block * width + low : block * width + high] = matmul(h_t[which], ref[...]).astype(LOW)
    if blocks.room > blocks.total:
        grad[:, blocks.total :] = jnp.zeros((width, blocks.room - blocks.total), LOW)
    store_pieces(
        pos,
        lambda doc, inner: grad.at[
            pl.ds(pl.multiple_of(inner * rows, rows), rows),
            pl.ds(blocks.start_dynamic(doc), blocks.wide),
        ],
        sums, half, targets, (0, blocks.wide), sem,
    )
    dgain_ref[...] = jnp.zeros_like(dgain_ref)
    take(len(loads) - 1)
    own_ref[...] = sum(
        matmul_nt(trio[0][...], weight[:, low:high]) for (low, high), trio in zip(runs, grads)
    )
    begin(own_ref, own_out, sems.at[0])
    flat[...] = sum(
        matmul_nt(trio[block][...], weight[:, block * width + low : block * width + high])
        for (low, high), trio in zip(runs, grads)
        for block in (1, 2)
    )
    for i in range(parts):
        part = pl.ds(i * CHUNK, CHUNK)
        unit, _ = normed(own[part, :].astype(FULL))
        dgain_ref[pl.ds(pos[2], 1), :] += jnp.sum(own_ref[part, :] * unit, axis=0, keepdims=True)
        unit, _ = normed(other[part, :].astype(FULL))
        value = flat[part, :]
        oth_ref[part, :] = value.astype(LOW)
        dgain_ref[pl.ds(1 - pos[2], 1), :] += jnp.sum(value * unit, axis=0, keepdims=True)
    finish(own_ref, own_out, sems.at[0])
    for target in targets:
        wait_whole(target, sem)


def tail_kernel(length, own, gain, mine, theirs, dmid, out_ref):
    for i in range(length // CHUNK):
        part = pl.ds(i * CHUNK, CHUNK)
        unit, scale = normed(own[part, :].astype(FULL))
        grad = mine[part, :] + theirs[part, :].astype(FULL)
        out_ref[part, :] = dmid[part, :] + norm_back(grad, unit, scale, gain[...])


VMEM = pl.BlockSpec(memory_space=pltpu.VMEM)
HBM = pl.BlockSpec(memory_space=pltpu.HBM)
SMEM = pl.BlockSpec(memory_space=pltpu.SMEM)


LITTLE = pl.CostEstimate(flops=1_000, bytes_accessed=1_000, transcendentals=0)


def params(mebibytes):
    return pltpu.CompilerParams(vmem_limit_bytes=mebibytes * 1024 * 1024)


def adam_update(weight, first, second, grad, rate, decay):
    first_new = 0.9 * first + 0.1 * grad
    second_new = 0.999 * second + 0.001 * grad * grad
    first_hat = first_new / (1.0 - 0.9**STEP)
    second_hat = second_new / (1.0 - 0.999**STEP)
    weight_new = weight - rate * (first_hat / (jnp.sqrt(second_hat) + 1e-08) + decay * weight)
    return (weight_new, first_new, second_new)


def shards(
    rows, cot_stream, cot_joined, page, key_mask,
    w_qkv, m_qkv, v_qkv, w_out, m_out, v_out, w_up, m_up, v_up, w_down, m_down, v_down,
    gains, m_gains, v_gains,
):
    docs, wide = lax.axis_size("docs"), lax.axis_size("wide")
    half = wide // 2
    doc, place = lax.axis_index("docs"), lax.axis_index("wide")
    stream = place // half
    is_text = stream == 0
    pos = jnp.stack((doc, place % half, stream)).astype(jnp.int32)
    length, width = rows.shape
    half_rows = length // 2
    factor = float(width // HEADS) ** (-0.5)
    piece_rows = w_qkv.shape[1]
    hidden = w_up.shape[2] * docs
    qkvs, outs, ups = Blocks(docs, w_qkv.shape[2]), Blocks(docs, w_out.shape[2]), Blocks(docs, w_up.shape[2])
    downs = Blocks(wide, w_down.shape[1])
    down_rows = w_down.shape[2]

    core = [("wide", 1)]
    along_x = [("docs", 1)]
    along_y = [("docs", 1 << b) for b in range(1, docs.bit_length() - 1)]
    along_z = [("wide", 1 << b) for b in range(1, half.bit_length() - 1)]
    across = ("wide", half)

    def swap(value):
        return flip(value, *across)

    column = doc * w_qkv.shape[2] + lax.iota(jnp.int32, w_qkv.shape[2])
    is_query = (column < width)[None, None, :]
    pair_qkv = jnp.where(is_query, w_qkv, w_qkv[::-1]).astype(LOW)

    def own_first(pair):
        return jnp.where(is_text, pair, pair[::-1])

    unit_a = qkvs.pad(own_first(pair_qkv), doc)
    unit_b = jnp.concatenate(
        (ups.pad(own_first(w_up.astype(LOW)), doc), outs.pad(own_first(w_out.astype(LOW)), doc)), axis=-1
    )
    unit_c = downs.pad(jnp.swapaxes(own_first(w_down.astype(LOW)), 1, 2), place)
    folds = down_rows // piece_rows

    def folded(unit):
        return jnp.concatenate([unit[i * piece_rows : (i + 1) * piece_rows] for i in range(folds)], axis=-1)

    page_col, page_row = page[:, None], page[None, :]
    mask_row = key_mask[None, :]
    gain_own = lax.dynamic_index_in_dim(gains, stream, 0, keepdims=True)
    gain_oth = lax.dynamic_index_in_dim(gains, 1 - stream, 0, keepdims=True)
    gain_one = jnp.concatenate((gain_own, gain_oth), axis=0)
    gain_two = lax.dynamic_index_in_dim(gains, 2 + stream, 0, keepdims=True)
    mix = jax.nn.sigmoid(gains[4])[None, :]
    coef = jnp.where(is_text, mix, 1.0 - mix)

    cot_low = cot_joined.astype(LOW)
    unit_a_oth = swap(unit_a[1])
    unit_b_oth = swap(after(unit_b[1], unit_a_oth)) if FIRST_A else swap(unit_b[1])
    if downs.aligned:
        unit_c_oth = swap(after(unit_c[1], unit_a_oth))
    else:
        raw = jnp.swapaxes(own_first(w_down.astype(LOW)), 1, 2)
        unit_c_oth = downs.pad(swap(raw[1]), (place + half) % wide)
    zxy, zyx = along_z + along_x + along_y, along_z + along_y + along_x
    a_own, a_oth = Doubling(unit_a[0], 0, zxy), Doubling(unit_a_oth, 1, zyx)
    b_own = Doubling(unit_b[0], 0, along_y + along_x + along_z)
    c_own = Doubling(folded(unit_c[0]), 0, along_y + along_z + along_x)
    b_oth, c_oth = Doubling(unit_b_oth, 1, zxy), Doubling(folded(unit_c_oth), 1, zyx)
    steps_y, steps_x = len(along_y), len(along_x)
    chunks, begin = [], 0
    for size in [length * part // sum(ROW_PARTS) for part in ROW_PARTS]:
        some = rows[begin : begin + size]
        chunks.append(swap(after(some, chunks[-1] if chunks else unit_a_oth)))
        begin += size
    for _ in range(steps_y):
        b_own.send()
    for _ in range(steps_y):
        c_own.send()
    for _ in range(steps_x):
        b_own.send(unit_a_oth)
    for _ in along_z:
        c_own.send(unit_a_oth)
    a_own.send_all()
    a_oth.send_all()
    first = (a_oth.arrays[len(along_z) + steps_y], a_own.arrays[len(along_z) + steps_x])
    rest = (a_oth.arrays[-1], a_own.arrays[-1])
    for one in (b_oth, c_oth):
        for _ in along_z:
            one.send(*first, page_col, gain_one, gain_two, coef, cot_low)
    met = b_oth.last + c_oth.last
    for one in (b_own, c_own):
        while one.step < len(one.order):
            one.send(*met)
    for one, steps in ((b_oth, steps_x), (c_oth, steps_y)):
        for _ in range(steps):
            one.send(*rest, chunks[1])
    for one, own in ((b_oth, b_own), (c_oth, c_own)):
        while one.step < len(one.order):
            one.send(chunks[-1], *own.last)
    pieces_a, codes_a = [], []
    for one in (a_own, a_oth):
        for value, known in one.split_newest():
            one.add(value, known, *core[0])
        pieces_a += one.arrays
        codes_a += one.slotted()
    waiting, passed = [], []
    for one in (b_own, b_oth, c_own, c_oth):
        early, late = one.split_newest()
        passed.append(one.add(after(early[0], chunks[-1]), early[1], *core[0]))
        waiting.append((one, *late))
    other_joined = swap(after(cot_low, chunks[-1], *passed))

    low_rows = jax.ShapeDtypeStruct((length, width), LOW)
    full_rows = jax.ShapeDtypeStruct((length, width), FULL)

    sizes = tuple(chunk.shape[0] for chunk in chunks)
    shape = (codes_a, half, piece_rows, qkvs, length, width, factor, sizes)
    made = (low_rows, low_rows, low_rows, low_rows, jax.ShapeDtypeStruct((length, LANES), FULL),
            jax.ShapeDtypeStruct((width, 3 * width), LOW), low_rows)
    queries, keys, values, attended, lse, weight_qkv, other_rows = pl.pallas_call(
        functools.partial(project_kernel, shape),
        out_shape=made,
        in_specs=[SMEM] + [VMEM] * 4 + [HBM] * (1 + len(chunks) + len(pieces_a)),
        out_specs=(HBM,) * 7,
        scratch_shapes=[pltpu.VMEM(one.shape, one.dtype) for one in made] + [
            pltpu.VMEM((length, width), LOW),
            pltpu.VMEM((docs, width, qkvs.wide), LOW),
            pltpu.VMEM((length, width), LOW),
            pltpu.VMEM((length, width), LOW),
            pltpu.VMEM((length, length), FULL),
            pltpu.SemaphoreType.DMA,
            pltpu.SemaphoreType.DMA((7,)),
            pltpu.SemaphoreType.DMA((1 + len(chunks),)),
        ],
        compiler_params=params(60),
        cost_estimate=LITTLE,
        name="project_attend",
    )(pos, gain_one, page_col, page_row, mask_row, rows, *chunks, *pieces_a)

    here = [value for _, value, _ in waiting]
    for one, value, known in waiting:
        one.add(after(value, lse, other_joined, *here), known, *core[0])
    streams = (b_own, b_oth, c_own, c_oth)
    pieces_b = sum((one.arrays for one in streams), [])
    codes_b = sum((one.slotted() for one in streams), [])
    counts = len(b_own.arrays) + len(b_oth.arrays)
    xy, yx = along_x + along_y, along_y + along_x
    steps_b = [core * 2, *zip(xy, yx), *((step, step) for step in along_z)]
    steps_c = [core * 2, *((step, step) for step in along_z), *zip(xy, yx)]
    sums_of = [tuple(sum_codes([pair[slot] for pair in steps]) for slot in (0, 1)) for steps in (steps_b, steps_c)]
    sent_count = len(sums_of[0][0])
    block = 8 * LANES
    shape = (codes_b, counts, *sums_of, half, piece_rows, down_rows, ups, outs, downs, length, width, hidden, block)
    shape_b = jax.ShapeDtypeStruct((sent_count, piece_rows, ups.wide + outs.wide), LOW)
    shape_c = jax.ShapeDtypeStruct((sent_count, down_rows, downs.wide), LOW)
    (stream_out, middle_grad, attended_grad, away, dgain_two, kept_b, sent_b, kept_c, sent_c) = pl.pallas_call(
        functools.partial(feed_kernel, shape),
        out_shape=(full_rows, full_rows, low_rows, jax.ShapeDtypeStruct((half_rows, width), LOW),
                   jax.ShapeDtypeStruct((8, width), FULL), shape_b, shape_b, shape_c, shape_c),
        in_specs=[SMEM] + [VMEM] * 3 + [HBM] * (5 + len(pieces_b)),
        out_specs=(HBM,) * 3 + (VMEM,) * 2 + (HBM,) * 4,
        scratch_shapes=[
            pltpu.VMEM((width, hidden), LOW),
            pltpu.VMEM(held_shape(outs, width), LOW),
            pltpu.VMEM((width, width), LOW),
            pltpu.VMEM(held_shape(downs, width), LOW),
            pltpu.VMEM((8, LANES) if downs.aligned else (width, hidden), LOW),
            pltpu.VMEM((width, hidden), LOW),
            pltpu.VMEM((width, outs.room), LOW),
            pltpu.VMEM((width, downs.room), LOW),
            pltpu.VMEM((length, width), LOW),
            pltpu.VMEM((length, width), LOW),
            pltpu.VMEM((length, width), FULL),
            pltpu.VMEM((half_rows, width), FULL),
            pltpu.VMEM((half_rows, width), LOW),
            pltpu.VMEM((length, width), FULL),
            pltpu.VMEM((length, width), LOW),
            pltpu.VMEM((width, length), LOW),
            pltpu.VMEM((length, width), LOW),
            pltpu.VMEM((width, length), LOW),
            pltpu.VMEM((width, length), LOW),
            pltpu.VMEM((length, block), LOW),
            pltpu.VMEM((length, block), LOW),
            pltpu.VMEM((length, width), FULL),
            pltpu.VMEM((length, width), FULL),
            pltpu.VMEM((length, width), LOW),
        ] + [pltpu.SemaphoreType.DMA] * 5 + [pltpu.SemaphoreType.DMA((5,))],
        compiler_params=params(60),
        cost_estimate=LITTLE,
        name="feed_forward_back",
    )(pos, coef, gain_two, page_col, attended, rows, cot_stream, cot_joined, other_joined, *pieces_b)

    def attend_scratch(pairs):
        piece = pltpu.VMEM((length, (pairs[1] - pairs[0]) * LANES), LOW)
        return [piece] * 5 + [pltpu.VMEM((length, LANES), FULL)] + [piece] * 3 + [
            pltpu.VMEM((length, length), FULL),
            pltpu.VMEM((LANES, length), FULL),
            pltpu.VMEM((LANES, length), FULL),
            pltpu.SemaphoreType.DMA((6,)),
        ]

    def attend_back(pairs, *operands):
        low_cols = jax.ShapeDtypeStruct((length, (pairs[1] - pairs[0]) * LANES), LOW)
        return pl.pallas_call(
            functools.partial(scores_back_kernel, (length, width, factor), pairs),
            out_shape=(low_cols,) * 3,
            in_specs=[VMEM] * 3 + [HBM] * 6,
            out_specs=(HBM,) * 3,
            scratch_shapes=attend_scratch(pairs),
            compiler_params=params(60),
            cost_estimate=LITTLE,
            name="attend_back",
        )(page_col, page_row, mask_row, *operands)

    sums_b, sums_c = Halving(kept_b, sent_b, steps_b), Halving(kept_c, sent_c, steps_c)
    sums_b.send()
    sums_c.send()
    partner_rows = swap(away)
    pair_count = width // LANES
    cuts = (0, pair_count * 2 // 3, pair_count)
    grads_one = attend_back(cuts[:2], queries, keys, values, attended, attended_grad, lse)
    met = (*sums_b.last, *sums_c.last, partner_rows)
    second = after(queries, grads_one[0], *met)
    sums_b.hold(grads_one[0])
    sums_c.hold(grads_one[0])
    sums_b.send(*met)
    sums_c.send(*met[:-1])
    runs = tuple((low * LANES, high * LANES) for low, high in zip(cuts[:-1], cuts[1:]))
    shape = (sums_of[0], half, piece_rows, qkvs, length, width, runs)
    shape_a = jax.ShapeDtypeStruct((sent_count, piece_rows, qkvs.wide), LOW)
    own_part, away_part, dgain_one, kept_a, sent_a = pl.pallas_call(
        functools.partial(project_back_kernel, shape, cuts[1:], factor),
        out_shape=(full_rows, low_rows, jax.ShapeDtypeStruct((8, width), FULL)) + (shape_a,) * 2,
        in_specs=[SMEM] + [VMEM] * 4 + [HBM] * (6 + 3 * len(runs)),
        out_specs=(HBM,) + (VMEM,) * 2 + (HBM,) * 2,
        scratch_shapes=[
            pltpu.VMEM((2, width, length), LOW),
            pltpu.VMEM((length, width), FULL),
            pltpu.VMEM((length, width), FULL),
            pltpu.VMEM((width, qkvs.room), LOW),
            pltpu.VMEM((length, width), LOW),
            pltpu.VMEM((length, width), LOW),
            pltpu.VMEM((width, 3 * width), LOW),
            pltpu.SemaphoreType.DMA,
            pltpu.SemaphoreType.DMA((3 * len(runs),)),
        ] + [pltpu.VMEM((length, high - low), LOW) for low, high in runs[:-1] for _ in range(3)] + attend_scratch(cuts[1:]),
        compiler_params=params(60),
        cost_estimate=LITTLE,
        name="project_back",
    )(pos, gain_one, page_col, page_row, mask_row, rows, other_rows, weight_qkv,
      second, keys, values, attended, attended_grad, lse, *grads_one)

    own_rows = lax.dynamic_slice_in_dim(stream_out, stream * half_rows, half_rows, 0)
    partner_rows = partner_rows.astype(FULL)
    text_rows = jnp.where(is_text, own_rows, partner_rows)
    image_rows = jnp.where(is_text, partner_rows, own_rows)
    gate_grad = jnp.sum(cot_joined * (text_rows - image_rows), axis=0, keepdims=True) * mix * (1.0 - mix)

    slot_index = lax.iota(jnp.int32, 5)[:, None]
    small = dgain_one[:5] + dgain_two[:5] + jnp.where(slot_index == 4, gate_grad, 0.0)
    sums_a = Halving(kept_a, sent_a, steps_b)
    sums_a.hold(*sums_b.last, *sums_c.last)
    sums_a.send()
    sums_a.rider = rider_rows(small + flip(small, *core[0]), qkvs.wide)
    back_part = swap(away_part)
    sums_a.send()
    sums_b.hold(*sums_a.messages)
    sums_b.send()
    sums_a.hold(*sums_b.messages)
    sums_a.send()
    sums_c.hold(*sums_a.messages)
    sums_c.send()
    sums_b.hold(*sums_a.messages)

    total_a, total_b, total_c = sums_a.total(), sums_b.total(), sums_c.total()

    last = total_a[1].astype(LOW)[None]
    packed = with_rider(last, sums_a.rider)
    arrived = swap(packed)
    packed_c = total_c[1].astype(LOW)
    grad_rows = pl.pallas_call(
        functools.partial(tail_kernel, length),
        out_shape=full_rows,
        in_specs=[VMEM] * 5,
        out_specs=VMEM,
        compiler_params=params(10),
        name="norm_tail",
    )(rows, gain_own, own_part, back_part, after(middle_grad, packed, packed_c))

    text_late, image_late = after(text_rows, packed, packed_c), after(image_rows, packed, packed_c)
    joined_rows = mix * text_late + (1.0 - mix) * image_late

    def both(total):
        return total[0], swap(total[1].astype(LOW))

    def placed(mine, theirs):
        theirs = theirs.astype(FULL)
        return jnp.where(is_text, jnp.stack((mine, theirs)), jnp.stack((theirs, mine)))

    mine_b, theirs_b = both(total_b)
    theirs_b = after(theirs_b, packed, packed_c)
    grad_b = placed(mine_b, theirs_b)
    grad_up = ups.cut(grad_b[..., : ups.wide], doc)
    grad_out = outs.cut(grad_b[..., ups.wide :], doc)
    out_new = adam_update(w_out, m_out, v_out, grad_out, 0.5, 0.01)
    up_new = adam_update(w_up, m_up, v_up, grad_up, 0.12, 0.01)
    if downs.aligned:
        mine_c, theirs_c = total_c[0], swap(packed_c)
    else:
        mine_c = downs.cut(total_c[0], place)
        theirs_c = swap(downs.cut(total_c[1], (place + half) % wide).astype(LOW))
    theirs_c = after(theirs_c, packed, grad_rows, up_new[0], out_new[0])
    grad_down = jnp.swapaxes(placed(mine_c, theirs_c), 1, 2)
    down_new = adam_update(w_down, m_down, v_down, grad_down, 0.06, 0.01)
    arrived = after(arrived, grad_rows, up_new[0], out_new[0], down_new[0])
    last, rider = rider_of(arrived, sums_a.rider.shape, last.shape)
    gains_grad = rider_value(kept_rider(sums_a.rider) + rider, gains.shape)
    mine_a, theirs_a = total_a[0], last[0]
    mine_a, theirs_a = qkvs.cut(mine_a, doc), qkvs.cut(theirs_a.astype(FULL), doc)
    query_here = is_query[0]
    grad_qkv = placed(
        jnp.where(query_here, mine_a, theirs_a), jnp.where(query_here, theirs_a, mine_a)
    )

    qkv_new = adam_update(w_qkv, m_qkv, v_qkv, grad_qkv, 0.12, 0.01)
    gains_new = adam_update(gains, m_gains, v_gains, gains_grad, 0.8, 0.0)
    return (stream_out, joined_rows, grad_rows, *qkv_new, *out_new, *up_new, *down_new, *gains_new)


def solution(mesh):
    by_rows = P(("docs", "wide"), None)
    by_row = P(("docs", "wide"))
    weight = P(None, "wide", "docs")
    return jax.shard_map(
        shards,
        mesh=mesh,
        in_specs=(by_rows,) * 3 + (by_row,) * 2 + (weight,) * 12 + (P(),) * 3,
        out_specs=(by_rows,) * 3 + (weight,) * 12 + (P(),) * 3,
        check_vma=False,
    )
```

```python
import functools
import math

import jax
import jax.numpy as jnp
from jax import lax
from jax.experimental import pallas as pl
from jax.experimental.pallas import tpu as pltpu
from jax.sharding import PartitionSpec as P

HEADS = 12
STEP = 10
LANES = 128
CHUNK = 128
ROW_PARTS = (5, 6, 5)
FIRST_A = False
NEG = -1000000000.0
LOW = jnp.bfloat16
FULL = jnp.float32


def flip(value, axis, mask):
    count = lax.axis_size(axis)
    return lax.ppermute(value, axis, [(i, i ^ mask) for i in range(count)])


def flipped(codes, axis, mask):
    d_mask = mask if axis == "docs" else 0
    w_mask = mask if axis == "wide" else 0
    return [(d ^ d_mask, w ^ w_mask) for d, w in codes]


def after(value, *others):
    return lax.optimization_barrier((value, *others))[0]


class Doubling:
    def __init__(self, unit, slot, order):
        self.slot, self.order, self.step = slot, order, 0
        self.arrays, self.codes = [unit[None]], [[(0, 0)]]
        self.last = ()

    def held(self):
        held = self.arrays[0] if len(self.arrays) == 1 else jnp.concatenate(self.arrays, axis=0)
        return held, [code for group in self.codes for code in group]

    def send(self, *others):
        held, known = self.held()
        if others:
            held = after(held, *others)
        axis, mask = self.order[self.step]
        self.arrays.append(flip(held, axis, mask))
        self.codes.append(flipped(known, axis, mask))
        self.step, self.last = self.step + 1, (self.arrays[-1],)

    def send_all(self):
        while self.step < len(self.order):
            self.send()

    def split_newest(self):
        newest, newest_known = self.arrays.pop(), self.codes.pop()
        held, known = self.held()
        self.arrays.append(newest)
        self.codes.append(newest_known)
        return (held, known), (newest, newest_known)

    def add(self, value, known, axis, mask):
        self.arrays.append(flip(value, axis, mask))
        self.codes.append(flipped(known, axis, mask))
        return self.arrays[-1]

    def slotted(self):
        return [(self.slot, group) for group in self.codes]


def sum_codes(order):
    codes = [(0, 0)]
    for axis, mask in reversed(order):
        codes = codes + flipped(codes, axis, mask)
    return codes


def halves_of(value):
    high = lax.reduce_precision(value, 8, 7)
    return high, lax.reduce_precision(value - high, 8, 7)


def rider_rows(value, lanes):
    rows, width = value.shape
    runs = [value[:, i : i + lanes] for i in range(0, width, lanes)]
    runs = [jnp.pad(run, ((0, -rows % 8), (0, lanes - run.shape[1]))) for run in runs]
    return jnp.concatenate(runs, axis=0)


def rider_value(laid, shape):
    rows, width = shape
    high = rows + -rows % 8
    runs = [laid[i * high : i * high + rows] for i in range(laid.shape[0] // high)]
    return jnp.concatenate(runs, axis=1)[:, :width]


def with_rider(value, rider):
    lanes = value.shape[-1]
    tail = [part.astype(LOW) for part in halves_of(rider)]
    return jnp.concatenate((value.reshape(-1, lanes), *tail), axis=0)


def rider_of(message, shape, value_shape):
    count, rows = math.prod(value_shape[:-1]), shape[0]
    parts = message[count : count + rows], message[count + rows :]
    return message[:count].reshape(value_shape), parts[0].astype(FULL) + parts[1].astype(FULL)


def kept_rider(rider):
    high, low = halves_of(rider)
    return high + low


class Halving:
    def __init__(self, kept, sent, steps):
        self.slots, self.sent, self.steps = [[half] for half in split(kept)], sent, steps
        self.step, self.last, self.messages, self.waits = 0, (), (), ()
        self.rider = None

    def left(self):
        return self.step < len(self.steps)

    def hold(self, *others):
        self.waits = self.waits + others

    def carry(self, value, axis, mask):
        if self.rider is None or self.step == 0:
            self.messages += (value,)
            return flip(value, axis, mask)
        message = with_rider(value, self.rider)
        self.messages += (message,)
        message = flip(message, axis, mask)
        value, rider = rider_of(message, self.rider.shape, value.shape)
        self.rider = kept_rider(self.rider) + rider
        return value

    def part_sums(self):
        outgoing = []
        for slot, parts in enumerate(self.slots):
            if self.waits:
                parts = parts[:-1] + [after(parts[-1], *self.waits)]
            half = parts[0].shape[0] // 2
            outgoing.append(sum(part[half:].astype(FULL) for part in parts).astype(LOW))
            self.slots[slot] = [part[:half] for part in parts]
        return outgoing

    def send(self, *others):
        one, two = self.steps[self.step]
        self.messages = ()
        if self.step == 0:
            whole = after(self.sent, *self.waits) if self.waits else self.sent
        else:
            outgoing = self.part_sums()
            if others:
                outgoing = [after(value, *others) for value in outgoing]
            whole = jnp.concatenate(outgoing, axis=0) if one == two else None
        if one == two:
            arrived = self.carry(whole, *one)
            self.last = (arrived,)
            arrived = split(arrived)
        else:
            arrived = [self.carry(outgoing[0], *one), flip(outgoing[1], *two)]
            self.messages += (outgoing[1],)
            self.last = tuple(arrived)
        self.slots = [parts + [new] for parts, new in zip(self.slots, arrived)]
        self.step, self.waits = self.step + 1, ()

    def total(self):
        while self.left():
            self.send()
        slots = [parts[:-1] + [after(parts[-1], *self.waits)] if self.waits else parts for parts in self.slots]
        return tuple(sum(part[0].astype(FULL) for part in parts) for parts in slots)


def split(value):
    middle = value.shape[0] // 2
    return [value[:middle], value[middle:]]


class Blocks:
    def __init__(self, count, size):
        self.count, self.size = count, size
        shifts = [(i * size) % LANES for i in range(count)]
        self.shifts = sorted(set(shifts))
        self.wide = -(-(size + max(shifts)) // LANES) * LANES
        self.aligned = max(shifts) == 0 and size % LANES == 0
        self.total = count * size
        self.room = max(self.start(i) + self.wide for i in range(count))

    def start(self, index):
        return index * self.size // LANES * LANES

    def start_dynamic(self, index):
        return pl.multiple_of(index * self.size // LANES * LANES, LANES)

    def pad(self, value, index):
        result = None
        for shift in self.shifts:
            low = [(0, 0)] * (value.ndim - 1) + [(shift, self.wide - self.size - shift)]
            placed = jnp.pad(value, low)
            here = (index * self.size) % LANES == shift
            result = placed if result is None else jnp.where(here, placed, result)
        return result

    def cut(self, value, index):
        result = None
        for shift in self.shifts:
            piece = value[..., shift : shift + self.size]
            here = (index * self.size) % LANES == shift
            result = piece if result is None else jnp.where(here, piece, result)
        return result

    def tile_owners(self, tile):
        low, high = tile * LANES, (tile + 1) * LANES
        return [
            (i, low - self.start(i))
            for i in range(self.count)
            if i * self.size < high and (i + 1) * self.size > low
        ]


def matmul(left, right):
    return lax.dot_general(left, right, (((1,), (0,)), ((), ())), preferred_element_type=FULL)


def matmul_nt(left, right):
    return lax.dot_general(left, right, (((1,), (1,)), ((), ())), preferred_element_type=FULL)


def matmul_tn(left, right):
    return lax.dot_general(left, right, (((0,), (0,)), ((), ())), preferred_element_type=FULL)


def normed(values):
    centred = values - jnp.mean(values, axis=-1, keepdims=True)
    spread = jnp.mean(centred * centred, axis=-1, keepdims=True)
    scale = lax.rsqrt(spread + 1e-05)
    return centred * scale, scale


def norm_back(grad, unit, scale, gain):
    inner = grad * gain
    mean_inner = jnp.mean(inner, axis=-1, keepdims=True)
    mean_both = jnp.mean(inner * unit, axis=-1, keepdims=True)
    return scale * (inner - mean_inner - unit * mean_both)


def rows_at(index, size=CHUNK):
    return pl.ds(pl.multiple_of(index * size, size), size)


def places(pos, slot, codes, half):
    owner = pos[2] if slot == 0 else 1 - pos[2]
    for index, (d_mask, w_mask) in enumerate(codes):
        yield index, pos[0] ^ d_mask, owner * half + (pos[1] ^ w_mask)


def load_pieces(pos, refs, codes, half, lanes, target, sem):
    for ref, (slot, group) in zip(refs, codes):
        for index, doc, inner in places(pos, slot, group, half):
            pltpu.make_async_copy(
                ref.at[index, :, pl.ds(lanes[0], lanes[1])], target(doc, inner), sem
            ).start()


def load_folded(pos, refs, codes, half, rows, blocks, begin, folds, held, sem):
    for fold in range(folds):
        def target(doc, inner):
            first = pl.ds(pl.multiple_of((doc * folds + fold) * rows, rows), rows)
            if blocks.aligned:
                return held.at[first, pl.ds(blocks.start_dynamic(inner), blocks.wide)]
            return held.at[inner, first, :]

        load_pieces(pos, refs, codes, half, (begin + fold * blocks.wide, blocks.wide), target, sem)


def begin(source, target, sem):
    pltpu.make_async_copy(source, target, sem).start()


def finish(source, target, sem):
    pltpu.make_async_copy(source, target, sem).wait()


def store_pieces(pos, source, sums, half, targets, lanes, sem):
    for slot, codes in enumerate(sums):
        count = len(codes) // 2
        for index, doc, inner in places(pos, slot, codes, half):
            pltpu.make_async_copy(
                source(doc, inner),
                targets[index // count].at[slot * count + index % count, :, pl.ds(lanes[0], lanes[1])],
                sem,
            ).start()


def wait_whole(ref, sem):
    pltpu.make_async_copy(ref, ref, sem).wait()


def row_target(ref, blocks, rows):
    if blocks.aligned:
        return lambda doc, inner: ref.at[
            pl.ds(pl.multiple_of(inner * rows, rows), rows),
            pl.ds(blocks.start_dynamic(doc), blocks.wide),
        ]
    return lambda doc, inner: ref.at[doc, pl.ds(pl.multiple_of(inner * rows, rows), rows), :]


def held_shape(blocks, height):
    return (height, blocks.total) if blocks.aligned else (blocks.count, height, blocks.wide)


def merge_tiles(held, whole, blocks):
    for tile in range(blocks.total // LANES):
        value = None
        for index, offset in blocks.tile_owners(tile):
            piece = held[index, :, offset : offset + LANES]
            value = piece if value is None else value + piece
        whole[:, tile * LANES : (tile + 1) * LANES] = value


def project_kernel(shape, pos, gains, page_col, page_row, mask_row, own_hbm, *refs):
    codes, half, rows, blocks, length, width, factor, chunks = shape
    arrived, refs = refs[: len(chunks)], refs[len(chunks) :]
    pieces, refs = refs[: len(codes)], refs[len(codes) :]
    outs, refs = refs[:7], refs[7:]
    (q_out, k_out, v_out, att_out, lse_out, weight, other) = kept = refs[:7]
    (own, held, h_own, h_oth, allowed, sem, sem_out, sem_in) = refs[7:]
    begin(own_hbm, own, sem_in.at[0])
    load_pieces(pos, pieces, codes, half, (0, blocks.wide), row_target(held, blocks, rows), sem)
    starts = [sum(chunks[:i]) for i in range(len(chunks))]
    places_in = [other.at[pl.ds(start, size), :] for start, size in zip(starts, chunks)]
    for i, (ref, place) in enumerate(zip(arrived, places_in)):
        begin(ref, place, sem_in.at[i + 1])
    finish(own_hbm, own, sem_in.at[0])
    for i, (ref, place) in enumerate(zip(arrived, places_in)):
        finish(ref, place, sem_in.at[i + 1])
    begin(other, outs[6], sem_out.at[6])
    for i in range(length // CHUNK):
        part = pl.ds(i * CHUNK, CHUNK)
        unit, _ = normed(own[part, :].astype(FULL))
        h_own[part, :] = (unit * gains[0:1, :]).astype(LOW)
        unit, _ = normed(other[part, :].astype(FULL))
        h_oth[part, :] = (unit * gains[1:2, :]).astype(LOW)
        row = lax.broadcasted_iota(jnp.int32, (CHUNK, length), 0) + i * CHUNK
        col = lax.broadcasted_iota(jnp.int32, (CHUNK, length), 1)
        ok = (page_col[part, :] == page_row[...]) & ((mask_row[...] == 1) | (row == col))
        allowed[part, :] = jnp.where(ok, 1.0, 0.0)
    wait_whole(held, sem)
    merge_tiles(held, weight, blocks)
    begin(weight, outs[5], sem_out.at[5])
    lse_out[...] = jnp.zeros_like(lse_out)

    q_out[...] = (matmul(h_own[...], weight[:, :width]).astype(LOW) * factor).astype(LOW)
    k_out[...] = matmul(h_oth[...], weight[:, width : 2 * width]).astype(LOW)
    v_out[...] = matmul(h_oth[...], weight[:, 2 * width :]).astype(LOW)
    for i in range(3):
        begin(kept[i], outs[i], sem_out.at[i])
    size = width // HEADS
    per = LANES // size

    @pl.loop(0, width // LANES)
    def _(pair):
        cols = pl.ds(pl.multiple_of(pair * LANES, LANES), LANES)
        keys, values, queries = k_out[:, cols], v_out[:, cols], q_out[:, cols]
        lane = lax.broadcasted_iota(jnp.int32, queries.shape, 1)
        result, sums = None, lse_out[...]
        for sub in range(per):
            inside = lane // size == sub
            scores = matmul_nt(jnp.where(inside, queries, jnp.zeros_like(queries)), keys)
            scores = jnp.where(allowed[...] > 0.5, scores, NEG)
            top = jnp.max(scores, axis=-1, keepdims=True)
            exps = jnp.exp(scores - top)
            total = jnp.sum(exps, axis=-1, keepdims=True)
            out = matmul(exps.astype(LOW), values) * (1.0 / total)
            result = out if result is None else jnp.where(inside, out, result)
            sums = jnp.where(lane == pair * per + sub, top + jnp.log(total), sums)
        lse_out[...] = sums
        att_out[:, cols] = result.astype(LOW)

    for i in (3, 4):
        begin(kept[i], outs[i], sem_out.at[i])
    for i, ref in enumerate(kept):
        finish(ref, outs[i], sem_out.at[i])


def feed_kernel(shape, pos, coef, gain, page_col, att_hbm, own_hbm, cot_hbm, cotj_hbm, arrived_hbm, *refs):
    (codes, counts, sums_b, sums_c, half, rows, down_rows, ups, outs, downs, length, width, hidden, block) = shape
    pieces, refs = refs[: len(codes)], refs[len(codes) :]
    out_ref, dmid_ref, datt_ref, away_ref, dgain_ref = refs[:5]
    up_targets, down_targets = refs[5:7], refs[7:9]
    (w_up, o_held, w_out, d_held, w_down, g_up, g_out, g_down, att, own, cot, cotj_own, cotj_oth, mid, h2, h2_t, dffn, dffn_t,
     att_t, acts, dpre, acc, dacc, dbranch, sem_up, sem_out, sem_down, sem_gup, sem_gdown, sems) = refs[9:]
    begin(att_hbm, att, sems.at[0])
    last = counts
    load_pieces(pos, pieces[:last], codes[:last], half, (ups.wide, outs.wide), row_target(o_held, outs, rows), sem_out)
    begin(own_hbm, own, sems.at[1])
    begin(cot_hbm, cot, sems.at[2])
    begin(cotj_hbm, cotj_own, sems.at[3])
    begin(arrived_hbm, cotj_oth, sems.at[4])
    load_pieces(pos, pieces[:last], codes[:last], half, (0, ups.wide), row_target(w_up, ups, rows), sem_up)
    folds = down_rows // rows
    load_folded(pos, pieces[last:], codes[last:], half, rows, downs, 0, folds, d_held, sem_down)
    half_rows = length // 2
    parts = length // CHUNK

    def valid_at(part):
        return jnp.where(page_col[part, :] >= 0, 1.0, 0.0)

    finish(att_hbm, att, sems.at[0])
    wait_whole(o_held, sem_out)
    merge_tiles(o_held, w_out, outs)
    mid[...] = matmul(att[...], w_out[...])
    att_t[...] = att[...].T
    finish(own_hbm, own, sems.at[1])
    for i in range(parts):
        part = pl.ds(i * CHUNK, CHUNK)
        middle = own[part, :].astype(FULL) + valid_at(part) * mid[part, :]
        mid[part, :] = middle
        unit, _ = normed(middle)
        h2[part, :] = (unit * gain[...]).astype(LOW)
    finish(cot_hbm, cot, sems.at[2])
    finish(cotj_hbm, cotj_own, sems.at[3])
    finish(arrived_hbm, cotj_oth, sems.at[4])
    for which, ref in ((pos[2], cotj_own), (1 - pos[2], cotj_oth)):
        for i in range(half_rows // CHUNK):
            part = pl.ds(pl.multiple_of(which * half_rows + i * CHUNK, CHUNK), CHUNK)
            grad = cot[part, :] + coef[...] * ref[pl.ds(i * CHUNK, CHUNK), :].astype(FULL)
            cot[part, :] = grad
            dffn[part, :] = (grad * valid_at(part)).astype(LOW)
    dffn_t[...] = dffn[...].T
    h2_t[...] = h2[...].T
    acc[...] = jnp.zeros_like(acc)
    dacc[...] = jnp.zeros_like(dacc)
    wait_whole(w_up, sem_up)
    wait_whole(d_held, sem_down)
    if not downs.aligned:
        merge_tiles(d_held, w_down, downs)
    down = d_held if downs.aligned else w_down
    c0, c1 = 0.7978845608028654, 0.044715

    @pl.loop(0, hidden // block)
    def _(f):
        cols = pl.ds(pl.multiple_of(f * block, LANES), block)
        pre = matmul(h2[...], w_up[:, cols])
        dact = matmul(dffn[...], down[:, cols])
        square = pre * pre
        flat = jnp.tanh(c0 * (pre + c1 * square * pre))
        cdf = 0.5 * (1.0 + flat)
        slope = cdf + pre * (0.5 * (1.0 - flat * flat)) * (c0 * (1.0 + 3.0 * c1 * square))
        acts[...] = (pre * cdf).astype(LOW)
        dpre[...] = (slope * dact).astype(LOW)
        acc[...] += matmul_nt(acts[...], down[:, cols])
        dacc[...] += matmul_nt(dpre[...], w_up[:, cols])
        g_down[:, cols] = matmul(dffn_t[...], acts[...]).astype(LOW)
        g_up[:, cols] = matmul(h2_t[...], dpre[...]).astype(LOW)

    if downs.room > downs.total:
        g_down[:, downs.total :] = jnp.zeros((width, downs.room - downs.total), LOW)
    store_pieces(
        pos,
        lambda doc, inner: g_down.at[
            pl.ds(pl.multiple_of(doc * down_rows, down_rows), down_rows),
            pl.ds(downs.start_dynamic(inner), downs.wide),
        ],
        sums_c, half, down_targets, (0, downs.wide), sem_gdown,
    )
    store_pieces(
        pos,
        lambda doc, inner: g_up.at[
            pl.ds(pl.multiple_of(inner * rows, rows), rows),
            pl.ds(ups.start_dynamic(doc), ups.wide),
        ],
        sums_b, half, up_targets, (0, ups.wide), sem_gup,
    )
    dgain_ref[...] = jnp.zeros_like(dgain_ref)
    for i in range(parts):
        part = pl.ds(i * CHUNK, CHUNK)
        valid = valid_at(part)
        middle = mid[part, :]
        acc[part, :] = middle + valid * acc[part, :]
        unit, scale = normed(middle)
        grad = dacc[part, :]
        dgain_ref[pl.ds(2 + pos[2], 1), :] += jnp.sum(grad * unit, axis=0, keepdims=True)
        dmid = cot[part, :] + norm_back(grad, unit, scale, gain[...])
        dacc[part, :] = dmid
        dbranch[part, :] = (dmid * valid).astype(LOW)
    begin(acc, out_ref, sems.at[0])
    begin(dacc, dmid_ref, sems.at[1])
    h2[...] = matmul_nt(dbranch[...], w_out[...]).astype(LOW)
    begin(h2, datt_ref, sems.at[2])
    g_out[:, : outs.total] = matmul(att_t[...], dbranch[...]).astype(LOW)
    if outs.room > outs.total:
        g_out[:, outs.total :] = jnp.zeros((width, outs.room - outs.total), LOW)
    store_pieces(
        pos,
        lambda doc, inner: g_out.at[
            pl.ds(pl.multiple_of(inner * rows, rows), rows),
            pl.ds(outs.start_dynamic(doc), outs.wide),
        ],
        sums_b, half, up_targets, (ups.wide, outs.wide), sem_gup,
    )
    for i in range(half_rows // CHUNK):
        part = pl.ds(pl.multiple_of((1 - pos[2]) * half_rows + i * CHUNK, CHUNK), CHUNK)
        away_ref[pl.ds(i * CHUNK, CHUNK), :] = acc[part, :].astype(LOW)
    for target in down_targets:
        wait_whole(target, sem_gdown)
    for target in up_targets:
        wait_whole(target, sem_gup)
    finish(acc, out_ref, sems.at[0])
    finish(dacc, dmid_ref, sems.at[1])
    finish(h2, datt_ref, sems.at[2])


def scores_back(shape, pairs, page_col, page_row, mask_row, sources, scratch, more_loads):
    length, width, factor = shape
    q_hbm, k_hbm, v_hbm, att_hbm, datt_hbm, lse_hbm = sources
    (q_ref, k_ref, v_ref, att, datt, lse, dq, dk, dv, allowed, lse_t, dots_t, sems) = scratch
    size = width // HEADS
    per = LANES // size
    cols_here = pl.ds(pairs[0] * LANES, (pairs[1] - pairs[0]) * LANES)
    loads = [(source.at[:, cols_here], target) for source, target in
             ((datt_hbm, datt), (att_hbm, att), (q_hbm, q_ref), (k_hbm, k_ref), (v_hbm, v_ref))]
    loads.append((lse_hbm, lse))
    for i, (source, target) in enumerate(loads):
        begin(source, target, sems.at[i])
    more_loads()
    mask = jnp.broadcast_to(mask_row[...].astype(FULL), (LANES, length)).T[:, 0:1]
    row = lax.broadcasted_iota(jnp.int32, (length, length), 0)
    col = lax.broadcasted_iota(jnp.int32, (length, length), 1)
    ok = (page_col[...] == page_row[...]) & ((mask == 1.0) | (row == col))
    allowed[...] = jnp.where(ok, 1.0, 0.0)
    here_width = cols_here.size
    head = lax.broadcasted_iota(jnp.int32, (LANES, here_width), 0)
    lane = lax.broadcasted_iota(jnp.int32, (LANES, here_width), 1)
    chosen = jnp.where(lane // size == head, 1.0, 0.0)
    for i, (source, target) in enumerate(loads):
        finish(source, target, sems.at[i])
    dots_t[...] = lax.dot_general(
        chosen, att[...].astype(FULL) * datt[...].astype(FULL), (((1,), (1,)), ((), ())),
        preferred_element_type=FULL, precision=lax.Precision.HIGHEST,
    )
    lse_t[...] = lse[...].T

    @pl.loop(0, pairs[1] - pairs[0])
    def _(pair):
        cols = pl.ds(pl.multiple_of(pair * LANES, LANES), LANES)
        queries, grads = q_ref[:, cols], datt[:, cols]
        keys, values = k_ref[:, cols], v_ref[:, cols]
        lane = lax.broadcasted_iota(jnp.int32, (length, LANES), 1)
        zero = jnp.zeros_like(queries)
        trio = None
        for sub in range(per):
            inside = lane // size == sub
            lse_row = lse_t[pl.ds((pair + pairs[0]) * per + sub, 1), :]
            dot_row = dots_t[pl.ds(pair * per + sub, 1), :]
            scores = matmul_nt(keys, jnp.where(inside, queries, zero))
            scores = jnp.where(allowed[...] > 0.5, scores, NEG)
            probs = jnp.exp(scores - lse_row)
            dprob = matmul_nt(values, jnp.where(inside, grads, zero))
            low = (probs * (dprob - dot_row)).astype(LOW)
            three = (matmul_tn(low, keys), matmul(low, queries), matmul(probs.astype(LOW), grads))
            trio = three if trio is None else [jnp.where(inside, new, old) for new, old in zip(three, trio)]
        dq[:, cols] = (trio[0] * factor).astype(LOW)
        dk[:, cols] = trio[1].astype(LOW)
        dv[:, cols] = trio[2].astype(LOW)


def scores_back_kernel(shape, pairs, page_col, page_row, mask_row, *refs):
    sources, outs, scratch = refs[:6], refs[6:9], refs[9:]
    scores_back(shape, pairs, page_col, page_row, mask_row, sources, scratch, lambda: None)
    made, sems = scratch[6:9], scratch[-1]
    for i, (source, target) in enumerate(zip(made, outs)):
        begin(source, target, sems.at[i])
    for i, (source, target) in enumerate(zip(made, outs)):
        finish(source, target, sems.at[i])


def project_back_kernel(
    shape, pairs, factor, pos, gains, page_col, page_row, mask_row, own_hbm, other_hbm, weight_hbm, *refs
):
    (sums, half, rows, blocks, length, width, runs) = shape
    sources, refs = refs[:6], refs[6:]
    given, refs = refs[: 3 * (len(runs) - 1)], refs[3 * (len(runs) - 1) :]
    own_out, oth_ref, dgain_ref = refs[:3]
    targets, refs = refs[3:5], refs[5:]
    h_t, flat, own_ref, grad, own, other, weight, sem, sems = refs[:9]
    copies, scratch = refs[9 : 9 + len(given)], refs[9 + len(given) :]
    grads = [copies[3 * i : 3 * i + 3] for i in range(len(runs) - 1)] + [scratch[6:9]]
    parts = length // CHUNK
    loads = [(own_hbm, own), (other_hbm, other), *zip(given, copies), (weight_hbm, weight)]

    def begin_loads():
        for i, (source, target) in enumerate(loads):
            begin(source, target, sems.at[i])

    scores_back((length, width, factor), pairs, page_col, page_row, mask_row, sources, scratch, begin_loads)

    def take(i):
        finish(*loads[i], sems.at[i])

    for which, source in ((0, own), (1, other)):
        take(which)
        for i in range(parts):
            part = pl.ds(i * CHUNK, CHUNK)
            unit, _ = normed(source[part, :].astype(FULL))
            flat[part, :] = unit * gains[which : which + 1, :]
        h_t[which] = flat[...].astype(LOW).T
    for i in range(2, len(loads) - 1):
        take(i)
    for (low, high), trio in zip(runs, grads):
        for block, (which, ref) in enumerate(zip((0, 1, 1), trio)):
            grad[:, block * width + low : block * width + high] = matmul(h_t[which], ref[...]).astype(LOW)
    if blocks.room > blocks.total:
        grad[:, blocks.total :] = jnp.zeros((width, blocks.room - blocks.total), LOW)
    store_pieces(
        pos,
        lambda doc, inner: grad.at[
            pl.ds(pl.multiple_of(inner * rows, rows), rows),
            pl.ds(blocks.start_dynamic(doc), blocks.wide),
        ],
        sums, half, targets, (0, blocks.wide), sem,
    )
    dgain_ref[...] = jnp.zeros_like(dgain_ref)
    take(len(loads) - 1)
    own_ref[...] = sum(
        matmul_nt(trio[0][...], weight[:, low:high]) for (low, high), trio in zip(runs, grads)
    )
    begin(own_ref, own_out, sems.at[0])
    flat[...] = sum(
        matmul_nt(trio[block][...], weight[:, block * width + low : block * width + high])
        for (low, high), trio in zip(runs, grads)
        for block in (1, 2)
    )
    for i in range(parts):
        part = pl.ds(i * CHUNK, CHUNK)
        unit, _ = normed(own[part, :].astype(FULL))
        dgain_ref[pl.ds(pos[2], 1), :] += jnp.sum(own_ref[part, :] * unit, axis=0, keepdims=True)
        unit, _ = normed(other[part, :].astype(FULL))
        value = flat[part, :]
        oth_ref[part, :] = value.astype(LOW)
        dgain_ref[pl.ds(1 - pos[2], 1), :] += jnp.sum(value * unit, axis=0, keepdims=True)
    finish(own_ref, own_out, sems.at[0])
    for target in targets:
        wait_whole(target, sem)


def tail_kernel(length, own, gain, mine, theirs, dmid, out_ref):
    for i in range(length // CHUNK):
        part = pl.ds(i * CHUNK, CHUNK)
        unit, scale = normed(own[part, :].astype(FULL))
        grad = mine[part, :] + theirs[part, :].astype(FULL)
        out_ref[part, :] = dmid[part, :] + norm_back(grad, unit, scale, gain[...])


VMEM = pl.BlockSpec(memory_space=pltpu.VMEM)
HBM = pl.BlockSpec(memory_space=pltpu.HBM)
SMEM = pl.BlockSpec(memory_space=pltpu.SMEM)


LITTLE = pl.CostEstimate(flops=1_000, bytes_accessed=1_000, transcendentals=0)


def params(mebibytes):
    return pltpu.CompilerParams(vmem_limit_bytes=mebibytes * 1024 * 1024)


def adam_update(weight, first, second, grad, rate, decay):
    first_new = 0.9 * first + 0.1 * grad
    second_new = 0.999 * second + 0.001 * grad * grad
    first_hat = first_new / (1.0 - 0.9**STEP)
    second_hat = second_new / (1.0 - 0.999**STEP)
    weight_new = weight - rate * (first_hat / (jnp.sqrt(second_hat) + 1e-08) + decay * weight)
    return (weight_new, first_new, second_new)


def shards(
    rows, cot_stream, cot_joined, page, key_mask,
    w_qkv, m_qkv, v_qkv, w_out, m_out, v_out, w_up, m_up, v_up, w_down, m_down, v_down,
    gains, m_gains, v_gains,
):
    docs, wide = lax.axis_size("docs"), lax.axis_size("wide")
    half = wide // 2
    doc, place = lax.axis_index("docs"), lax.axis_index("wide")
    stream = place // half
    is_text = stream == 0
    pos = jnp.stack((doc, place % half, stream)).astype(jnp.int32)
    length, width = rows.shape
    half_rows = length // 2
    factor = float(width // HEADS) ** (-0.5)
    piece_rows = w_qkv.shape[1]
    hidden = w_up.shape[2] * docs
    qkvs, outs, ups = Blocks(docs, w_qkv.shape[2]), Blocks(docs, w_out.shape[2]), Blocks(docs, w_up.shape[2])
    downs = Blocks(wide, w_down.shape[1])
    down_rows = w_down.shape[2]

    core = [("wide", 1)]
    along_x = [("docs", 1)]
    along_y = [("docs", 1 << b) for b in range(1, docs.bit_length() - 1)]
    along_z = [("wide", 1 << b) for b in range(1, half.bit_length() - 1)]
    across = ("wide", half)

    def swap(value):
        return flip(value, *across)

    column = doc * w_qkv.shape[2] + lax.iota(jnp.int32, w_qkv.shape[2])
    is_query = (column < width)[None, None, :]
    pair_qkv = jnp.where(is_query, w_qkv, w_qkv[::-1]).astype(LOW)

    def own_first(pair):
        return jnp.where(is_text, pair, pair[::-1])

    unit_a = qkvs.pad(own_first(pair_qkv), doc)
    unit_b = jnp.concatenate(
        (ups.pad(own_first(w_up.astype(LOW)), doc), outs.pad(own_first(w_out.astype(LOW)), doc)), axis=-1
    )
    unit_c = downs.pad(jnp.swapaxes(own_first(w_down.astype(LOW)), 1, 2), place)
    folds = down_rows // piece_rows

    def folded(unit):
        return jnp.concatenate([unit[i * piece_rows : (i + 1) * piece_rows] for i in range(folds)], axis=-1)

    page_col, page_row = page[:, None], page[None, :]
    mask_row = key_mask[None, :]
    gain_own = lax.dynamic_index_in_dim(gains, stream, 0, keepdims=True)
    gain_oth = lax.dynamic_index_in_dim(gains, 1 - stream, 0, keepdims=True)
    gain_one = jnp.concatenate((gain_own, gain_oth), axis=0)
    gain_two = lax.dynamic_index_in_dim(gains, 2 + stream, 0, keepdims=True)
    mix = jax.nn.sigmoid(gains[4])[None, :]
    coef = jnp.where(is_text, mix, 1.0 - mix)

    cot_low = cot_joined.astype(LOW)
    unit_a_oth = swap(unit_a[1])
    unit_b_oth = swap(after(unit_b[1], unit_a_oth)) if FIRST_A else swap(unit_b[1])
    if downs.aligned:
        unit_c_oth = swap(after(unit_c[1], unit_a_oth))
    else:
        raw = jnp.swapaxes(own_first(w_down.astype(LOW)), 1, 2)
        unit_c_oth = downs.pad(swap(raw[1]), (place + half) % wide)
    zxy, zyx = along_z + along_x + along_y, along_z + along_y + along_x
    a_own, a_oth = Doubling(unit_a[0], 0, zxy), Doubling(unit_a_oth, 1, zyx)
    b_own = Doubling(unit_b[0], 0, along_y + along_x + along_z)
    c_own = Doubling(folded(unit_c[0]), 0, along_y + along_z + along_x)
    b_oth, c_oth = Doubling(unit_b_oth, 1, zxy), Doubling(folded(unit_c_oth), 1, zyx)
    steps_y, steps_x = len(along_y), len(along_x)
    chunks, begin = [], 0
    for size in [length * part // sum(ROW_PARTS) for part in ROW_PARTS]:
        some = rows[begin : begin + size]
        chunks.append(swap(after(some, chunks[-1] if chunks else unit_a_oth)))
        begin += size
    for _ in range(steps_y):
        b_own.send()
    for _ in range(steps_y):
        c_own.send()
    for _ in range(steps_x):
        b_own.send(unit_a_oth)
    for _ in along_z:
        c_own.send(unit_a_oth)
    a_own.send_all()
    a_oth.send_all()
    first = (a_oth.arrays[len(along_z) + steps_y], a_own.arrays[len(along_z) + steps_x])
    rest = (a_oth.arrays[-1], a_own.arrays[-1])
    for one in (b_oth, c_oth):
        for _ in along_z:
            one.send(*first, page_col, gain_one, gain_two, coef, cot_low)
    met = b_oth.last + c_oth.last
    for one in (b_own, c_own):
        while one.step < len(one.order):
            one.send(*met)
    for one, steps in ((b_oth, steps_x), (c_oth, steps_y)):
        for _ in range(steps):
            one.send(*rest, chunks[1])
    for one, own in ((b_oth, b_own), (c_oth, c_own)):
        while one.step < len(one.order):
            one.send(chunks[-1], *own.last)
    pieces_a, codes_a = [], []
    for one in (a_own, a_oth):
        for value, known in one.split_newest():
            one.add(value, known, *core[0])
        pieces_a += one.arrays
        codes_a += one.slotted()
    waiting, passed = [], []
    for one in (b_own, b_oth, c_own, c_oth):
        early, late = one.split_newest()
        passed.append(one.add(after(early[0], chunks[-1]), early[1], *core[0]))
        waiting.append((one, *late))
    other_joined = swap(after(cot_low, chunks[-1], *passed))

    low_rows = jax.ShapeDtypeStruct((length, width), LOW)
    full_rows = jax.ShapeDtypeStruct((length, width), FULL)

    sizes = tuple(chunk.shape[0] for chunk in chunks)
    shape = (codes_a, half, piece_rows, qkvs, length, width, factor, sizes)
    made = (low_rows, low_rows, low_rows, low_rows, jax.ShapeDtypeStruct((length, LANES), FULL),
            jax.ShapeDtypeStruct((width, 3 * width), LOW), low_rows)
    queries, keys, values, attended, lse, weight_qkv, other_rows = pl.pallas_call(
        functools.partial(project_kernel, shape),
        out_shape=made,
        in_specs=[SMEM] + [VMEM] * 4 + [HBM] * (1 + len(chunks) + len(pieces_a)),
        out_specs=(HBM,) * 7,
        scratch_shapes=[pltpu.VMEM(one.shape, one.dtype) for one in made] + [
            pltpu.VMEM((length, width), LOW),
            pltpu.VMEM((docs, width, qkvs.wide), LOW),
            pltpu.VMEM((length, width), LOW),
            pltpu.VMEM((length, width), LOW),
            pltpu.VMEM((length, length), FULL),
            pltpu.SemaphoreType.DMA,
            pltpu.SemaphoreType.DMA((7,)),
            pltpu.SemaphoreType.DMA((1 + len(chunks),)),
        ],
        compiler_params=params(60),
        cost_estimate=LITTLE,
        name="project_attend",
    )(pos, gain_one, page_col, page_row, mask_row, rows, *chunks, *pieces_a)

    here = [value for _, value, _ in waiting]
    for one, value, known in waiting:
        one.add(after(value, lse, other_joined, *here), known, *core[0])
    streams = (b_own, b_oth, c_own, c_oth)
    pieces_b = sum((one.arrays for one in streams), [])
    codes_b = sum((one.slotted() for one in streams), [])
    counts = len(b_own.arrays) + len(b_oth.arrays)
    xy, yx = along_x + along_y, along_y + along_x
    steps_b = [core * 2, *zip(xy, yx), *((step, step) for step in along_z)]
    steps_c = [core * 2, *((step, step) for step in along_z), *zip(xy, yx)]
    sums_of = [tuple(sum_codes([pair[slot] for pair in steps]) for slot in (0, 1)) for steps in (steps_b, steps_c)]
    sent_count = len(sums_of[0][0])
    block = 8 * LANES
    shape = (codes_b, counts, *sums_of, half, piece_rows, down_rows, ups, outs, downs, length, width, hidden, block)
    shape_b = jax.ShapeDtypeStruct((sent_count, piece_rows, ups.wide + outs.wide), LOW)
    shape_c = jax.ShapeDtypeStruct((sent_count, down_rows, downs.wide), LOW)
    (stream_out, middle_grad, attended_grad, away, dgain_two, kept_b, sent_b, kept_c, sent_c) = pl.pallas_call(
        functools.partial(feed_kernel, shape),
        out_shape=(full_rows, full_rows, low_rows, jax.ShapeDtypeStruct((half_rows, width), LOW),
                   jax.ShapeDtypeStruct((8, width), FULL), shape_b, shape_b, shape_c, shape_c),
        in_specs=[SMEM] + [VMEM] * 3 + [HBM] * (5 + len(pieces_b)),
        out_specs=(HBM,) * 3 + (VMEM,) * 2 + (HBM,) * 4,
        scratch_shapes=[
            pltpu.VMEM((width, hidden), LOW),
            pltpu.VMEM(held_shape(outs, width), LOW),
            pltpu.VMEM((width, width), LOW),
            pltpu.VMEM(held_shape(downs, width), LOW),
            pltpu.VMEM((8, LANES) if downs.aligned else (width, hidden), LOW),
            pltpu.VMEM((width, hidden), LOW),
            pltpu.VMEM((width, outs.room), LOW),
            pltpu.VMEM((width, downs.room), LOW),
            pltpu.VMEM((length, width), LOW),
            pltpu.VMEM((length, width), LOW),
            pltpu.VMEM((length, width), FULL),
            pltpu.VMEM((half_rows, width), FULL),
            pltpu.VMEM((half_rows, width), LOW),
            pltpu.VMEM((length, width), FULL),
            pltpu.VMEM((length, width), LOW),
            pltpu.VMEM((width, length), LOW),
            pltpu.VMEM((length, width), LOW),
            pltpu.VMEM((width, length), LOW),
            pltpu.VMEM((width, length), LOW),
            pltpu.VMEM((length, block), LOW),
            pltpu.VMEM((length, block), LOW),
            pltpu.VMEM((length, width), FULL),
            pltpu.VMEM((length, width), FULL),
            pltpu.VMEM((length, width), LOW),
        ] + [pltpu.SemaphoreType.DMA] * 5 + [pltpu.SemaphoreType.DMA((5,))],
        compiler_params=params(60),
        cost_estimate=LITTLE,
        name="feed_forward_back",
    )(pos, coef, gain_two, page_col, attended, rows, cot_stream, cot_joined, other_joined, *pieces_b)

    def attend_scratch(pairs):
        piece = pltpu.VMEM((length, (pairs[1] - pairs[0]) * LANES), LOW)
        return [piece] * 5 + [pltpu.VMEM((length, LANES), FULL)] + [piece] * 3 + [
            pltpu.VMEM((length, length), FULL),
            pltpu.VMEM((LANES, length), FULL),
            pltpu.VMEM((LANES, length), FULL),
            pltpu.SemaphoreType.DMA((6,)),
        ]

    def attend_back(pairs, *operands):
        low_cols = jax.ShapeDtypeStruct((length, (pairs[1] - pairs[0]) * LANES), LOW)
        return pl.pallas_call(
            functools.partial(scores_back_kernel, (length, width, factor), pairs),
            out_shape=(low_cols,) * 3,
            in_specs=[VMEM] * 3 + [HBM] * 6,
            out_specs=(HBM,) * 3,
            scratch_shapes=attend_scratch(pairs),
            compiler_params=params(60),
            cost_estimate=LITTLE,
            name="attend_back",
        )(page_col, page_row, mask_row, *operands)

    sums_b, sums_c = Halving(kept_b, sent_b, steps_b), Halving(kept_c, sent_c, steps_c)
    sums_b.send()
    sums_c.send()
    partner_rows = swap(away)
    pair_count = width // LANES
    cuts = (0, pair_count // 2, pair_count)
    grads_one = attend_back(cuts[:2], queries, keys, values, attended, attended_grad, lse)
    met = (*sums_b.last, *sums_c.last, partner_rows)
    second = after(queries, grads_one[0], *met)
    sums_b.hold(grads_one[0])
    sums_c.hold(grads_one[0])
    sums_b.send(*met)
    sums_c.send(*met[:-1])
    runs = tuple((low * LANES, high * LANES) for low, high in zip(cuts[:-1], cuts[1:]))
    shape = (sums_of[0], half, piece_rows, qkvs, length, width, runs)
    shape_a = jax.ShapeDtypeStruct((sent_count, piece_rows, qkvs.wide), LOW)
    own_part, away_part, dgain_one, kept_a, sent_a = pl.pallas_call(
        functools.partial(project_back_kernel, shape, cuts[1:], factor),
        out_shape=(full_rows, low_rows, jax.ShapeDtypeStruct((8, width), FULL)) + (shape_a,) * 2,
        in_specs=[SMEM] + [VMEM] * 4 + [HBM] * (6 + 3 * len(runs)),
        out_specs=(HBM,) + (VMEM,) * 2 + (HBM,) * 2,
        scratch_shapes=[
            pltpu.VMEM((2, width, length), LOW),
            pltpu.VMEM((length, width), FULL),
            pltpu.VMEM((length, width), FULL),
            pltpu.VMEM((width, qkvs.room), LOW),
            pltpu.VMEM((length, width), LOW),
            pltpu.VMEM((length, width), LOW),
            pltpu.VMEM((width, 3 * width), LOW),
            pltpu.SemaphoreType.DMA,
            pltpu.SemaphoreType.DMA((3 * len(runs),)),
        ] + [pltpu.VMEM((length, high - low), LOW) for low, high in runs[:-1] for _ in range(3)] + attend_scratch(cuts[1:]),
        compiler_params=params(60),
        cost_estimate=LITTLE,
        name="project_back",
    )(pos, gain_one, page_col, page_row, mask_row, rows, other_rows, weight_qkv,
      second, keys, values, attended, attended_grad, lse, *grads_one)

    own_rows = lax.dynamic_slice_in_dim(stream_out, stream * half_rows, half_rows, 0)
    partner_rows = partner_rows.astype(FULL)
    text_rows = jnp.where(is_text, own_rows, partner_rows)
    image_rows = jnp.where(is_text, partner_rows, own_rows)
    gate_grad = jnp.sum(cot_joined * (text_rows - image_rows), axis=0, keepdims=True) * mix * (1.0 - mix)

    slot_index = lax.iota(jnp.int32, 5)[:, None]
    small = dgain_one[:5] + dgain_two[:5] + jnp.where(slot_index == 4, gate_grad, 0.0)
    sums_a = Halving(kept_a, sent_a, steps_b)
    sums_a.hold(*sums_b.last, *sums_c.last)
    sums_a.send()
    sums_a.rider = rider_rows(small + flip(small, *core[0]), qkvs.wide)
    back_part = swap(away_part)
    sums_a.send()
    sums_b.hold(*sums_a.messages)
    sums_b.send()
    sums_a.hold(*sums_b.messages)
    sums_a.send()
    sums_c.hold(*sums_a.messages)
    sums_c.send()
    sums_b.hold(*sums_a.messages)

    total_a, total_b, total_c = sums_a.total(), sums_b.total(), sums_c.total()

    last = total_a[1].astype(LOW)[None]
    packed = with_rider(last, sums_a.rider)
    arrived = swap(packed)
    packed_c = total_c[1].astype(LOW)
    grad_rows = pl.pallas_call(
        functools.partial(tail_kernel, length),
        out_shape=full_rows,
        in_specs=[VMEM] * 5,
        out_specs=VMEM,
        compiler_params=params(10),
        name="norm_tail",
    )(rows, gain_own, own_part, back_part, after(middle_grad, packed, packed_c))

    text_late, image_late = after(text_rows, packed, packed_c), after(image_rows, packed, packed_c)
    joined_rows = mix * text_late + (1.0 - mix) * image_late

    def both(total):
        return total[0], swap(total[1].astype(LOW))

    def placed(mine, theirs):
        theirs = theirs.astype(FULL)
        return jnp.where(is_text, jnp.stack((mine, theirs)), jnp.stack((theirs, mine)))

    mine_b, theirs_b = both(total_b)
    theirs_b = after(theirs_b, packed, packed_c)
    grad_b = placed(mine_b, theirs_b)
    grad_up = ups.cut(grad_b[..., : ups.wide], doc)
    grad_out = outs.cut(grad_b[..., ups.wide :], doc)
    out_new = adam_update(w_out, m_out, v_out, grad_out, 0.5, 0.01)
    up_new = adam_update(w_up, m_up, v_up, grad_up, 0.12, 0.01)
    if downs.aligned:
        mine_c, theirs_c = total_c[0], swap(packed_c)
    else:
        mine_c = downs.cut(total_c[0], place)
        theirs_c = swap(downs.cut(total_c[1], (place + half) % wide).astype(LOW))
    theirs_c = after(theirs_c, packed, grad_rows, up_new[0], out_new[0])
    grad_down = jnp.swapaxes(placed(mine_c, theirs_c), 1, 2)
    down_new = adam_update(w_down, m_down, v_down, grad_down, 0.06, 0.01)
    arrived = after(arrived, grad_rows, up_new[0], out_new[0], down_new[0])
    last, rider = rider_of(arrived, sums_a.rider.shape, last.shape)
    gains_grad = rider_value(kept_rider(sums_a.rider) + rider, gains.shape)
    mine_a, theirs_a = total_a[0], last[0]
    mine_a, theirs_a = qkvs.cut(mine_a, doc), qkvs.cut(theirs_a.astype(FULL), doc)
    query_here = is_query[0]
    grad_qkv = placed(
        jnp.where(query_here, mine_a, theirs_a), jnp.where(query_here, theirs_a, mine_a)
    )

    qkv_new = adam_update(w_qkv, m_qkv, v_qkv, grad_qkv, 0.12, 0.01)
    gains_new = adam_update(gains, m_gains, v_gains, gains_grad, 0.8, 0.0)
    return (stream_out, joined_rows, grad_rows, *qkv_new, *out_new, *up_new, *down_new, *gains_new)


def solution(mesh):
    by_rows = P(("docs", "wide"), None)
    by_row = P(("docs", "wide"))
    weight = P(None, "wide", "docs")
    return jax.shard_map(
        shards,
        mesh=mesh,
        in_specs=(by_rows,) * 3 + (by_row,) * 2 + (weight,) * 12 + (P(),) * 3,
        out_specs=(by_rows,) * 3 + (weight,) * 12 + (P(),) * 3,
        check_vma=False,
    )
```
